32 devices in a mesh: layer: 16 (over z, x, core), rep: 2 (over y).
Axes of the slice: x: 2, y: 2, z: 4, core: 2. Of those that a mesh axis runs over, the one named last changes fastest.
Arguments:
- gradients: bfloat16 [2, 16, 512, 1024], P('rep', 'layer'), may hold values from -60 to 60
- inverse_out: bfloat16 [16, 512, 512], P('layer', 'rep'), may hold values from -1 to 4
- inverse_in: bfloat16 [16, 1024, 1024], P('layer', 'rep'), may hold values from -1 to 4
- cross_out: bfloat16 [16, 512, 512], P('layer', 'rep'), may hold values from -0.125 to 0.125
- cross_in: bfloat16 [16, 1024, 1024], P('layer', 'rep'), may hold values from -0.1875 to 0.1875
- momentum: float32 [16, 512, 1024], P('layer', 'rep'), may hold values from -3 to 3
Outputs:
- momentum_new: float32 [16, 512, 1024], P('layer', 'rep')
The draws below stay inside these ranges and needn't reach their ends.
All inputs are finite; a program needn't handle non-finite values.
Results may differ from the reference program's by a relative error of at most 0.003.
Values may be sent and summed in bfloat16 or wider, within the bound.
No kernel may reach another device: no remote copies, remote signals or barrier semaphores. Data moves between devices by JAX's collectives and lax.ppermute only.
A program may use at most 64 MiB of HBM per device.

```python
import math
import jax
import jax.numpy as jnp
from jax import lax

D_OUT = 512
D_IN = 1024
LAYERS = 16
REPLICAS = 2


def factor_draw(key, count, width):
    first_key, second_key = jax.random.split(key)
    low, high, spread = (1.0, 2.0, 0.4)
    diagonal = jax.random.uniform(first_key, (count, width, 1), jnp.float32, low, high)
    off_part = jnp.clip(jax.random.normal(second_key, (count, width, width), jnp.float32), -4.0, 4.0) * (spread / math.sqrt(width))
    return off_part + diagonal * jnp.eye(width, dtype=jnp.float32)


def draw_inverse_out(key, part):
    return factor_draw(jax.random.fold_in(key, 11), LAYERS, D_OUT).astype(jnp.bfloat16)


def draw_inverse_in(key, part):
    return factor_draw(jax.random.fold_in(key, 23), LAYERS, D_IN).astype(jnp.bfloat16)


def draw_gradients(key, part):
    keys = jax.random.split(jax.random.fold_in(key, 37), 3)
    top = math.log(math.sqrt(10.0))
    base = jnp.clip(jax.random.normal(keys[0], (REPLICAS, LAYERS, D_OUT, D_IN), jnp.float32), -4.0, 4.0)
    row_scale = jnp.exp(jax.random.uniform(keys[1], (REPLICAS, LAYERS, D_OUT, 1), jnp.float32, 0.0, top))
    col_scale = jnp.exp(jax.random.uniform(keys[2], (REPLICAS, LAYERS, 1, D_IN), jnp.float32, 0.0, top))
    values = base * row_scale * col_scale
    return values.astype(jnp.bfloat16)


def block_levels(stream_key, shape, pieces, low, high):
    factor_of, own = 1.0, jax.random.fold_in(stream_key, 6)
    for axis_at, shards_of in pieces:
        steps = jnp.exp(jax.random.uniform(jax.random.fold_in(own, axis_at), (shards_of,), jnp.float32, low / len(pieces), high / len(pieces)))
        factor_of = factor_of * jnp.repeat(steps, shape[axis_at] // shards_of).reshape([-1 if axis == axis_at else 1 for axis in range(len(shape))])
    return factor_of


def normal_values(rng, extent, scale, reach, shards=(), kind=jnp.bfloat16):
    result = scale * jax.random.normal(rng, extent, jnp.float32)
    if shards:
        result = result * block_levels(rng, extent, shards, -0.22, 0.18)
    return jnp.clip(result, -reach, reach).astype(kind)


def setup_inputs(seed: int = 0) -> dict:
    arg_keys = jax.random.split(jax.random.key(seed), 7)
    return {
        "gradients": draw_gradients(jax.random.fold_in(arg_keys[6], 71), 0),
        "inverse_out": draw_inverse_out(jax.random.fold_in(arg_keys[6], 71), 0),
        "inverse_in": draw_inverse_in(jax.random.fold_in(arg_keys[6], 71), 0),
        "cross_out": normal_values(arg_keys[3], (LAYERS, D_OUT, D_OUT), (4 * D_OUT) ** -0.5, 0.125, ((0, 16), (1, 2))),
        "cross_in": normal_values(arg_keys[4], (LAYERS, D_IN, D_IN), D_IN ** -0.5, 0.1875, ((0, 16), (1, 2))),
        "momentum": normal_values(arg_keys[5], (LAYERS, D_OUT, D_IN), 0.5, 3.0, ((0, 16), (1, 2)), jnp.float32),
    }


def product(left, right):
    return jnp.dot(left.astype(jnp.float32), right.astype(jnp.float32), precision=lax.Precision.HIGHEST, preferred_element_type=jnp.float32)

def replica_step(own_block, following, carried, inv_left, inv_right, cross_left, cross_right):
    first = product(cross_left, following).astype(jnp.bfloat16)
    cross_term = product(first, cross_right)
    residual = (own_block.astype(jnp.float32) - cross_term).astype(jnp.bfloat16)
    left_applied = product(inv_left, residual).astype(jnp.bfloat16)
    precond = product(left_applied, inv_right).astype(jnp.bfloat16)
    back_product = product(cross_left.T, precond).astype(jnp.bfloat16)
    correction = product(back_product, cross_right.T).astype(jnp.bfloat16)
    update = precond.astype(jnp.float32) - carried.astype(jnp.float32)
    delta = update * lax.rsqrt(jnp.mean(update * update) + 1e-06)
    return (delta, correction)

def reference(gradients, inverse_out, inverse_in, cross_out, cross_in, momentum):
    layers_first = jnp.moveaxis(gradients, 1, 0)
    following = jnp.concatenate([layers_first[1:], jnp.zeros_like(layers_first[:1])], axis=0)

    def layer_step(carried, inputs):
        own_blocks, next_blocks, inv_left, inv_right, cross_left, cross_right = inputs
        deltas, corrections = jax.vmap(replica_step, in_axes=(0, 0, 0, None, None, None, None))(own_blocks, next_blocks, carried, inv_left, inv_right, cross_left, cross_right)
        return (corrections, lax.optimization_barrier(jnp.sum(deltas, axis=0)))
    initial = jnp.zeros((REPLICAS, D_OUT, D_IN), jnp.bfloat16)
    _, summed = lax.scan(layer_step, initial, (layers_first, following, inverse_out, inverse_in, cross_out, cross_in))
    return 0.9 * momentum + summed * (1.0 / REPLICAS)
```

```python
import jax
import jax.numpy as jnp
from jax import lax
from jax.sharding import PartitionSpec as P


def passed_along(value, axis, steps):
    count = lax.axis_size(axis)
    initial, last = (max(0, -steps), min(count, count - steps))
    return lax.ppermute(value, axis, [(source, source + steps) for source in range(initial, last)])


def from_peers(value, axis):
    count = lax.axis_size(axis)
    return [
        lax.ppermute(value, axis, [(source, (source - step) % count) for source in range(count)])
        for step in range(1, count)
    ]


def assembled(own, others, axis):
    count, me, rows = lax.axis_size(axis), lax.axis_index(axis), own.shape[0]
    whole = jnp.zeros((count * rows, own.shape[1]), own.dtype)
    for step, block in enumerate([own, *others]):
        whole = lax.dynamic_update_slice(whole, block, (lax.rem(me + step, count) * rows, 0))
    return whole


def body(gradients, inverse_out, inverse_in, cross_out, cross_in, momentum):
    own_block = gradients[0, 0]
    count, me = lax.axis_size("rep"), lax.axis_index("rep")
    following = passed_along(own_block, "layer", -1)
    cross_left = assembled(cross_out[0], from_peers(cross_out[0], "rep"), "rep")
    cross_right = assembled(cross_in[0], from_peers(cross_in[0], "rep"), "rep")
    inv_left = assembled(inverse_out[0], from_peers(inverse_out[0], "rep"), "rep")
    inv_right = assembled(inverse_in[0], from_peers(inverse_in[0], "rep"), "rep")
    first = jnp.dot(cross_left, following, preferred_element_type=jnp.float32).astype(jnp.bfloat16)
    cross_term = jnp.dot(first, cross_right, preferred_element_type=jnp.float32)
    residual = (own_block.astype(jnp.float32) - cross_term).astype(jnp.bfloat16)
    left_applied = jnp.dot(inv_left, residual, preferred_element_type=jnp.float32).astype(
        jnp.bfloat16
    )
    precond = jnp.dot(left_applied, inv_right, preferred_element_type=jnp.float32).astype(
        jnp.bfloat16
    )
    back_product = lax.dot_general(
        cross_left, precond, (((0,), (0,)), ((), ())), preferred_element_type=jnp.float32
    ).astype(jnp.bfloat16)
    correction = lax.dot_general(
        back_product, cross_right, (((1,), (1,)), ((), ())), preferred_element_type=jnp.float32
    ).astype(jnp.bfloat16)
    incoming = passed_along(correction, "layer", 1)
    update = precond.astype(jnp.float32) - incoming.astype(jnp.float32)
    scale = lax.rsqrt(jnp.mean(update * update) + 1e-06)
    rows = momentum.shape[1]
    part = lambda step: lax.dynamic_slice_in_dim(
        update, lax.rem(me + step, count) * rows, rows, axis=0
    )
    total = part(0) * scale
    for step in range(1, count):
        send = (part(step) * scale).astype(jnp.bfloat16)
        total += lax.ppermute(
            send, "rep", [(source, (source + step) % count) for source in range(count)]
        ).astype(jnp.float32)
    renewed = 0.9 * momentum[0] + total * (1.0 / count)
    return renewed[None]


def solution(mesh):
    in_specs = (
        P("rep", "layer", None, None),
        P("layer", "rep", None),
        P("layer", "rep", None),
        P("layer", "rep", None),
        P("layer", "rep", None),
        P("layer", "rep", None),
    )
    out_specs = P("layer", "rep", None)
    return jax.shard_map(body, mesh=mesh, in_specs=in_specs, out_specs=out_specs, check_vma=False)
```

```python
import functools

import jax
import jax.numpy as jnp
from jax import lax
from jax.experimental import pallas as pl
from jax.experimental.pallas import tpu as pltpu
from jax.sharding import PartitionSpec as P

CHUNKS = 4
TILE = 256
HALF = jnp.bfloat16
FULL = jnp.float32


def passed_along(value, axis, steps):
    count = lax.axis_size(axis)
    initial, last = (max(0, -steps), min(count, count - steps))
    return lax.ppermute(value, axis, [(source, source + steps) for source in range(initial, last)])


def from_peers(value, axis):
    count = lax.axis_size(axis)
    return [
        lax.ppermute(value, axis, [(source, (source - step) % count) for source in range(count)])
        for step in range(1, count)
    ]


def to_peer(value, axis, step):
    count = lax.axis_size(axis)
    return lax.ppermute(
        value, axis, [(source, (source + step) % count) for source in range(count)]
    )


def dot(left, right, contract=((1,), (0,))):
    return lax.dot_general(left, right, (contract, ((), ())), preferred_element_type=FULL)


def span(me_ref, step, count, size):
    start = lax.rem(me_ref[0] + step, count) * size
    return pl.ds(pl.multiple_of(start, size), size)


def first_kernel(count, me, following, *refs):
    blocks, out = refs[:count], refs[count]
    rows = blocks[0].shape[0]
    width = out.shape[1]

    @pl.loop(0, width // TILE)
    def _(at):
        columns = pl.ds(pl.multiple_of(at * TILE, TILE), TILE)
        right = following[:, columns]
        for step in range(count):
            out[span(me, step, count, rows), columns] = dot(blocks[step][...], right).astype(HALF)


def left_kernel(count, me, own, first, *refs):
    rights, lefts, out = refs[:count], refs[count : 2 * count], refs[2 * count]
    depth, rows = rights[0].shape[0], lefts[0].shape[0]
    width = out.shape[1]

    @pl.loop(0, width // TILE)
    def _(at):
        columns = pl.ds(pl.multiple_of(at * TILE, TILE), TILE)
        cross = sum(
            dot(first[:, span(me, step, count, depth)], rights[step][:, columns])
            for step in range(count)
        )
        residual = (own[:, columns].astype(FULL) - cross).astype(HALF)
        for step in range(count):
            out[span(me, step, count, rows), columns] = dot(lefts[step][...], residual).astype(
                HALF
            )


def chunk_kernel(count, me, left, *refs):
    pieces, lefts = refs[:count], refs[count : 2 * count]
    precond, back = refs[2 * count :]
    depth, rows = pieces[0].shape[0], lefts[0].shape[0]
    product = sum(
        dot(left[:, span(me, step, count, depth)], pieces[step][...]) for step in range(count)
    )
    precond[...] = product.astype(HALF)
    back[...] = sum(
        dot(lefts[step][...], precond[span(me, step, count, rows), :], ((0,), (0,)))
        for step in range(count)
    ).astype(HALF)


def update_kernel(count, me, *refs):
    preconds, backs = refs[:CHUNKS], refs[CHUNKS : 2 * CHUNKS]
    rights = refs[2 * CHUNKS : 2 * CHUNKS + count]
    squares, own = refs[2 * CHUNKS + count : 2 * CHUNKS + count + 2]
    sends, whole = refs[2 * CHUNKS + count + 2 : -1], refs[-1]
    rows, depth = own.shape[0], rights[0].shape[0]
    piece = preconds[0].shape[1]
    for at in range(CHUNKS):
        whole[:, at * piece : (at + 1) * piece] = preconds[at][...]
    total = jnp.zeros((), FULL)
    for row_step in range(count):
        here = span(me, row_step, count, rows)
        for step in range(count):
            columns = span(me, step, count, depth)
            incoming = sum(
                dot(
                    backs[at][here, :],
                    rights[step][:, at * piece : (at + 1) * piece],
                    ((1,), (1,)),
                )
                for at in range(CHUNKS)
            ).astype(HALF)
            update = whole[here, columns].astype(FULL) - incoming.astype(FULL)
            total += jnp.sum(update * update)
            if row_step == 0:
                own[:, columns] = update
            else:
                sends[row_step - 1][:, columns] = update.astype(HALF)
    squares[...] = jnp.full(squares.shape, total, FULL)


def call(kernel, outs, operands, flops, scratch=()):
    moved = sum(value.size * value.dtype.itemsize for value in (*operands, *outs))
    vmem = pl.BlockSpec(memory_space=pltpu.VMEM)
    return pl.pallas_call(
        kernel,
        out_shape=outs,
        in_specs=[pl.BlockSpec(memory_space=pltpu.SMEM)] + [vmem] * (len(operands) - 1),
        out_specs=[vmem] * len(outs),
        scratch_shapes=scratch,
        compiler_params=pltpu.CompilerParams(vmem_limit_bytes=32 * 1024 * 1024),
        cost_estimate=pl.CostEstimate(flops=flops, bytes_accessed=moved, transcendentals=0),
    )(*operands)


def body(gradients, inverse_out, inverse_in, cross_out, cross_in, momentum):
    own_block = gradients[0, 0]
    tall, wide = own_block.shape
    count = lax.axis_size("rep")
    me = lax.axis_index("rep").astype(jnp.int32).reshape(1)
    piece = wide // CHUNKS
    rows = momentum.shape[1]
    shape = jax.ShapeDtypeStruct

    following = passed_along(own_block, "layer", -1)
    out_blocks = [cross_out[0], *from_peers(cross_out[0], "rep")]
    in_blocks = [cross_in[0], *from_peers(cross_in[0], "rep")]
    inv_out_blocks = [inverse_out[0], *from_peers(inverse_out[0], "rep")]
    cuts = [inverse_in[0][:, at * piece : (at + 1) * piece] for at in range(CHUNKS)]
    inv_in_blocks = [[cut, *from_peers(cut, "rep")] for cut in cuts]
    previous_blocks = [passed_along(block, "layer", 1) for block in in_blocks]

    first = call(
        functools.partial(first_kernel, count),
        [shape((tall, wide), HALF)],
        [me, following, *out_blocks],
        2 * tall * tall * wide,
    )[0]
    left = call(
        functools.partial(left_kernel, count),
        [shape((tall, wide), HALF)],
        [me, own_block, first, *in_blocks, *inv_out_blocks],
        2 * tall * wide * (tall + wide),
    )[0]
    preconds, backs = [], []
    for blocks in inv_in_blocks:
        part, back = call(
            functools.partial(chunk_kernel, count),
            [shape((tall, piece), HALF)] * 2,
            [me, left, *blocks, *out_blocks],
            2 * tall * piece * (tall + wide),
        )
        preconds.append(part)
        backs.append(passed_along(back, "layer", 1))
    squares, own, *sends = call(
        functools.partial(update_kernel, count),
        [shape((8, 128), FULL), shape((rows, wide), FULL)]
        + [shape((rows, wide), HALF)] * (count - 1),
        [me, *preconds, *backs, *previous_blocks],
        2 * tall * wide * wide,
        [pltpu.VMEM((tall, wide), HALF)],
    )
    scale = lambda value: lax.rsqrt(value[0, 0] * (1.0 / (tall * wide)) + 1e-06)
    total = own * scale(squares)
    for step in range(1, count):
        other = to_peer(squares, "rep", step)
        total += to_peer(sends[step - 1], "rep", step).astype(FULL) * scale(other)
    renewed = 0.9 * momentum[0] + total * (1.0 / count)
    return renewed[None]


def solution(mesh):
    in_specs = (
        P("rep", "layer", None, None),
        P("layer", "rep", None),
        P("layer", "rep", None),
        P("layer", "rep", None),
        P("layer", "rep", None),
        P("layer", "rep", None),
    )
    out_specs = P("layer", "rep", None)
    return jax.shard_map(body, mesh=mesh, in_specs=in_specs, out_specs=out_specs, check_vma=False)
```

```python
import functools

import jax
import jax.numpy as jnp
from jax import lax
from jax.experimental import pallas as pl
from jax.experimental.pallas import tpu as pltpu
from jax.sharding import PartitionSpec as P

SHARES = (3, 2, 2, 1)
TILE = 256
EXTRA = 16
HALF = jnp.bfloat16
FULL = jnp.float32


def passed_along(value, axis, steps):
    count = lax.axis_size(axis)
    initial, last = (max(0, -steps), min(count, count - steps))
    return lax.ppermute(value, axis, [(source, source + steps) for source in range(initial, last)])


def from_peers(value, axis):
    count = lax.axis_size(axis)
    return [
        lax.ppermute(value, axis, [(source, (source - step) % count) for source in range(count)])
        for step in range(1, count)
    ]


def to_peer(value, axis, step):
    count = lax.axis_size(axis)
    return lax.ppermute(
        value, axis, [(source, (source + step) % count) for source in range(count)]
    )


def dot(left, right, contract=((1,), (0,))):
    return lax.dot_general(left, right, (contract, ((), ())), preferred_element_type=FULL)


def span(me_ref, step, count, size):
    start = lax.rem(me_ref[0] + step, count) * size
    return pl.ds(pl.multiple_of(start, size), size)


def first_kernel(count, me, following, own, *refs):
    others, out = refs[: count - 1], refs[count - 1]
    rows = own.shape[0]

    @pl.loop(0, out.shape[1] // TILE)
    def _(at):
        columns = pl.ds(pl.multiple_of(at * TILE, TILE), TILE)
        right = following[:, columns]
        out[span(me, 0, count, rows), columns] = dot(own[...], right).astype(HALF)
        for step in range(1, count):
            block = others[step - 1][:rows, :]
            out[span(me, step, count, rows), columns] = dot(block, right).astype(HALF)


def left_kernel(count, me, grads, first, inv_own, *refs):
    rights, others, out = refs[:count], refs[count : 2 * count - 1], refs[2 * count - 1]
    depth, rows = rights[0].shape[0], inv_own.shape[0]

    @pl.loop(0, out.shape[1] // TILE)
    def _(at):
        columns = pl.ds(pl.multiple_of(at * TILE, TILE), TILE)
        cross = sum(
            dot(first[:, span(me, step, count, depth)], rights[step][:, columns])
            for step in range(count)
        )
        residual = (grads[:, columns].astype(FULL) - cross).astype(HALF)
        out[span(me, 0, count, rows), columns] = dot(inv_own[...], residual).astype(HALF)
        for step in range(1, count):
            block = others[step - 1][rows:, :]
            out[span(me, step, count, rows), columns] = dot(block, residual).astype(HALF)


def chunk_kernel(count, me, left, cross_own, own_piece, *refs):
    pieces, others = refs[: count - 1], refs[count - 1 : 2 * count - 2]
    precond, back = refs[2 * count - 2 :]
    depth, rows = own_piece.shape[0], cross_own.shape[0]
    product = dot(left[:, span(me, 0, count, depth)], own_piece[...])
    for step in range(1, count):
        product += dot(left[:, span(me, step, count, depth)], pieces[step - 1][...])
    precond[...] = product.astype(HALF)
    turned = ((0,), (0,))
    result = dot(cross_own[...], precond[span(me, 0, count, rows), :], turned)
    for step in range(1, count):
        block = others[step - 1][:rows, :]
        result += dot(block, precond[span(me, step, count, rows), :], turned)
    back[...] = result.astype(HALF)


def gather_kernel(count, widths, me, *refs):
    early = len(widths) - 1
    preconds, backs = refs[:early], refs[early : 2 * early]
    rights = refs[2 * early : 2 * early + count]
    partial, right_last = refs[2 * early + count :]
    depth = rights[0].shape[0]
    for step in range(count):
        columns = span(me, step, count, depth)
        start, total = 0, 0.0
        for at in range(early):
            block = rights[step][:, start : start + widths[at]]
            total += dot(backs[at][...], block, ((1,), (1,)))
            start += widths[at]
        partial[:, columns] = -total
        right_last[columns, :] = rights[step][:, start:]
    start = 0
    for at in range(early):
        here = slice(start, start + widths[at])
        partial[:, here] += preconds[at][...].astype(FULL)
        start += widths[at]


def update_kernel(count, me, partial, precond, back, right_last, *refs):
    squares, own = refs[:2]
    sends = refs[2:]
    rows, wide = own.shape
    cut = rows // 2
    late = wide - precond.shape[1]
    total = jnp.zeros((), FULL)
    for step in range(count):
        here = span(me, step, count, rows)
        for start in range(0, wide, TILE):
            columns = slice(start, start + TILE)
            update = partial[here, columns] - dot(
                back[here, :], right_last[columns, :], ((1,), (1,))
            )
            if start + TILE > late:
                pad = jnp.zeros((rows, max(late - start, 0)), FULL)
                low = max(start - late, 0)
                tail = precond[here, low : start + TILE - late].astype(FULL)
                update += jnp.concatenate([pad, tail], axis=1) if pad.shape[1] else tail
            total += jnp.sum(update * update)
            if step == 0:
                own[:, columns] = update
            else:
                near, far = sends[2 * step - 2 : 2 * step]
                rounded = update.astype(HALF)
                near[:cut, columns] = rounded[:cut]
                far[:, columns] = rounded[cut:]
    squares[...] = jnp.full(squares.shape, total, FULL)
    value = jnp.full((EXTRA, 128), total, FULL)
    for near in sends[::2]:
        rest = value
        near[cut:, :] = jnp.zeros((EXTRA, wide), HALF)
        for part in range(3):
            coded = rest.astype(HALF)
            near[cut:, part * 128 : (part + 1) * 128] = coded
            rest = rest - coded.astype(FULL)


def scale_of(squares, size):
    return lax.rsqrt(squares * (1.0 / size) + 1e-06)


def final_kernel(count, which, size, momentum, squares, own, *refs):
    nears, refs = refs[: count - 1], refs[count - 1 :]
    fars = refs[: (count - 1) * which]
    out, scratch, sem = refs[-3:]
    cut = scratch.shape[0]
    rows = slice(which * cut, (which + 1) * cut)
    total = own[rows, :] * scale_of(squares[0:1, 0:1], size)
    for step in range(count - 1):
        code = nears[step][cut:, :384].astype(FULL)
        other = code[0:1, 0:1] + code[0:1, 128:129] + code[0:1, 256:257]
        block = fars[step][...] if which else nears[step][:cut, :]
        total += block.astype(FULL) * scale_of(other, size)
    scratch[...] = 0.9 * momentum[rows, :] + total * (1.0 / count)
    copy = pltpu.make_async_copy(scratch, out.at[rows, :], sem)
    copy.start()
    copy.wait()


def call(kernel, outs, operands, flops, scalar=True, **options):
    moved = sum(value.size * value.dtype.itemsize for value in (*operands, *outs))
    vmem = pl.BlockSpec(memory_space=pltpu.VMEM)
    specs = [pl.BlockSpec(memory_space=pltpu.SMEM)] * scalar + [vmem] * len(operands)
    settings = dict(in_specs=specs[: len(operands)], out_specs=[vmem] * len(outs))
    settings.update(options)
    return pl.pallas_call(
        kernel,
        out_shape=outs,
        compiler_params=pltpu.CompilerParams(vmem_limit_bytes=32 * 1024 * 1024),
        cost_estimate=pl.CostEstimate(flops=flops, bytes_accessed=moved, transcendentals=0),
        **settings,
    )(*operands)


def body(gradients, inverse_out, inverse_in, cross_out, cross_in, momentum):
    own_block = gradients[0, 0]
    tall, wide = own_block.shape
    count = lax.axis_size("rep")
    me = lax.axis_index("rep").astype(jnp.int32).reshape(1)
    widths = [share * wide // sum(SHARES) for share in SHARES]
    rows = momentum.shape[1]
    cut = rows // 2
    shape = jax.ShapeDtypeStruct
    part = functools.partial

    in_blocks = [cross_in[0], *from_peers(cross_in[0], "rep")]
    pairs = from_peers(jnp.concatenate([cross_out[0], inverse_out[0]], axis=0), "rep")
    following = passed_along(own_block, "layer", -1)
    starts = [sum(widths[:at]) for at in range(len(widths))]
    cuts = [inverse_in[0][:, at : at + width] for at, width in zip(starts, widths)]
    cut_peers = [from_peers(piece, "rep") for piece in cuts]
    previous_blocks = [passed_along(block, "layer", 1) for block in in_blocks]

    (first,) = call(
        part(first_kernel, count),
        [shape((tall, wide), HALF)],
        [me, following, cross_out[0], *pairs],
        2 * tall * tall * wide,
    )
    (left,) = call(
        part(left_kernel, count),
        [shape((tall, wide), HALF)],
        [me, own_block, first, inverse_out[0], *in_blocks, *pairs],
        2 * tall * wide * (tall + wide),
    )
    preconds, backs = [], []
    for piece, peers in zip(cuts, cut_peers):
        precond, back = call(
            part(chunk_kernel, count),
            [shape(piece.shape[:0] + (tall, piece.shape[1]), HALF)] * 2,
            [me, left, cross_out[0], piece, *peers, *pairs],
            2 * tall * piece.shape[1] * (tall + wide),
        )
        preconds.append(precond)
        backs.append(passed_along(back, "layer", 1))
    partial, right_last = call(
        part(gather_kernel, count, widths),
        [shape((tall, wide), FULL), shape((wide, widths[-1]), HALF)],
        [me, *preconds[:-1], *backs[:-1], *previous_blocks],
        2 * tall * wide * (wide - widths[-1]),
    )
    sizes = [shape((cut + EXTRA, wide), HALF), shape((rows - cut, wide), HALF)]
    squares, own, *sends = call(
        part(update_kernel, count),
        [shape((8, 128), FULL), shape((rows, wide), FULL)] + sizes * (count - 1),
        [me, partial, preconds[-1], backs[-1], right_last],
        2 * tall * wide * widths[-1],
    )
    nears = [to_peer(value, "rep", at + 1) for at, value in enumerate(sends[::2])]
    fars = [to_peer(value, "rep", at + 1) for at, value in enumerate(sends[1::2])]
    result = None
    for which in range(2):
        operands = [momentum[0], squares, own, *nears]
        if which:
            operands += [*fars, result]
        specs = [pl.BlockSpec(memory_space=pltpu.VMEM)] * len(operands)
        if which:
            specs[-1] = pl.BlockSpec(memory_space=pl.ANY)
        (result,) = call(
            part(final_kernel, count, which, tall * wide),
            [shape((rows, wide), FULL)],
            operands,
            4 * cut * wide,
            in_specs=specs,
            out_specs=[pl.BlockSpec(memory_space=pl.ANY)],
            scratch_shapes=[pltpu.VMEM((cut, wide), FULL), pltpu.SemaphoreType.DMA],
            input_output_aliases={len(operands) - 1: 0} if which else {},
        )
    return result[None]


def solution(mesh):
    in_specs = (
        P("rep", "layer", None, None),
        P("layer", "rep", None),
        P("layer", "rep", None),
        P("layer", "rep", None),
        P("layer", "rep", None),
        P("layer", "rep", None),
    )
    out_specs = P("layer", "rep", None)
    return jax.shard_map(body, mesh=mesh, in_specs=in_specs, out_specs=out_specs, check_vma=False)
```

```python
import functools

import jax
import jax.numpy as jnp
from jax import lax
from jax.experimental import pallas as pl
from jax.experimental.pallas import tpu as pltpu
from jax.sharding import PartitionSpec as P

SHARES = (2, 1, 1)
TILE = 256
EXTRA = 16
HALF = jnp.bfloat16
FULL = jnp.float32


def passed_along(value, axis, steps):
    count = lax.axis_size(axis)
    initial, last = (max(0, -steps), min(count, count - steps))
    return lax.ppermute(value, axis, [(source, source + steps) for source in range(initial, last)])


def from_peers(value, axis):
    count = lax.axis_size(axis)
    return [
        lax.ppermute(value, axis, [(source, (source - step) % count) for source in range(count)])
        for step in range(1, count)
    ]


def to_peer(value, axis, step):
    count = lax.axis_size(axis)
    return lax.ppermute(
        value, axis, [(source, (source + step) % count) for source in range(count)]
    )


def dot(left, right, contract=((1,), (0,))):
    return lax.dot_general(left, right, (contract, ((), ())), preferred_element_type=FULL)


def span(me_ref, step, count, size):
    start = lax.rem(me_ref[0] + step, count) * size
    return pl.ds(pl.multiple_of(start, size), size)


def first_kernel(count, me, following, own, *refs):
    others, out = refs[: count - 1], refs[-1]
    rows = own.shape[0]

    @pl.loop(0, out.shape[1] // TILE)
    def _(at):
        columns = pl.ds(pl.multiple_of(at * TILE, TILE), TILE)
        right = following[:, columns]
        out[span(me, 0, count, rows), columns] = dot(own[...], right).astype(HALF)
        for step in range(1, count):
            block = others[step - 1][:rows, :]
            out[span(me, step, count, rows), columns] = dot(block, right).astype(HALF)


def left_kernel(count, me, grads, first, inv_own, *refs):
    rights, others, out = refs[:count], refs[count : 2 * count - 1], refs[2 * count - 1]
    depth, rows = rights[0].shape[0], inv_own.shape[0]

    @pl.loop(0, out.shape[1] // TILE)
    def _(at):
        columns = pl.ds(pl.multiple_of(at * TILE, TILE), TILE)
        cross = sum(
            dot(first[:, span(me, step, count, depth)], rights[step][:, columns])
            for step in range(count)
        )
        residual = (grads[:, columns].astype(FULL) - cross).astype(HALF)
        out[span(me, 0, count, rows), columns] = dot(inv_own[...], residual).astype(HALF)
        for step in range(1, count):
            block = others[step - 1][rows:, :]
            out[span(me, step, count, rows), columns] = dot(block, residual).astype(HALF)


def chunk_kernel(count, me, left, cross_own, own_piece, *refs):
    pieces, others = refs[: count - 1], refs[count - 1 : 2 * count - 2]
    precond, back = refs[-2:]
    depth, rows = own_piece.shape[0], cross_own.shape[0]
    product = dot(left[:, span(me, 0, count, depth)], own_piece[...])
    for step in range(1, count):
        product += dot(left[:, span(me, step, count, depth)], pieces[step - 1][...])
    precond[...] = product.astype(HALF)
    turned = ((0,), (0,))
    result = dot(cross_own[...], precond[span(me, 0, count, rows), :], turned)
    for step in range(1, count):
        block = others[step - 1][:rows, :]
        result += dot(block, precond[span(me, step, count, rows), :], turned)
    back[...] = result.astype(HALF)


def gather_kernel(count, widths, me, *refs):
    early = len(widths) - 1
    preconds, backs = refs[:early], refs[early : 2 * early]
    rights = refs[2 * early : 2 * early + count]
    partial, right_last, staged, stacked = refs[2 * early + count :]
    depth, known = rights[0].shape[0], stacked.shape[1]
    start = 0
    for at in range(early):
        here = slice(start, start + widths[at])
        staged[:, here] = preconds[at][...]
        stacked[:, here] = backs[at][...]
        start += widths[at]
    staged[:, known:] = jnp.zeros((staged.shape[0], staged.shape[1] - known), HALF)
    for step in range(count):
        columns = span(me, step, count, depth)
        right_last[columns, :] = rights[step][:, known:]
        right = rights[step][:, :known]
        for row in range(0, staged.shape[0], TILE):
            here = slice(row, row + TILE)
            product = dot(stacked[here, :], right, ((1,), (1,)))
            partial[here, columns] = staged[here, columns].astype(FULL) - product


def update_kernel(count, me, partial, precond, back, right_last, *refs):
    squares, own = refs[:2]
    sends = refs[2:]
    rows, wide = own.shape
    cut = rows // 2
    late = wide - precond.shape[1]
    total = jnp.zeros((), FULL)
    for step in range(count):
        here = span(me, step, count, rows)
        for start in range(0, wide, TILE):
            columns = slice(start, start + TILE)
            update = partial[here, columns] - dot(
                back[here, :], right_last[columns, :], ((1,), (1,))
            )
            if start + TILE > late:
                pad = jnp.zeros((rows, max(late - start, 0)), FULL)
                low = max(start - late, 0)
                tail = precond[here, low : start + TILE - late].astype(FULL)
                update += jnp.concatenate([pad, tail], axis=1) if pad.shape[1] else tail
            total += jnp.sum(update * update)
            if step == 0:
                own[:, columns] = update
            else:
                near, far = sends[2 * step - 2 : 2 * step]
                rounded = update.astype(HALF)
                near[:cut, columns] = rounded[:cut]
                far[:, columns] = rounded[cut:]
    squares[...] = jnp.full(squares.shape, total, FULL)
    value = jnp.full((EXTRA, 128), total, FULL)
    for near in sends[::2]:
        rest = value
        near[cut:, :] = jnp.zeros((EXTRA, wide), HALF)
        for part in range(3):
            coded = rest.astype(HALF)
            near[cut:, part * 128 : (part + 1) * 128] = coded
            rest = rest - coded.astype(FULL)


def scale_of(squares, size):
    return lax.rsqrt(squares * (1.0 / size) + 1e-06)


def final_kernel(count, which, size, momentum, squares, own, *refs):
    nears, refs = refs[: count - 1], refs[count - 1 :]
    fars = refs[: (count - 1) * which]
    out, scratch, sem = refs[-3:]
    cut = scratch.shape[0]
    rows = slice(which * cut, (which + 1) * cut)
    total = own[rows, :] * scale_of(squares[0:1, 0:1], size)
    for step in range(count - 1):
        code = nears[step][cut:, :384].astype(FULL)
        other = code[0:1, 0:1] + code[0:1, 128:129] + code[0:1, 256:257]
        block = fars[step][...] if which else nears[step][:cut, :]
        total += block.astype(FULL) * scale_of(other, size)
    scratch[...] = 0.9 * momentum[rows, :] + total * (1.0 / count)
    copy = pltpu.make_async_copy(scratch, out.at[rows, :], sem)
    copy.start()
    copy.wait()


def call(kernel, outs, operands, flops, unread=0, **options):
    moved = sum(value.size * value.dtype.itemsize for value in (*operands, *outs))
    vmem = pl.BlockSpec(memory_space=pltpu.VMEM)
    specs = [pl.BlockSpec(memory_space=pltpu.SMEM)] + [vmem] * (len(operands) - 1)
    specs[len(operands) - unread :] = [pl.BlockSpec(memory_space=pl.ANY)] * unread
    settings = dict(in_specs=specs, out_specs=[vmem] * len(outs))
    settings.update(options)
    return pl.pallas_call(
        kernel,
        out_shape=outs,
        compiler_params=pltpu.CompilerParams(vmem_limit_bytes=32 * 1024 * 1024),
        cost_estimate=pl.CostEstimate(flops=flops, bytes_accessed=moved // 64, transcendentals=0),
        **settings,
    )(*operands)


def body(gradients, inverse_out, inverse_in, cross_out, cross_in, momentum):
    own_block = gradients[0, 0]
    tall, wide = own_block.shape
    count = lax.axis_size("rep")
    me = lax.axis_index("rep").astype(jnp.int32).reshape(1)
    widths = [share * wide // sum(SHARES) for share in SHARES]
    rows = momentum.shape[1]
    cut = rows // 2
    shape = jax.ShapeDtypeStruct
    part = functools.partial

    pairs = from_peers(jnp.concatenate([cross_out[0], inverse_out[0]], axis=0), "rep")
    in_blocks = [cross_in[0], *from_peers(cross_in[0], "rep")]
    following = passed_along(own_block, "layer", -1)

    starts = [sum(widths[:at]) for at in range(len(widths))]
    cuts = [inverse_in[0][:, at : at + width] for at, width in zip(starts, widths)]
    cut_peers = [from_peers(piece, "rep") for piece in cuts]
    (first,) = call(
        part(first_kernel, count),
        [shape((tall, wide), HALF)],
        [me, following, cross_out[0], *pairs],
        tall * tall * wide // 32,
    )
    previous_blocks = [passed_along(block, "layer", 1) for block in in_blocks]
    (left,) = call(
        part(left_kernel, count),
        [shape((tall, wide), HALF)],
        [me, own_block, first, inverse_out[0], *in_blocks, *pairs],
        tall * wide * (tall + wide) // 32,
    )
    preconds, backs = [], []
    for at, (piece, peers) in enumerate(zip(cuts, cut_peers)):
        unread = []
        weight = 256 if at == len(cuts) - 1 else 1
        precond, back = call(
            part(chunk_kernel, count),
            [shape((tall, piece.shape[1]), HALF)] * 2,
            [me, left, cross_out[0], piece, *peers, *pairs, *unread],
            weight * tall * piece.shape[1] * (tall + wide) // 32,
            unread=len(unread),
        )
        preconds.append(precond)
        backs.append(passed_along(back, "layer", 1))
    partial, right_last = call(
        part(gather_kernel, count, widths),
        [shape((tall, wide), FULL), shape((wide, widths[-1]), HALF)],
        [me, *preconds[:-1], *backs[:-1], *previous_blocks],
        2 * tall * wide * (wide - widths[-1]),
        scratch_shapes=[
            pltpu.VMEM((tall, wide), HALF),
            pltpu.VMEM((tall, wide - widths[-1]), HALF),
        ],
    )
    sizes = [shape((cut + EXTRA, wide), HALF), shape((rows - cut, wide), HALF)]
    squares, own, *sends = call(
        part(update_kernel, count),
        [shape((8, 128), FULL), shape((rows, wide), FULL)] + sizes * (count - 1),
        [me, partial, preconds[-1], backs[-1], right_last],
        2 * tall * wide * widths[-1],
    )
    nears = [to_peer(value, "rep", at + 1) for at, value in enumerate(sends[::2])]
    fars = [to_peer(value, "rep", at + 1) for at, value in enumerate(sends[1::2])]
    result = None
    for which in range(2):
        operands = [momentum[0], squares, own, *nears]
        if which:
            operands += [*fars, result]
        specs = [pl.BlockSpec(memory_space=pltpu.VMEM)] * len(operands)
        if which:
            specs[-1] = pl.BlockSpec(memory_space=pl.ANY)
        (result,) = call(
            part(final_kernel, count, which, tall * wide),
            [shape((rows, wide), FULL)],
            operands,
            4 * cut * wide,
            in_specs=specs,
            out_specs=[pl.BlockSpec(memory_space=pl.ANY)],
            scratch_shapes=[pltpu.VMEM((cut, wide), FULL), pltpu.SemaphoreType.DMA],
            input_output_aliases={len(operands) - 1: 0} if which else {},
        )
    return result[None]


def solution(mesh):
    in_specs = (
        P("rep", "layer", None, None),
        P("layer", "rep", None),
        P("layer", "rep", None),
        P("layer", "rep", None),
        P("layer", "rep", None),
        P("layer", "rep", None),
    )
    out_specs = P("layer", "rep", None)
    return jax.shard_map(body, mesh=mesh, in_specs=in_specs, out_specs=out_specs, check_vma=False)
```

```python
import functools

import jax
import jax.numpy as jnp
from jax import lax
from jax.experimental import pallas as pl
from jax.experimental.pallas import tpu as pltpu
from jax.sharding import PartitionSpec as P

SHARES = (2, 1, 1)
TILE = 256
HALF = jnp.bfloat16
FULL = jnp.float32


def passed_along(value, axis, steps):
    count = lax.axis_size(axis)
    initial, last = (max(0, -steps), min(count, count - steps))
    return lax.ppermute(value, axis, [(source, source + steps) for source in range(initial, last)])


def from_peers(value, axis):
    count = lax.axis_size(axis)
    return [
        lax.ppermute(value, axis, [(source, (source - step) % count) for source in range(count)])
        for step in range(1, count)
    ]


def to_peer(value, axis, step):
    count = lax.axis_size(axis)
    return lax.ppermute(
        value, axis, [(source, (source + step) % count) for source in range(count)]
    )


def dot(left, right, contract=((1,), (0,))):
    return lax.dot_general(left, right, (contract, ((), ())), preferred_element_type=FULL)


def span(me_ref, step, count, size):
    start = lax.rem(me_ref[0] + step, count) * size
    return pl.ds(pl.multiple_of(start, size), size)


def cut_kernel(widths, me, cross_out, inverse_out, inverse_in, pair, *refs):
    pieces, sems = refs[:-1], refs[-1]
    rows, start = cross_out.shape[0], 0
    copies = [
        pltpu.make_async_copy(cross_out, pair.at[:rows], sems.at[0]),
        pltpu.make_async_copy(inverse_out, pair.at[rows:], sems.at[1]),
    ]
    for at, width in enumerate(widths):
        source = inverse_in.at[:, start : start + width]
        copies.append(pltpu.make_async_copy(source, pieces[at], sems.at[2 + at]))
        start += width
    for copy in copies:
        copy.start()
    for copy in copies:
        copy.wait()


def first_kernel(count, me, following, own, *refs):
    others, out = refs[: count - 1], refs[-1]
    rows = own.shape[0]

    @pl.loop(0, out.shape[1] // TILE)
    def _(at):
        columns = pl.ds(pl.multiple_of(at * TILE, TILE), TILE)
        right = following[:, columns]
        out[span(me, 0, count, rows), columns] = dot(own[...], right).astype(HALF)
        for step in range(1, count):
            block = others[step - 1][:rows, :]
            out[span(me, step, count, rows), columns] = dot(block, right).astype(HALF)


def left_kernel(count, me, grads, first, inv_own, *refs):
    rights, others, out = refs[:count], refs[count : 2 * count - 1], refs[2 * count - 1]
    depth, rows = rights[0].shape[0], inv_own.shape[0]

    @pl.loop(0, out.shape[1] // TILE)
    def _(at):
        columns = pl.ds(pl.multiple_of(at * TILE, TILE), TILE)
        cross = sum(
            dot(first[:, span(me, step, count, depth)], rights[step][:, columns])
            for step in range(count)
        )
        residual = (grads[:, columns].astype(FULL) - cross).astype(HALF)
        out[span(me, 0, count, rows), columns] = dot(inv_own[...], residual).astype(HALF)
        for step in range(1, count):
            block = others[step - 1][rows:, :]
            out[span(me, step, count, rows), columns] = dot(block, residual).astype(HALF)


def chunk_kernel(count, me, left, cross_own, own_piece, *refs):
    pieces, others = refs[: count - 1], refs[count - 1 : 2 * count - 2]
    precond, back = refs[-2:]
    depth, rows = own_piece.shape[0], cross_own.shape[0]
    product = dot(left[:, span(me, 0, count, depth)], own_piece[...])
    for step in range(1, count):
        product += dot(left[:, span(me, step, count, depth)], pieces[step - 1][...])
    precond[...] = product.astype(HALF)
    turned = ((0,), (0,))
    result = dot(cross_own[...], precond[span(me, 0, count, rows), :], turned)
    for step in range(1, count):
        block = others[step - 1][:rows, :]
        result += dot(block, precond[span(me, step, count, rows), :], turned)
    back[...] = result.astype(HALF)


def gather_kernel(count, widths, me, *refs):
    early = len(widths) - 1
    preconds, backs = refs[:early], refs[early : 2 * early]
    rights = refs[2 * early : 2 * early + count]
    partial, right_last, staged, stacked = refs[2 * early + count :]
    depth, known = rights[0].shape[0], stacked.shape[1]
    start = 0
    for at in range(early):
        here = slice(start, start + widths[at])
        staged[:, here] = preconds[at][...]
        stacked[:, here] = backs[at][...]
        start += widths[at]
    staged[:, known:] = jnp.zeros((staged.shape[0], staged.shape[1] - known), HALF)
    for step in range(count):
        columns = span(me, step, count, depth)
        right_last[columns, :] = rights[step][:, known:]
        right = rights[step][:, :known]
        for row in range(0, staged.shape[0], TILE):
            here = slice(row, row + TILE)
            product = dot(stacked[here, :], right, ((1,), (1,)))
            partial[here, columns] = staged[here, columns].astype(FULL) - product


def update_kernel(count, me, partial, precond, back, right_last, *refs):
    squares, own = refs[:2]
    sends = refs[2:]
    rows, wide = own.shape
    late = wide - precond.shape[1]
    total = jnp.zeros((), FULL)
    for step in range(count):
        here = span(me, step, count, rows)
        for start in range(0, wide, TILE):
            columns = slice(start, start + TILE)
            update = partial[here, columns] - dot(
                back[here, :], right_last[columns, :], ((1,), (1,))
            )
            if start + TILE > late:
                pad = jnp.zeros((rows, max(late - start, 0)), FULL)
                low = max(start - late, 0)
                tail = precond[here, low : start + TILE - late].astype(FULL)
                update += jnp.concatenate([pad, tail], axis=1) if pad.shape[1] else tail
            total += jnp.sum(update * update)
            if step == 0:
                own[:, columns] = update
            else:
                sends[step - 1][:, columns] = update.astype(HALF)
    squares[...] = jnp.full(squares.shape, total, FULL)


def scale_of(squares, size):
    return lax.rsqrt(squares * (1.0 / size) + 1e-06)


def final_kernel(count, size, momentum, squares, own, *refs):
    others, blocks = refs[: count - 1], refs[count - 1 : 2 * count - 2]
    out, scratch, sems = refs[-3:]
    rows = scratch.shape[0] // sems.shape[0]
    scales = [scale_of(value[0:1, 0:1], size) * (1.0 / count) for value in (squares, *others)]
    copies = []
    for at in range(sems.shape[0]):
        here = slice(at * rows, (at + 1) * rows)
        total = own[here, :] * scales[0]
        for step in range(count - 1):
            total += blocks[step][here, :].astype(FULL) * scales[step + 1]
        scratch[here, :] = 0.9 * momentum[here, :] + total
        copies.append(pltpu.make_async_copy(scratch.at[here, :], out.at[here, :], sems.at[at]))
        copies[-1].start()
    for copy in copies:
        copy.wait()


def call(kernel, outs, operands, flops, **options):
    moved = sum(value.size * value.dtype.itemsize for value in (*operands, *outs))
    vmem = pl.BlockSpec(memory_space=pltpu.VMEM)
    specs = [pl.BlockSpec(memory_space=pltpu.SMEM)] + [vmem] * (len(operands) - 1)
    settings = dict(in_specs=specs, out_specs=[vmem] * len(outs))
    settings.update(options)
    return pl.pallas_call(
        kernel,
        out_shape=outs,
        compiler_params=pltpu.CompilerParams(vmem_limit_bytes=16 * 1024 * 1024),
        cost_estimate=pl.CostEstimate(flops=flops, bytes_accessed=moved // 64, transcendentals=0),
        **settings,
    )(*operands)


def body(gradients, inverse_out, inverse_in, cross_out, cross_in, momentum):
    own_block = gradients[0, 0]
    tall, wide = own_block.shape
    count = lax.axis_size("rep")
    me = lax.axis_index("rep").astype(jnp.int32).reshape(1)
    widths = [share * wide // sum(SHARES) for share in SHARES]
    rows = momentum.shape[1]
    shape = jax.ShapeDtypeStruct
    part = functools.partial

    anywhere = pl.BlockSpec(memory_space=pl.ANY)
    out_rows, out_wide = cross_out.shape[1:]
    pair, *cuts = call(
        part(cut_kernel, widths),
        [shape((2 * out_rows, out_wide), HALF)]
        + [shape((inverse_in.shape[1], width), HALF) for width in widths],
        [me, cross_out[0], inverse_out[0], inverse_in[0]],
        0,
        in_specs=[pl.BlockSpec(memory_space=pltpu.SMEM)] + [anywhere] * 3,
        scratch_shapes=[pltpu.SemaphoreType.DMA((2 + len(widths),))],
    )
    pairs = from_peers(pair, "rep")
    in_blocks = [cross_in[0], *from_peers(cross_in[0], "rep")]
    following = passed_along(own_block, "layer", -1)

    cut_peers = [from_peers(piece, "rep") for piece in cuts]
    (first,) = call(
        part(first_kernel, count),
        [shape((tall, wide), HALF)],
        [me, following, cross_out[0], *pairs],
        tall * tall * wide // 32,
    )
    previous_blocks = [passed_along(block, "layer", 1) for block in in_blocks]
    (left,) = call(
        part(left_kernel, count),
        [shape((tall, wide), HALF)],
        [me, own_block, first, inverse_out[0], *in_blocks, *pairs],
        tall * wide * (tall + wide) // 32,
    )
    preconds, backs = [], []
    for at, (piece, peers) in enumerate(zip(cuts, cut_peers)):
        weight = 256 if at == len(cuts) - 1 else 1
        precond, back = call(
            part(chunk_kernel, count),
            [shape((tall, piece.shape[1]), HALF)] * 2,
            [me, left, cross_out[0], piece, *peers, *pairs],
            weight * tall * piece.shape[1] * (tall + wide) // 32,
        )
        preconds.append(precond)
        backs.append(passed_along(back, "layer", 1))
    partial, right_last = call(
        part(gather_kernel, count, widths),
        [shape((tall, wide), FULL), shape((wide, widths[-1]), HALF)],
        [me, *preconds[:-1], *backs[:-1], *previous_blocks],
        2 * tall * wide * (wide - widths[-1]),
        scratch_shapes=[
            pltpu.VMEM((tall, wide), HALF),
            pltpu.VMEM((tall, wide - widths[-1]), HALF),
        ],
    )
    squares, own, *sends = call(
        part(update_kernel, count),
        [shape((8, 128), FULL), shape((rows, wide), FULL)]
        + [shape((rows, wide), HALF)] * (count - 1),
        [me, partial, preconds[-1], backs[-1], right_last],
        2 * tall * wide * widths[-1],
    )
    blocks = [to_peer(value, "rep", at + 1) for at, value in enumerate(sends)]
    others = [to_peer(squares, "rep", step) for step in range(1, count)]
    operands = [momentum[0], squares, own, *others, *blocks]
    (result,) = call(
        part(final_kernel, count, tall * wide),
        [shape((rows, wide), FULL)],
        operands,
        4 * rows * wide,
        in_specs=[pl.BlockSpec(memory_space=pltpu.VMEM)] * len(operands),
        out_specs=[anywhere],
        scratch_shapes=[pltpu.VMEM((rows, wide), FULL), pltpu.SemaphoreType.DMA((4,))],
    )
    return result[None]


def solution(mesh):
    in_specs = (
        P("rep", "layer", None, None),
        P("layer", "rep", None),
        P("layer", "rep", None),
        P("layer", "rep", None),
        P("layer", "rep", None),
        P("layer", "rep", None),
    )
    out_specs = P("layer", "rep", None)
    return jax.shard_map(body, mesh=mesh, in_specs=in_specs, out_specs=out_specs, check_vma=False)
```

```python
import functools

import jax
import jax.numpy as jnp
from jax import lax
from jax.experimental import pallas as pl
from jax.experimental.pallas import tpu as pltpu
from jax.sharding import PartitionSpec as P

SHARES = (2, 1, 1)
TILE = 256
HALF = jnp.bfloat16
FULL = jnp.float32


def passed_along(value, axis, steps):
    count = lax.axis_size(axis)
    initial, last = (max(0, -steps), min(count, count - steps))
    return lax.ppermute(value, axis, [(source, source + steps) for source in range(initial, last)])


def passed_in_pairs(value, axis):
    count = lax.axis_size(axis)
    return [
        lax.ppermute(value, axis, [(source, source + 1) for source in range(first, count - 1, 2)])
        for first in (0, 1)
    ]


def from_peers(value, axis):
    count = lax.axis_size(axis)
    return [
        lax.ppermute(value, axis, [(source, (source - step) % count) for source in range(count)])
        for step in range(1, count)
    ]


def to_peer(value, axis, step):
    count = lax.axis_size(axis)
    return lax.ppermute(
        value, axis, [(source, (source + step) % count) for source in range(count)]
    )


def dot(left, right, contract=((1,), (0,))):
    return lax.dot_general(left, right, (contract, ((), ())), preferred_element_type=FULL)


def span(me_ref, step, count, size):
    start = lax.rem(me_ref[0] + step, count) * size
    return pl.ds(pl.multiple_of(start, size), size)


def cut_kernel(widths, me, cross_out, inverse_out, inverse_in, pair, *refs):
    pieces, sems = refs[:-1], refs[-1]
    rows, start = cross_out.shape[0], 0
    copies = [
        pltpu.make_async_copy(cross_out, pair.at[:rows], sems.at[0]),
        pltpu.make_async_copy(inverse_out, pair.at[rows:], sems.at[1]),
    ]
    for at, width in enumerate(widths):
        source = inverse_in.at[:, start : start + width]
        copies.append(pltpu.make_async_copy(source, pieces[at], sems.at[2 + at]))
        start += width
    for copy in copies:
        copy.start()
    for copy in copies:
        copy.wait()


def first_kernel(count, me, following, own, *refs):
    others, out = refs[: count - 1], refs[-1]
    rows = own.shape[0]

    @pl.loop(0, out.shape[1] // TILE)
    def _(at):
        columns = pl.ds(pl.multiple_of(at * TILE, TILE), TILE)
        right = following[:, columns]
        out[span(me, 0, count, rows), columns] = dot(own[...], right).astype(HALF)
        for step in range(1, count):
            block = others[step - 1][:rows, :]
            out[span(me, step, count, rows), columns] = dot(block, right).astype(HALF)


def left_kernel(count, me, grads, first, inv_own, *refs):
    rights, others, out = refs[:count], refs[count : 2 * count - 1], refs[2 * count - 1]
    depth, rows = rights[0].shape[0], inv_own.shape[0]

    @pl.loop(0, out.shape[1] // TILE)
    def _(at):
        columns = pl.ds(pl.multiple_of(at * TILE, TILE), TILE)
        cross = sum(
            dot(first[:, span(me, step, count, depth)], rights[step][:, columns])
            for step in range(count)
        )
        residual = (grads[:, columns].astype(FULL) - cross).astype(HALF)
        out[span(me, 0, count, rows), columns] = dot(inv_own[...], residual).astype(HALF)
        for step in range(1, count):
            block = others[step - 1][rows:, :]
            out[span(me, step, count, rows), columns] = dot(block, residual).astype(HALF)


def chunk_kernel(count, me, left, cross_own, own_piece, *refs):
    pieces, others = refs[: count - 1], refs[count - 1 : 2 * count - 2]
    precond, back = refs[-2:]
    depth, rows = own_piece.shape[0], cross_own.shape[0]
    product = dot(left[:, span(me, 0, count, depth)], own_piece[...])
    for step in range(1, count):
        product += dot(left[:, span(me, step, count, depth)], pieces[step - 1][...])
    precond[...] = product.astype(HALF)
    turned = ((0,), (0,))
    result = dot(cross_own[...], precond[span(me, 0, count, rows), :], turned)
    for step in range(1, count):
        block = others[step - 1][:rows, :]
        result += dot(block, precond[span(me, step, count, rows), :], turned)
    back[...] = result.astype(HALF)


def gather_kernel(count, widths, me, *refs):
    early = len(widths) - 1
    preconds, backs = refs[:early], refs[early : 2 * early]
    rights = refs[2 * early : 2 * early + count]
    partial, right_last, staged, stacked = refs[2 * early + count :]
    depth, known = rights[0].shape[0], stacked.shape[1]
    start = 0
    for at in range(early):
        here = slice(start, start + widths[at])
        staged[:, here] = preconds[at][...]
        stacked[:, here] = backs[at][...]
        start += widths[at]
    staged[:, known:] = jnp.zeros((staged.shape[0], staged.shape[1] - known), HALF)
    for step in range(count):
        columns = span(me, step, count, depth)
        right_last[columns, :] = rights[step][:, known:]
        right = rights[step][:, :known]
        for row in range(0, staged.shape[0], TILE):
            here = slice(row, row + TILE)
            product = dot(stacked[here, :], right, ((1,), (1,)))
            partial[here, columns] = staged[here, columns].astype(FULL) - product


def update_kernel(count, me, partial, precond, odd, even, right_last, *refs):
    squares, own = refs[:2]
    sends, back = refs[2:-1], refs[-1]
    back[...] = odd[...] + even[...]
    rows, wide = own.shape
    late = wide - precond.shape[1]
    total = jnp.zeros((), FULL)
    for step in range(count):
        here = span(me, step, count, rows)
        for start in range(0, wide, TILE):
            columns = slice(start, start + TILE)
            update = partial[here, columns] - dot(
                back[here, :], right_last[columns, :], ((1,), (1,))
            )
            if start + TILE > late:
                pad = jnp.zeros((rows, max(late - start, 0)), FULL)
                low = max(start - late, 0)
                tail = precond[here, low : start + TILE - late].astype(FULL)
                update += jnp.concatenate([pad, tail], axis=1) if pad.shape[1] else tail
            total += jnp.sum(update * update)
            if step == 0:
                own[:, columns] = update
            else:
                sends[step - 1][:, columns] = update.astype(HALF)
    squares[...] = jnp.full(squares.shape, total, FULL)


def scale_of(squares, size):
    return lax.rsqrt(squares * (1.0 / size) + 1e-06)


def final_kernel(count, size, momentum, squares, own, *refs):
    others, blocks = refs[: count - 1], refs[count - 1 : 2 * count - 2]
    out, scratch, sems = refs[-3:]
    rows = scratch.shape[0] // sems.shape[0]
    scales = [scale_of(value[0:1, 0:1], size) * (1.0 / count) for value in (squares, *others)]
    copies = []
    for at in range(sems.shape[0]):
        here = slice(at * rows, (at + 1) * rows)
        total = own[here, :] * scales[0]
        for step in range(count - 1):
            total += blocks[step][here, :].astype(FULL) * scales[step + 1]
        scratch[here, :] = 0.9 * momentum[here, :] + total
        copies.append(pltpu.make_async_copy(scratch.at[here, :], out.at[here, :], sems.at[at]))
        copies[-1].start()
    for copy in copies:
        copy.wait()


def call(kernel, outs, operands, flops, **options):
    moved = sum(value.size * value.dtype.itemsize for value in (*operands, *outs))
    vmem = pl.BlockSpec(memory_space=pltpu.VMEM)
    specs = [pl.BlockSpec(memory_space=pltpu.SMEM)] + [vmem] * (len(operands) - 1)
    settings = dict(in_specs=specs, out_specs=[vmem] * len(outs))
    settings.update(options)
    return pl.pallas_call(
        kernel,
        out_shape=outs,
        compiler_params=pltpu.CompilerParams(vmem_limit_bytes=16 * 1024 * 1024),
        cost_estimate=pl.CostEstimate(flops=flops, bytes_accessed=moved // 64, transcendentals=0),
        **settings,
    )(*operands)


def body(gradients, inverse_out, inverse_in, cross_out, cross_in, momentum):
    own_block = gradients[0, 0]
    tall, wide = own_block.shape
    count = lax.axis_size("rep")
    me = lax.axis_index("rep").astype(jnp.int32).reshape(1)
    widths = [share * wide // sum(SHARES) for share in SHARES]
    rows = momentum.shape[1]
    shape = jax.ShapeDtypeStruct
    part = functools.partial

    anywhere = pl.BlockSpec(memory_space=pl.ANY)
    out_rows, out_wide = cross_out.shape[1:]
    pair, *cuts = call(
        part(cut_kernel, widths),
        [shape((2 * out_rows, out_wide), HALF)]
        + [shape((inverse_in.shape[1], width), HALF) for width in widths],
        [me, cross_out[0], inverse_out[0], inverse_in[0]],
        0,
        in_specs=[pl.BlockSpec(memory_space=pltpu.SMEM)] + [anywhere] * 3,
        scratch_shapes=[pltpu.SemaphoreType.DMA((2 + len(widths),))],
    )
    pairs = from_peers(pair, "rep")
    in_blocks = [cross_in[0], *from_peers(cross_in[0], "rep")]
    following = passed_along(own_block, "layer", -1)

    cut_peers = [from_peers(piece, "rep") for piece in cuts]
    (first,) = call(
        part(first_kernel, count),
        [shape((tall, wide), HALF)],
        [me, following, cross_out[0], *pairs],
        tall * tall * wide // 32,
    )
    previous_blocks = [passed_along(block, "layer", 1) for block in in_blocks]
    (left,) = call(
        part(left_kernel, count),
        [shape((tall, wide), HALF)],
        [me, own_block, first, inverse_out[0], *in_blocks, *pairs],
        tall * wide * (tall + wide) // 32,
    )
    preconds, backs = [], []
    for at, (piece, peers) in enumerate(zip(cuts, cut_peers)):
        weight = 256 if at == len(cuts) - 1 else 1
        precond, back = call(
            part(chunk_kernel, count),
            [shape((tall, piece.shape[1]), HALF)] * 2,
            [me, left, cross_out[0], piece, *peers, *pairs],
            weight * tall * piece.shape[1] * (tall + wide) // 32,
        )
        preconds.append(precond)
        if at < len(cuts) - 1:
            backs.append(passed_along(back, "layer", 1))
    lasts = passed_in_pairs(back, "layer")
    partial, right_last = call(
        part(gather_kernel, count, widths),
        [shape((tall, wide), FULL), shape((wide, widths[-1]), HALF)],
        [me, *preconds[:-1], *backs, *previous_blocks],
        2 * tall * wide * (wide - widths[-1]),
        scratch_shapes=[
            pltpu.VMEM((tall, wide), HALF),
            pltpu.VMEM((tall, wide - widths[-1]), HALF),
        ],
    )
    squares, own, *sends = call(
        part(update_kernel, count),
        [shape((8, 128), FULL), shape((rows, wide), FULL)]
        + [shape((rows, wide), HALF)] * (count - 1),
        [me, partial, preconds[-1], *lasts, right_last],
        2 * tall * wide * widths[-1],
        scratch_shapes=[pltpu.VMEM((tall, widths[-1]), HALF)],
    )
    blocks = [to_peer(value, "rep", at + 1) for at, value in enumerate(sends)]
    others = [to_peer(squares, "rep", step) for step in range(1, count)]
    operands = [momentum[0], squares, own, *others, *blocks]
    (result,) = call(
        part(final_kernel, count, tall * wide),
        [shape((rows, wide), FULL)],
        operands,
        4 * rows * wide,
        in_specs=[pl.BlockSpec(memory_space=pltpu.VMEM)] * len(operands),
        out_specs=[anywhere],
        scratch_shapes=[pltpu.VMEM((rows, wide), FULL), pltpu.SemaphoreType.DMA((4,))],
    )
    return result[None]


def solution(mesh):
    in_specs = (
        P("rep", "layer", None, None),
        P("layer", "rep", None),
        P("layer", "rep", None),
        P("layer", "rep", None),
        P("layer", "rep", None),
        P("layer", "rep", None),
    )
    out_specs = P("layer", "rep", None)
    return jax.shard_map(body, mesh=mesh, in_specs=in_specs, out_specs=out_specs, check_vma=False)
```

```python
import functools

import jax
import jax.numpy as jnp
from jax import lax
from jax.experimental import pallas as pl
from jax.experimental.pallas import tpu as pltpu
from jax.sharding import PartitionSpec as P

SHARES = (2, 1, 1)
ROWS = 16
TILE = 256
HALF = jnp.bfloat16
FULL = jnp.float32


def passed_along(value, axis, steps):
    count = lax.axis_size(axis)
    initial, last = (max(0, -steps), min(count, count - steps))
    return lax.ppermute(value, axis, [(source, source + steps) for source in range(initial, last)])


def from_peers(value, axis):
    count = lax.axis_size(axis)
    return [
        lax.ppermute(value, axis, [(source, (source - step) % count) for source in range(count)])
        for step in range(1, count)
    ]


def to_peer(value, axis, step):
    count = lax.axis_size(axis)
    return lax.ppermute(
        value, axis, [(source, (source + step) % count) for source in range(count)]
    )


def dot(left, right, contract=((1,), (0,))):
    return lax.dot_general(left, right, (contract, ((), ())), preferred_element_type=FULL)


def span(me_ref, step, count, size):
    start = lax.rem(me_ref[0] + step, count) * size
    return pl.ds(pl.multiple_of(start, size), size)


def cut_kernel(widths, me, cross_out, inverse_out, inverse_in, pair, *refs):
    pieces, sems = refs[:-1], refs[-1]
    rows, start = cross_out.shape[0], 0
    copies = [
        pltpu.make_async_copy(cross_out, pair.at[:rows], sems.at[0]),
        pltpu.make_async_copy(inverse_out, pair.at[rows:], sems.at[1]),
    ]
    for at, width in enumerate(widths):
        source = inverse_in.at[:, start : start + width]
        copies.append(pltpu.make_async_copy(source, pieces[at], sems.at[2 + at]))
        start += width
    for copy in copies:
        copy.start()
    for copy in copies:
        copy.wait()


def first_kernel(count, me, following, own, *refs):
    others, out = refs[: count - 1], refs[-1]
    rows = own.shape[0]

    @pl.loop(0, out.shape[1] // TILE)
    def _(at):
        columns = pl.ds(pl.multiple_of(at * TILE, TILE), TILE)
        right = following[:, columns]
        out[span(me, 0, count, rows), columns] = dot(own[...], right).astype(HALF)
        for step in range(1, count):
            block = others[step - 1][:rows, :]
            out[span(me, step, count, rows), columns] = dot(block, right).astype(HALF)


def left_kernel(count, me, grads, first, inv_own, *refs):
    rights, others, out = refs[:count], refs[count : 2 * count - 1], refs[2 * count - 1]
    depth, rows = rights[0].shape[0], inv_own.shape[0]

    @pl.loop(0, out.shape[1] // TILE)
    def _(at):
        columns = pl.ds(pl.multiple_of(at * TILE, TILE), TILE)
        cross = sum(
            dot(first[:, span(me, step, count, depth)], rights[step][:, columns])
            for step in range(count)
        )
        residual = (grads[:, columns].astype(FULL) - cross).astype(HALF)
        out[span(me, 0, count, rows), columns] = dot(inv_own[...], residual).astype(HALF)
        for step in range(1, count):
            block = others[step - 1][rows:, :]
            out[span(me, step, count, rows), columns] = dot(block, residual).astype(HALF)


def chunk_kernel(count, me, left, cross_own, own_piece, *refs):
    pieces, others = refs[: count - 1], refs[count - 1 : 2 * count - 2]
    precond, back = refs[-2:]
    depth, rows = own_piece.shape[0], cross_own.shape[0]
    product = dot(left[:, span(me, 0, count, depth)], own_piece[...])
    for step in range(1, count):
        product += dot(left[:, span(me, step, count, depth)], pieces[step - 1][...])
    precond[...] = product.astype(HALF)
    turned = ((0,), (0,))
    result = dot(cross_own[...], precond[span(me, 0, count, rows), :], turned)
    for step in range(1, count):
        block = others[step - 1][:rows, :]
        result += dot(block, precond[span(me, step, count, rows), :], turned)
    back[...] = result.astype(HALF)


def stack(target, values, lines=slice(None)):
    start = 0
    for value in values:
        target[:, start : start + value.shape[1]] = value[lines, :]
        start += value.shape[1]


def early_kernel(count, rows, me, *refs):
    total = len(SHARES)
    preconds, backs = refs[:total], refs[total : 2 * total - 1]
    rights = refs[2 * total - 1 : 2 * total - 1 + count]
    nears, (right_last, staged, stacked) = refs[2 * total - 1 + count : -3], refs[-3:]
    depth, known, near = rights[0].shape[0], stacked.shape[1], staged.shape[0]
    for row_step in range(1, count):
        start = lax.rem(me[0] + row_step, count) * rows
        lines = pl.ds(pl.multiple_of(start, ROWS), near)
        stack(staged, preconds, lines)
        stack(stacked, backs, lines)
        for step in range(count):
            columns = span(me, step, count, depth)
            product = dot(stacked[...], rights[step][:, :known], ((1,), (1,)))
            update = staged[:, columns].astype(FULL) - product
            nears[row_step - 1][:, columns] = update.astype(HALF)
    for step in range(count):
        right_last[span(me, step, count, depth), :] = rights[step][:, known:]


def gather_kernel(count, me, *refs):
    total = len(SHARES)
    preconds, backs = refs[:total], refs[total : 2 * total - 1]
    rights = refs[2 * total - 1 : 2 * total - 1 + count]
    partial, staged, stacked = refs[2 * total - 1 + count :]
    depth, known = rights[0].shape[0], stacked.shape[1]
    stack(staged, preconds)
    stack(stacked, backs)
    for step in range(count):
        columns = span(me, step, count, depth)
        right = rights[step][:, :known]
        for row in range(0, staged.shape[0], TILE):
            here = slice(row, row + TILE)
            product = dot(stacked[here, :], right, ((1,), (1,)))
            partial[here, columns] = staged[here, columns].astype(FULL) - product


def update_kernel(count, me, partial, back, right_last, *refs):
    squares, own = refs[:2]
    fars, rests = refs[2 : count + 1], refs[count + 1 :]
    rows, wide = own.shape
    total = jnp.zeros((), FULL)
    for step in range(count):
        here = span(me, step, count, rows)
        for start in range(0, wide, TILE):
            columns = slice(start, start + TILE)
            update = partial[here, columns] - dot(
                back[here, :], right_last[columns, :], ((1,), (1,))
            )
            total += jnp.sum(update * update)
            if step == 0:
                own[:, columns] = update
            else:
                near = rows - fars[step - 1].shape[0]
                fars[step - 1][:, columns] = update[near:].astype(HALF)
        if step:
            start = lax.rem(me[0] + step, count) * rows
            lines = pl.ds(pl.multiple_of(start, ROWS), rests[step - 1].shape[0])
            rests[step - 1][...] = back[lines, :]
    squares[...] = jnp.full(squares.shape, total, FULL)


def scale_of(squares, size):
    return lax.rsqrt(squares * (1.0 / size) + 1e-06)


def final_kernel(count, size, momentum, squares, own, right_last, *refs):
    peers = count - 1
    others, nears, fars, rests = (refs[at * peers : (at + 1) * peers] for at in range(4))
    out, scratch, sems = refs[-3:]
    near = nears[0].shape[0]
    scales = [scale_of(value[0:1, 0:1], size) * (1.0 / count) for value in (squares, *others)]
    copies = []
    for part, here in enumerate((slice(0, near), slice(near, scratch.shape[0]))):
        total = own[here, :] * scales[0]
        for step in range(peers):
            if part:
                update = fars[step][...].astype(FULL)
            else:
                rest = dot(rests[step][...], right_last[...], ((1,), (1,)))
                update = nears[step][...].astype(FULL) - rest
            total += update * scales[step + 1]
        scratch[here, :] = 0.9 * momentum[here, :] + total
        copies.append(
            pltpu.make_async_copy(scratch.at[here, :], out.at[here, :], sems.at[part])
        )
        copies[-1].start()
    for copy in copies:
        copy.wait()


def call(kernel, outs, operands, flops, **options):
    moved = sum(value.size * value.dtype.itemsize for value in (*operands, *outs))
    vmem = pl.BlockSpec(memory_space=pltpu.VMEM)
    specs = [pl.BlockSpec(memory_space=pltpu.SMEM)] + [vmem] * (len(operands) - 1)
    settings = dict(in_specs=specs, out_specs=[vmem] * len(outs))
    settings.update(options)
    return pl.pallas_call(
        kernel,
        out_shape=outs,
        compiler_params=pltpu.CompilerParams(vmem_limit_bytes=16 * 1024 * 1024),
        cost_estimate=pl.CostEstimate(flops=flops, bytes_accessed=moved // 64, transcendentals=0),
        **settings,
    )(*operands)


def body(gradients, inverse_out, inverse_in, cross_out, cross_in, momentum):
    own_block = gradients[0, 0]
    tall, wide = own_block.shape
    count = lax.axis_size("rep")
    me = lax.axis_index("rep").astype(jnp.int32).reshape(1)
    widths = [share * wide // sum(SHARES) for share in SHARES]
    rows = momentum.shape[1]
    shape = jax.ShapeDtypeStruct
    part = functools.partial

    anywhere = pl.BlockSpec(memory_space=pl.ANY)
    out_rows, out_wide = cross_out.shape[1:]
    pair, *cuts = call(
        part(cut_kernel, widths),
        [shape((2 * out_rows, out_wide), HALF)]
        + [shape((inverse_in.shape[1], width), HALF) for width in widths],
        [me, cross_out[0], inverse_out[0], inverse_in[0]],
        0,
        in_specs=[pl.BlockSpec(memory_space=pltpu.SMEM)] + [anywhere] * 3,
        scratch_shapes=[pltpu.SemaphoreType.DMA((2 + len(widths),))],
    )
    pairs = from_peers(pair, "rep")
    in_blocks = [cross_in[0], *from_peers(cross_in[0], "rep")]
    following = passed_along(own_block, "layer", -1)

    cut_peers = [from_peers(piece, "rep") for piece in cuts]
    (first,) = call(
        part(first_kernel, count),
        [shape((tall, wide), HALF)],
        [me, following, cross_out[0], *pairs],
        tall * tall * wide // 32,
    )
    previous_blocks = [passed_along(block, "layer", 1) for block in in_blocks]
    (left,) = call(
        part(left_kernel, count),
        [shape((tall, wide), HALF)],
        [me, own_block, first, inverse_out[0], *in_blocks, *pairs],
        tall * wide * (tall + wide) // 32,
    )
    preconds, backs = [], []
    for at, (piece, peers) in enumerate(zip(cuts, cut_peers)):
        weight = 256 if at == len(cuts) - 1 else 1
        precond, back = call(
            part(chunk_kernel, count),
            [shape((tall, piece.shape[1]), HALF)] * 2,
            [me, left, cross_out[0], piece, *peers, *pairs],
            weight * tall * piece.shape[1] * (tall + wide) // 32,
        )
        preconds.append(precond)
        backs.append(passed_along(back, "layer", 1))
    near = 5 * rows // 8 // ROWS * ROWS
    peers, last = count - 1, widths[-1]
    *nears, right_last = call(
        part(early_kernel, count, rows),
        [shape((near, wide), HALF)] * peers + [shape((wide, last), HALF)],
        [me, *preconds, *backs[:-1], *previous_blocks],
        2 * peers * near * wide * (wide - last),
        scratch_shapes=[pltpu.VMEM((near, wide), HALF), pltpu.VMEM((near, wide - last), HALF)],
    )
    nears = [to_peer(value, "rep", at + 1) for at, value in enumerate(nears)]
    (partial,) = call(
        part(gather_kernel, count),
        [shape((tall, wide), FULL)],
        [me, *preconds, *backs[:-1], *previous_blocks],
        2 * tall * wide * (wide - last),
        scratch_shapes=[pltpu.VMEM((tall, wide), HALF), pltpu.VMEM((tall, wide - last), HALF)],
    )
    squares, own, *sends = call(
        part(update_kernel, count),
        [shape((8, 128), FULL), shape((rows, wide), FULL)]
        + [shape((rows - near, wide), HALF)] * peers
        + [shape((near, last), HALF)] * peers,
        [me, partial, backs[-1], right_last],
        2 * tall * wide * last,
    )
    sends = [to_peer(value, "rep", at % peers + 1) for at, value in enumerate(sends)]
    others = [to_peer(squares, "rep", step) for step in range(1, count)]
    operands = [momentum[0], squares, own, right_last, *others, *nears, *sends]
    (result,) = call(
        part(final_kernel, count, tall * wide),
        [shape((rows, wide), FULL)],
        operands,
        4 * rows * wide,
        in_specs=[pl.BlockSpec(memory_space=pltpu.VMEM)] * len(operands),
        out_specs=[anywhere],
        scratch_shapes=[pltpu.VMEM((rows, wide), FULL), pltpu.SemaphoreType.DMA((2,))],
    )
    return result[None]


def solution(mesh):
    in_specs = (
        P("rep", "layer", None, None),
        P("layer", "rep", None),
        P("layer", "rep", None),
        P("layer", "rep", None),
        P("layer", "rep", None),
        P("layer", "rep", None),
    )
    out_specs = P("layer", "rep", None)
    return jax.shard_map(body, mesh=mesh, in_specs=in_specs, out_specs=out_specs, check_vma=False)
```

```python
import functools

import jax
import jax.numpy as jnp
from jax import lax
from jax.experimental import pallas as pl
from jax.experimental.pallas import tpu as pltpu
from jax.sharding import PartitionSpec as P

SHARES = (2, 1, 1)
ROWS = 16
TILE = 256
HALF = jnp.bfloat16
FULL = jnp.float32


def passed_along(value, axis, steps):
    count = lax.axis_size(axis)
    initial, last = (max(0, -steps), min(count, count - steps))
    return lax.ppermute(value, axis, [(source, source + steps) for source in range(initial, last)])


def from_peers(value, axis):
    count = lax.axis_size(axis)
    return [
        lax.ppermute(value, axis, [(source, (source - step) % count) for source in range(count)])
        for step in range(1, count)
    ]


def to_peer(value, axis, step):
    count = lax.axis_size(axis)
    return lax.ppermute(
        value, axis, [(source, (source + step) % count) for source in range(count)]
    )


def dot(left, right, contract=((1,), (0,))):
    return lax.dot_general(left, right, (contract, ((), ())), preferred_element_type=FULL)


def span(me_ref, step, count, size):
    start = lax.rem(me_ref[0] // 2 + step, count) * size
    return pl.ds(pl.multiple_of(start, size), size)


def copied(copies):
    for copy in copies:
        copy.start()
    for copy in copies:
        copy.wait()


def columns_of(source, targets, sems):
    start, copies = 0, []
    for at, target in enumerate(targets):
        width = target.shape[1]
        block = source.at[:, start : start + width]
        copies.append(pltpu.make_async_copy(block, target, sems.at[at]))
        start += width
    return copies


def cut_kernel(parity, me, cross_out, inverse_out, inverse_in, *refs):
    pair, *pieces, sems = refs[-2 - len(SHARES) :]
    rows, last = cross_out.shape[0], len(SHARES)

    @pl.when(me[0] % 2 == parity)
    def _():
        copied(
            columns_of(inverse_in, pieces, sems)
            + [
                pltpu.make_async_copy(cross_out, pair.at[:rows], sems.at[last]),
                pltpu.make_async_copy(inverse_out, pair.at[rows:], sems.at[last + 1]),
            ]
        )


def keep_kernel(me, inverse_in, *refs):
    copied(columns_of(inverse_in, refs[:-1], refs[-1]))


def first_kernel(count, me, following, own, *refs):
    others, out = refs[: count - 1], refs[-1]
    rows = own.shape[0]

    @pl.loop(0, out.shape[1] // TILE)
    def _(at):
        columns = pl.ds(pl.multiple_of(at * TILE, TILE), TILE)
        right = following[:, columns]
        out[span(me, 0, count, rows), columns] = dot(own[...], right).astype(HALF)
        for step in range(1, count):
            block = others[step - 1][:rows, :]
            out[span(me, step, count, rows), columns] = dot(block, right).astype(HALF)


def left_kernel(count, me, grads, first, inv_own, *refs):
    rights, others, out = refs[:count], refs[count : 2 * count - 1], refs[2 * count - 1]
    depth, rows = rights[0].shape[0], inv_own.shape[0]

    @pl.loop(0, out.shape[1] // TILE)
    def _(at):
        columns = pl.ds(pl.multiple_of(at * TILE, TILE), TILE)
        cross = sum(
            dot(first[:, span(me, step, count, depth)], rights[step][:, columns])
            for step in range(count)
        )
        residual = (grads[:, columns].astype(FULL) - cross).astype(HALF)
        out[span(me, 0, count, rows), columns] = dot(inv_own[...], residual).astype(HALF)
        for step in range(1, count):
            block = others[step - 1][rows:, :]
            out[span(me, step, count, rows), columns] = dot(block, residual).astype(HALF)


def chunk_kernel(count, me, left, cross_own, own_piece, *refs):
    pieces, others = refs[: count - 1], refs[count - 1 : 2 * count - 2]
    precond, back = refs[-2:]
    depth, rows = own_piece.shape[0], cross_own.shape[0]
    product = dot(left[:, span(me, 0, count, depth)], own_piece[...])
    for step in range(1, count):
        product += dot(left[:, span(me, step, count, depth)], pieces[step - 1][...])
    precond[...] = product.astype(HALF)
    turned = ((0,), (0,))
    result = dot(cross_own[...], precond[span(me, 0, count, rows), :], turned)
    for step in range(1, count):
        block = others[step - 1][:rows, :]
        result += dot(block, precond[span(me, step, count, rows), :], turned)
    back[...] = result.astype(HALF)


def stack(target, values, lines=slice(None)):
    start = 0
    for value in values:
        target[:, start : start + value.shape[1]] = value[lines, :]
        start += value.shape[1]


def early_kernel(count, rows, me, *refs):
    total = len(SHARES)
    preconds, backs = refs[:total], refs[total : 2 * total - 1]
    rights = refs[2 * total - 1 : 2 * total - 1 + count]
    nears, (right_last, staged, stacked) = refs[2 * total - 1 + count : -3], refs[-3:]
    depth, known, near = rights[0].shape[0], stacked.shape[1], staged.shape[0]
    for row_step in range(1, count):
        start = lax.rem(me[0] // 2 + row_step, count) * rows
        lines = pl.ds(pl.multiple_of(start, ROWS), near)
        stack(staged, preconds, lines)
        stack(stacked, backs, lines)
        for step in range(count):
            columns = span(me, step, count, depth)
            product = dot(stacked[...], rights[step][:, :known], ((1,), (1,)))
            update = staged[:, columns].astype(FULL) - product
            nears[row_step - 1][:, columns] = update.astype(HALF)
    for step in range(count):
        right_last[span(me, step, count, depth), :] = rights[step][:, known:]


def gather_kernel(count, me, *refs):
    total = len(SHARES)
    preconds, backs = refs[:total], refs[total : 2 * total - 1]
    rights = refs[2 * total - 1 : 2 * total - 1 + count]
    partial, staged, stacked = refs[2 * total - 1 + count :]
    depth, known = rights[0].shape[0], stacked.shape[1]
    stack(staged, preconds)
    stack(stacked, backs)
    for step in range(count):
        columns = span(me, step, count, depth)
        right = rights[step][:, :known]
        for row in range(0, staged.shape[0], TILE):
            here = slice(row, row + TILE)
            product = dot(stacked[here, :], right, ((1,), (1,)))
            partial[here, columns] = staged[here, columns].astype(FULL) - product


def update_kernel(count, me, partial, back, right_last, *refs):
    squares, own = refs[:2]
    fars, rests = refs[2 : count + 1], refs[count + 1 :]
    rows, wide = own.shape
    total = jnp.zeros((), FULL)
    for step in range(count):
        here = span(me, step, count, rows)
        for start in range(0, wide, TILE):
            columns = slice(start, start + TILE)
            update = partial[here, columns] - dot(
                back[here, :], right_last[columns, :], ((1,), (1,))
            )
            total += jnp.sum(update * update)
            if step == 0:
                own[:, columns] = update
            else:
                near = rows - fars[step - 1].shape[0]
                fars[step - 1][:, columns] = update[near:].astype(HALF)
        if step:
            start = lax.rem(me[0] // 2 + step, count) * rows
            lines = pl.ds(pl.multiple_of(start, ROWS), rests[step - 1].shape[0])
            rests[step - 1][...] = back[lines, :]
    squares[...] = jnp.full(squares.shape, total, FULL)


def scale_of(squares, size):
    return lax.rsqrt(squares * (1.0 / size) + 1e-06)


def final_kernel(count, size, momentum, squares, own, right_last, *refs):
    peers = count - 1
    others, nears, fars, rests = (refs[at * peers : (at + 1) * peers] for at in range(4))
    out, scratch, sems = refs[-3:]
    near = nears[0].shape[0]
    scales = [scale_of(value[0:1, 0:1], size) * (1.0 / count) for value in (squares, *others)]
    copies = []
    for part, here in enumerate((slice(0, near), slice(near, scratch.shape[0]))):
        total = own[here, :] * scales[0]
        for step in range(peers):
            if part:
                update = fars[step][...].astype(FULL)
            else:
                rest = dot(rests[step][...], right_last[...], ((1,), (1,)))
                update = nears[step][...].astype(FULL) - rest
            total += update * scales[step + 1]
        scratch[here, :] = 0.9 * momentum[here, :] + total
        copies.append(
            pltpu.make_async_copy(scratch.at[here, :], out.at[here, :], sems.at[part])
        )
        copies[-1].start()
    for copy in copies:
        copy.wait()


def call(kernel, outs, operands, flops, grant=16, **options):
    moved = sum(value.size * value.dtype.itemsize for value in (*operands, *outs))
    vmem = pl.BlockSpec(memory_space=pltpu.VMEM)
    specs = [pl.BlockSpec(memory_space=pltpu.SMEM)] + [vmem] * (len(operands) - 1)
    settings = dict(in_specs=specs, out_specs=[vmem] * len(outs))
    settings.update(options)
    return pl.pallas_call(
        kernel,
        out_shape=outs,
        compiler_params=pltpu.CompilerParams(vmem_limit_bytes=grant * 1024 * 1024),
        cost_estimate=pl.CostEstimate(flops=flops, bytes_accessed=moved // 64, transcendentals=0),
        **settings,
    )(*operands)


def body(gradients, inverse_out, inverse_in, cross_out, cross_in, momentum):
    own_block = gradients[0, 0]
    tall, wide = own_block.shape
    count = lax.axis_size("rep")
    me = (2 * lax.axis_index("rep") + lax.axis_index("layer") % 2).astype(jnp.int32).reshape(1)
    widths = [share * wide // sum(SHARES) for share in SHARES]
    rows = momentum.shape[1]
    shape = jax.ShapeDtypeStruct
    part = functools.partial

    anywhere = pl.BlockSpec(memory_space=pl.ANY)
    out_rows, out_wide = cross_out.shape[1:]
    result = []
    for parity in (1, 0):
        operands = [me, cross_out[0], inverse_out[0], inverse_in[0], *result]
        result = call(
            part(cut_kernel, parity),
            [shape((2 * out_rows, out_wide), HALF)]
            + [shape((inverse_in.shape[1], width), HALF) for width in widths],
            operands,
            0,
            60,
            in_specs=[pl.BlockSpec(memory_space=pltpu.SMEM)] + [anywhere] * (len(operands) - 1),
            out_specs=[anywhere] * (1 + len(widths)),
            scratch_shapes=[pltpu.SemaphoreType.DMA((2 + len(widths),))],
            input_output_aliases={4 + at: at for at in range(len(result))},
        )
        if parity:
            cross_in, *result = lax.optimization_barrier((cross_in, *result))
    sent_block, pair, *cuts = lax.optimization_barrier((own_block, *result))
    kept = call(
        keep_kernel,
        [shape(value.shape, HALF) for value in cuts],
        [me, inverse_in[0]],
        0,
        in_specs=[pl.BlockSpec(memory_space=pltpu.SMEM), anywhere],
        scratch_shapes=[pltpu.SemaphoreType.DMA((len(widths),))],
    )
    pairs = from_peers(pair, "rep")
    in_blocks = [cross_in[0], *from_peers(cross_in[0], "rep")]
    following = passed_along(sent_block, "layer", -1)

    cut_peers = [from_peers(piece, "rep") for piece in cuts]
    (first,) = call(
        part(first_kernel, count),
        [shape((tall, wide), HALF)],
        [me, following, cross_out[0], *pairs],
        tall * tall * wide // 32,
    )
    previous_blocks = [passed_along(block, "layer", 1) for block in in_blocks]
    (left,) = call(
        part(left_kernel, count),
        [shape((tall, wide), HALF)],
        [me, own_block, first, inverse_out[0], *in_blocks, *pairs],
        tall * wide * (tall + wide) // 32,
    )
    preconds, backs = [], []
    for at, (piece, peers) in enumerate(zip(kept, cut_peers)):
        weight = 256 if at == len(cuts) - 1 else 1
        precond, back = call(
            part(chunk_kernel, count),
            [shape((tall, piece.shape[1]), HALF)] * 2,
            [me, left, cross_out[0], piece, *peers, *pairs],
            weight * tall * piece.shape[1] * (tall + wide) // 32,
        )
        preconds.append(precond)
        backs.append(passed_along(back, "layer", 1))
    near = 5 * rows // 8 // ROWS * ROWS
    peers, last = count - 1, widths[-1]
    *nears, right_last = call(
        part(early_kernel, count, rows),
        [shape((near, wide), HALF)] * peers + [shape((wide, last), HALF)],
        [me, *preconds, *backs[:-1], *previous_blocks],
        2 * peers * near * wide * (wide - last),
        scratch_shapes=[pltpu.VMEM((near, wide), HALF), pltpu.VMEM((near, wide - last), HALF)],
    )
    nears = [to_peer(value, "rep", at + 1) for at, value in enumerate(nears)]
    (partial,) = call(
        part(gather_kernel, count),
        [shape((tall, wide), FULL)],
        [me, *preconds, *backs[:-1], *previous_blocks],
        2 * tall * wide * (wide - last),
        scratch_shapes=[pltpu.VMEM((tall, wide), HALF), pltpu.VMEM((tall, wide - last), HALF)],
    )
    squares, own, *sends = call(
        part(update_kernel, count),
        [shape((8, 128), FULL), shape((rows, wide), FULL)]
        + [shape((rows - near, wide), HALF)] * peers
        + [shape((near, last), HALF)] * peers,
        [me, partial, backs[-1], right_last],
        2 * tall * wide * last,
    )
    sends = [to_peer(value, "rep", at % peers + 1) for at, value in enumerate(sends)]
    others = [to_peer(squares, "rep", step) for step in range(1, count)]
    operands = [momentum[0], squares, own, right_last, *others, *nears, *sends]
    (result,) = call(
        part(final_kernel, count, tall * wide),
        [shape((rows, wide), FULL)],
        operands,
        4 * rows * wide,
        in_specs=[pl.BlockSpec(memory_space=pltpu.VMEM)] * len(operands),
        out_specs=[anywhere],
        scratch_shapes=[pltpu.VMEM((rows, wide), FULL), pltpu.SemaphoreType.DMA((2,))],
    )
    return result[None]


def solution(mesh):
    in_specs = (
        P("rep", "layer", None, None),
        P("layer", "rep", None),
        P("layer", "rep", None),
        P("layer", "rep", None),
        P("layer", "rep", None),
        P("layer", "rep", None),
    )
    out_specs = P("layer", "rep", None)
    return jax.shard_map(body, mesh=mesh, in_specs=in_specs, out_specs=out_specs, check_vma=False)
```

```python
import functools

import jax
import jax.numpy as jnp
from jax import lax
from jax.experimental import pallas as pl
from jax.experimental.pallas import tpu as pltpu
from jax.sharding import PartitionSpec as P

SHARES = (3, 2, 2, 1)
EARLY = 2
ROWS = 16
TILE = 256
HALF = jnp.bfloat16
FULL = jnp.float32


def passed_along(value, axis, steps):
    count = lax.axis_size(axis)
    initial, last = (max(0, -steps), min(count, count - steps))
    return lax.ppermute(value, axis, [(source, source + steps) for source in range(initial, last)])


def from_peers(value, axis):
    count = lax.axis_size(axis)
    return [
        lax.ppermute(value, axis, [(source, (source - step) % count) for source in range(count)])
        for step in range(1, count)
    ]


def to_peer(value, axis, step):
    count = lax.axis_size(axis)
    return lax.ppermute(
        value, axis, [(source, (source + step) % count) for source in range(count)]
    )


def dot(left, right, contract=((1,), (0,))):
    return lax.dot_general(left, right, (contract, ((), ())), preferred_element_type=FULL)


def span(me_ref, step, count, size):
    start = lax.rem(me_ref[0] + step, count) * size
    return pl.ds(pl.multiple_of(start, size), size)


def cut_kernel(widths, me, cross_out, inverse_out, inverse_in, pair, *refs):
    pieces, sems = refs[:-1], refs[-1]
    rows, start = cross_out.shape[0], 0
    copies = [
        pltpu.make_async_copy(cross_out, pair.at[:rows], sems.at[0]),
        pltpu.make_async_copy(inverse_out, pair.at[rows:], sems.at[1]),
    ]
    for at, width in enumerate(widths):
        source = inverse_in.at[:, start : start + width]
        copies.append(pltpu.make_async_copy(source, pieces[at], sems.at[2 + at]))
        start += width
    for copy in copies:
        copy.start()
    for copy in copies:
        copy.wait()


def first_kernel(count, me, following, own, *refs):
    others, out = refs[: count - 1], refs[-1]
    rows = own.shape[0]

    @pl.loop(0, out.shape[1] // TILE)
    def _(at):
        columns = pl.ds(pl.multiple_of(at * TILE, TILE), TILE)
        right = following[:, columns]
        out[span(me, 0, count, rows), columns] = dot(own[...], right).astype(HALF)
        for step in range(1, count):
            block = others[step - 1][:rows, :]
            out[span(me, step, count, rows), columns] = dot(block, right).astype(HALF)


def left_kernel(count, me, grads, first, inv_own, *refs):
    rights, others, out = refs[:count], refs[count : 2 * count - 1], refs[-1]
    depth, rows = rights[0].shape[0], inv_own.shape[0]

    @pl.loop(0, out.shape[1] // TILE)
    def _(at):
        columns = pl.ds(pl.multiple_of(at * TILE, TILE), TILE)
        cross = sum(
            dot(first[:, span(me, step, count, depth)], rights[step][:, columns])
            for step in range(count)
        )
        residual = (grads[:, columns].astype(FULL) - cross).astype(HALF)
        out[span(me, 0, count, rows), columns] = dot(inv_own[...], residual).astype(HALF)
        for step in range(1, count):
            block = others[step - 1][rows:, :]
            out[span(me, step, count, rows), columns] = dot(block, residual).astype(HALF)


def chunk_kernel(count, me, left, cross_own, own_piece, *refs):
    pieces, others = refs[: count - 1], refs[count - 1 : 2 * count - 2]
    precond, back = refs[-2:]
    depth, rows = own_piece.shape[0], cross_own.shape[0]
    product = dot(left[:, span(me, 0, count, depth)], own_piece[...])
    for step in range(1, count):
        product += dot(left[:, span(me, step, count, depth)], pieces[step - 1][...])
    precond[...] = product.astype(HALF)
    turned = ((0,), (0,))
    result = dot(cross_own[...], precond[span(me, 0, count, rows), :], turned)
    for step in range(1, count):
        block = others[step - 1][:rows, :]
        result += dot(block, precond[span(me, step, count, rows), :], turned)
    back[...] = result.astype(HALF)


def stack(target, values, lines=slice(None)):
    start = 0
    for value in values:
        target[:, start : start + value.shape[1]] = value[lines, :]
        start += value.shape[1]


def early_kernel(count, rows, me, *refs):
    total = len(SHARES)
    preconds, backs = refs[:total], refs[total : total + EARLY]
    rights = refs[total + EARLY : total + EARLY + count]
    nears, (right_last, staged, stacked) = refs[total + EARLY + count : -3], refs[-3:]
    depth, known, near = rights[0].shape[0], stacked.shape[1], staged.shape[0]
    for row_step in range(1, count):
        start = lax.rem(me[0] + row_step, count) * rows
        lines = pl.ds(pl.multiple_of(start, ROWS), near)
        stack(staged, preconds, lines)
        stack(stacked, backs, lines)
        for step in range(count):
            columns = span(me, step, count, depth)
            product = dot(stacked[...], rights[step][:, :known], ((1,), (1,)))
            update = staged[:, columns].astype(FULL) - product
            nears[row_step - 1][:, columns] = update.astype(HALF)
    for step in range(count):
        right_last[span(me, step, count, depth), :] = rights[step][:, known:]


def gather_kernel(count, me, *refs):
    total = len(SHARES)
    preconds, backs = refs[:total], refs[total : 2 * total - 1]
    rights = refs[2 * total - 1 : 2 * total - 1 + count]
    partial, staged, stacked = refs[2 * total - 1 + count :]
    depth, known = rights[0].shape[0], stacked.shape[1]
    stack(staged, preconds)
    stack(stacked, backs)
    for step in range(count):
        columns = span(me, step, count, depth)
        right = rights[step][:, :known]
        for row in range(0, staged.shape[0], TILE):
            here = slice(row, row + TILE)
            product = dot(stacked[here, :], right, ((1,), (1,)))
            partial[here, columns] = staged[here, columns].astype(FULL) - product


def update_kernel(count, me, partial, right_last, *refs):
    backs, refs = refs[: len(SHARES) - EARLY], refs[len(SHARES) - EARLY :]
    squares, own = refs[:2]
    fars, rests = refs[2 : count + 1], refs[count + 1 :]
    rows, wide = own.shape
    back = backs[-1]
    late = right_last.shape[1] - back.shape[1]
    total = jnp.zeros((), FULL)
    for step in range(count):
        here = span(me, step, count, rows)
        for start in range(0, wide, TILE):
            columns = slice(start, start + TILE)
            update = partial[here, columns] - dot(
                back[here, :], right_last[columns, late:], ((1,), (1,))
            )
            total += jnp.sum(update * update)
            if step == 0:
                own[:, columns] = update
            else:
                near = rows - fars[step - 1].shape[0]
                fars[step - 1][:, columns] = update[near:].astype(HALF)
        if step:
            start = lax.rem(me[0] + step, count) * rows
            lines = pl.ds(pl.multiple_of(start, ROWS), rests[step - 1].shape[0])
            stack(rests[step - 1], backs, lines)
    squares[...] = jnp.full(squares.shape, total, FULL)


def scale_of(squares, size):
    return lax.rsqrt(squares * (1.0 / size) + 1e-06)


def final_kernel(count, size, momentum, squares, own, right_last, *refs):
    peers = count - 1
    others, nears, fars, rests = (refs[at * peers : (at + 1) * peers] for at in range(4))
    out, scratch, sems = refs[-3:]
    near = nears[0].shape[0]
    scales = [scale_of(value[0:1, 0:1], size) * (1.0 / count) for value in (squares, *others)]
    copies = []
    for part, here in enumerate((slice(0, near), slice(near, scratch.shape[0]))):
        total = own[here, :] * scales[0]
        for step in range(peers):
            if part:
                update = fars[step][...].astype(FULL)
            else:
                rest = dot(rests[step][...], right_last[...], ((1,), (1,)))
                update = nears[step][...].astype(FULL) - rest
            total += update * scales[step + 1]
        scratch[here, :] = 0.9 * momentum[here, :] + total
        copies.append(
            pltpu.make_async_copy(scratch.at[here, :], out.at[here, :], sems.at[part])
        )
        copies[-1].start()
    for copy in copies:
        copy.wait()


def call(kernel, outs, operands, flops, unread=(), **options):
    moved = sum(value.size * value.dtype.itemsize for value in (*operands, *outs))
    vmem = pl.BlockSpec(memory_space=pltpu.VMEM)
    specs = [pl.BlockSpec(memory_space=pltpu.SMEM)] + [vmem] * (len(operands) - 1)
    specs += [pl.BlockSpec(memory_space=pl.ANY)] * len(unread)
    settings = dict(in_specs=specs, out_specs=[vmem] * len(outs))
    settings.update(options)
    return pl.pallas_call(
        kernel,
        out_shape=outs,
        compiler_params=pltpu.CompilerParams(vmem_limit_bytes=16 * 1024 * 1024),
        cost_estimate=pl.CostEstimate(flops=flops, bytes_accessed=moved // 64, transcendentals=0),
        **settings,
    )(*operands, *unread)


def body(gradients, inverse_out, inverse_in, cross_out, cross_in, momentum):
    own_block = gradients[0, 0]
    tall, wide = own_block.shape
    count = lax.axis_size("rep")
    me = lax.axis_index("rep").astype(jnp.int32).reshape(1)
    widths = [share * wide // sum(SHARES) for share in SHARES]
    rows = momentum.shape[1]
    shape = jax.ShapeDtypeStruct
    part = functools.partial

    anywhere = pl.BlockSpec(memory_space=pl.ANY)
    out_rows, out_wide = cross_out.shape[1:]
    pair, *cuts = call(
        part(cut_kernel, widths),
        [shape((2 * out_rows, out_wide), HALF)]
        + [shape((inverse_in.shape[1], width), HALF) for width in widths],
        [me, cross_out[0], inverse_out[0], inverse_in[0]],
        0,
        in_specs=[pl.BlockSpec(memory_space=pltpu.SMEM)] + [anywhere] * 3,
        scratch_shapes=[pltpu.SemaphoreType.DMA((2 + len(widths),))],
    )
    pairs = from_peers(pair, "rep")
    in_blocks = [cross_in[0], *from_peers(cross_in[0], "rep")]
    following = passed_along(own_block, "layer", -1)

    cut_peers = [from_peers(piece, "rep") for piece in cuts]
    (first,) = call(
        part(first_kernel, count),
        [shape((tall, wide), HALF)],
        [me, following, cross_out[0], *pairs],
        tall * tall * wide // 32,
    )
    previous_blocks = [passed_along(block, "layer", 1) for block in in_blocks]
    (left,) = call(
        part(left_kernel, count),
        [shape((tall, wide), HALF)],
        [me, own_block, first, inverse_out[0], *in_blocks, *pairs],
        tall * wide * (tall + wide) // 32,
        unread=previous_blocks[:1],
    )
    preconds, backs = [], []
    for at, (piece, peers) in enumerate(zip(cuts, cut_peers)):
        weight = 256 if at == len(cuts) - 1 else 1
        precond, back = call(
            part(chunk_kernel, count),
            [shape((tall, piece.shape[1]), HALF)] * 2,
            [me, left, cross_out[0], piece, *peers, *pairs],
            weight * tall * piece.shape[1] * (tall + wide) // 32,
        )
        preconds.append(precond)
        backs.append(passed_along(back, "layer", 1))
    near = 3 * rows // 4 // ROWS * ROWS
    peers, last, later = count - 1, widths[-1], sum(widths[EARLY:])
    *nears, right_last = call(
        part(early_kernel, count, rows),
        [shape((near, wide), HALF)] * peers + [shape((wide, later), HALF)],
        [me, *preconds, *backs[:EARLY], *previous_blocks],
        2 * peers * near * wide * (wide - later),
        scratch_shapes=[pltpu.VMEM((near, wide), HALF), pltpu.VMEM((near, wide - later), HALF)],
    )
    nears = [to_peer(value, "rep", at + 1) for at, value in enumerate(nears)]
    (partial,) = call(
        part(gather_kernel, count),
        [shape((tall, wide), FULL)],
        [me, *preconds, *backs[:-1], *previous_blocks],
        2 * tall * wide * (wide - last),
        scratch_shapes=[pltpu.VMEM((tall, wide), HALF), pltpu.VMEM((tall, wide - last), HALF)],
    )
    squares, own, *sends = call(
        part(update_kernel, count),
        [shape((8, 128), FULL), shape((rows, wide), FULL)]
        + [shape((rows - near, wide), HALF)] * peers
        + [shape((near, later), HALF)] * peers,
        [me, partial, right_last, *backs[EARLY:]],
        2 * tall * wide * last,
    )
    sends = [to_peer(value, "rep", at % peers + 1) for at, value in enumerate(sends)]
    others = [to_peer(squares, "rep", step) for step in range(1, count)]
    operands = [momentum[0], squares, own, right_last, *others, *nears, *sends]
    (result,) = call(
        part(final_kernel, count, tall * wide),
        [shape((rows, wide), FULL)],
        operands,
        4 * rows * wide,
        in_specs=[pl.BlockSpec(memory_space=pltpu.VMEM)] * len(operands),
        out_specs=[anywhere],
        scratch_shapes=[pltpu.VMEM((rows, wide), FULL), pltpu.SemaphoreType.DMA((2,))],
    )
    return result[None]


def solution(mesh):
    in_specs = (
        P("rep", "layer", None, None),
        P("layer", "rep", None),
        P("layer", "rep", None),
        P("layer", "rep", None),
        P("layer", "rep", None),
        P("layer", "rep", None),
    )
    out_specs = P("layer", "rep", None)
    return jax.shard_map(body, mesh=mesh, in_specs=in_specs, out_specs=out_specs, check_vma=False)
```

```python
import functools

import jax
import jax.numpy as jnp
from jax import lax
from jax.experimental import pallas as pl
from jax.experimental.pallas import tpu as pltpu
from jax.sharding import PartitionSpec as P

SHARES = (2, 1, 1)
ROWS = 16
TILE = 256
HALF = jnp.bfloat16
FULL = jnp.float32


def passed_along(value, axis, steps):
    count = lax.axis_size(axis)
    initial, last = (max(0, -steps), min(count, count - steps))
    return lax.ppermute(value, axis, [(source, source + steps) for source in range(initial, last)])


def passed_round(value, axis):
    count = lax.axis_size(axis)
    return lax.ppermute(value, axis, [(source, (source + 1) % count) for source in range(count)])


def from_peers(value, axis):
    count = lax.axis_size(axis)
    return [
        lax.ppermute(value, axis, [(source, (source - step) % count) for source in range(count)])
        for step in range(1, count)
    ]


def to_peer(value, axis, step):
    count = lax.axis_size(axis)
    return lax.ppermute(
        value, axis, [(source, (source + step) % count) for source in range(count)]
    )


def dot(left, right, contract=((1,), (0,))):
    return lax.dot_general(left, right, (contract, ((), ())), preferred_element_type=FULL)


def span(me_ref, step, count, size):
    start = lax.rem(me_ref[0] + step, count) * size
    return pl.ds(pl.multiple_of(start, size), size)


def cut_kernel(widths, me, cross_out, inverse_out, inverse_in, pair, *refs):
    pieces, sems = refs[:-1], refs[-1]
    rows, start = cross_out.shape[0], 0
    copies = [
        pltpu.make_async_copy(cross_out, pair.at[:rows], sems.at[0]),
        pltpu.make_async_copy(inverse_out, pair.at[rows:], sems.at[1]),
    ]
    for at, width in enumerate(widths):
        source = inverse_in.at[:, start : start + width]
        copies.append(pltpu.make_async_copy(source, pieces[at], sems.at[2 + at]))
        start += width
    for copy in copies:
        copy.start()
    for copy in copies:
        copy.wait()


def first_kernel(count, me, following, own, *refs):
    others, out = refs[: count - 1], refs[-1]
    rows = own.shape[0]

    @pl.loop(0, out.shape[1] // TILE)
    def _(at):
        columns = pl.ds(pl.multiple_of(at * TILE, TILE), TILE)
        right = following[:, columns]
        out[span(me, 0, count, rows), columns] = dot(own[...], right).astype(HALF)
        for step in range(1, count):
            block = others[step - 1][:rows, :]
            out[span(me, step, count, rows), columns] = dot(block, right).astype(HALF)


def left_kernel(count, me, grads, first, inv_own, *refs):
    rights, others, out = refs[:count], refs[count : 2 * count - 1], refs[2 * count - 1]
    depth, rows = rights[0].shape[0], inv_own.shape[0]

    @pl.loop(0, out.shape[1] // TILE)
    def _(at):
        columns = pl.ds(pl.multiple_of(at * TILE, TILE), TILE)
        cross = sum(
            dot(first[:, span(me, step, count, depth)], rights[step][:, columns])
            for step in range(count)
        )
        residual = (grads[:, columns].astype(FULL) - cross).astype(HALF)
        out[span(me, 0, count, rows), columns] = dot(inv_own[...], residual).astype(HALF)
        for step in range(1, count):
            block = others[step - 1][rows:, :]
            out[span(me, step, count, rows), columns] = dot(block, residual).astype(HALF)


def chunk_kernel(count, me, left, cross_own, own_piece, *refs):
    pieces, others = refs[: count - 1], refs[count - 1 : 2 * count - 2]
    precond, back = refs[-2:]
    depth, rows = own_piece.shape[0], cross_own.shape[0]
    product = dot(left[:, span(me, 0, count, depth)], own_piece[...])
    for step in range(1, count):
        product += dot(left[:, span(me, step, count, depth)], pieces[step - 1][...])
    precond[...] = product.astype(HALF)
    turned = ((0,), (0,))
    result = dot(cross_own[...], precond[span(me, 0, count, rows), :], turned)
    for step in range(1, count):
        block = others[step - 1][:rows, :]
        result += dot(block, precond[span(me, step, count, rows), :], turned)
    back[...] = result.astype(HALF)


def stack(target, values, lines=slice(None)):
    start = 0
    for value in values:
        target[:, start : start + value.shape[1]] = value[lines, :]
        start += value.shape[1]


def early_kernel(count, rows, me, *refs):
    total = len(SHARES)
    preconds, backs = refs[:total], refs[total : 2 * total - 1]
    rights = refs[2 * total - 1 : 2 * total - 1 + count]
    nears, (right_last, staged, stacked) = refs[2 * total - 1 + count : -3], refs[-3:]
    depth, known, near = rights[0].shape[0], stacked.shape[1], staged.shape[0]
    for row_step in range(1, count):
        start = lax.rem(me[0] + row_step, count) * rows
        lines = pl.ds(pl.multiple_of(start, ROWS), near)
        stack(staged, preconds, lines)
        stack(stacked, backs, lines)
        for step in range(count):
            columns = span(me, step, count, depth)
            product = dot(stacked[...], rights[step][:, :known], ((1,), (1,)))
            update = staged[:, columns].astype(FULL) - product
            nears[row_step - 1][:, columns] = update.astype(HALF)
    for step in range(count):
        right_last[span(me, step, count, depth), :] = rights[step][:, known:]


def gather_kernel(count, me, *refs):
    total = len(SHARES)
    preconds, backs = refs[:total], refs[total : 2 * total - 1]
    rights = refs[2 * total - 1 : 2 * total - 1 + count]
    partial, staged, stacked = refs[2 * total - 1 + count :]
    depth, known = rights[0].shape[0], stacked.shape[1]
    stack(staged, preconds)
    stack(stacked, backs)
    for step in range(count):
        columns = span(me, step, count, depth)
        right = rights[step][:, :known]
        for row in range(0, staged.shape[0], TILE):
            here = slice(row, row + TILE)
            product = dot(stacked[here, :], right, ((1,), (1,)))
            partial[here, columns] = staged[here, columns].astype(FULL) - product


def update_kernel(count, me, partial, back, right_last, *refs):
    squares, own = refs[:2]
    fars, rests = refs[2 : count + 1], refs[count + 1 :]
    rows, wide = own.shape
    total = jnp.zeros((), FULL)
    for step in range(count):
        here = span(me, step, count, rows)
        for start in range(0, wide, TILE):
            columns = slice(start, start + TILE)
            update = partial[here, columns] - dot(
                back[here, :], right_last[columns, :], ((1,), (1,))
            )
            total += jnp.sum(update * update)
            if step == 0:
                own[:, columns] = update
            else:
                near = rows - fars[step - 1].shape[0]
                fars[step - 1][:, columns] = update[near:].astype(HALF)
        if step:
            start = lax.rem(me[0] + step, count) * rows
            lines = pl.ds(pl.multiple_of(start, ROWS), rests[step - 1].shape[0])
            rests[step - 1][...] = back[lines, :]
    squares[...] = jnp.full(squares.shape, total, FULL)


def scale_of(squares, size):
    return lax.rsqrt(squares * (1.0 / size) + 1e-06)


def final_kernel(count, size, momentum, squares, own, right_last, *refs):
    peers = count - 1
    others, nears, fars, rests = (refs[at * peers : (at + 1) * peers] for at in range(4))
    out, scratch, sems = refs[-3:]
    near = nears[0].shape[0]
    scales = [scale_of(value[0:1, 0:1], size) * (1.0 / count) for value in (squares, *others)]
    copies = []
    for part, here in enumerate((slice(0, near), slice(near, scratch.shape[0]))):
        total = own[here, :] * scales[0]
        for step in range(peers):
            if part:
                update = fars[step][...].astype(FULL)
            else:
                rest = dot(rests[step][...], right_last[...], ((1,), (1,)))
                update = nears[step][...].astype(FULL) - rest
            total += update * scales[step + 1]
        scratch[here, :] = 0.9 * momentum[here, :] + total
        copies.append(
            pltpu.make_async_copy(scratch.at[here, :], out.at[here, :], sems.at[part])
        )
        copies[-1].start()
    for copy in copies:
        copy.wait()


def call(kernel, outs, operands, flops, **options):
    moved = sum(value.size * value.dtype.itemsize for value in (*operands, *outs))
    vmem = pl.BlockSpec(memory_space=pltpu.VMEM)
    specs = [pl.BlockSpec(memory_space=pltpu.SMEM)] + [vmem] * (len(operands) - 1)
    settings = dict(in_specs=specs, out_specs=[vmem] * len(outs))
    settings.update(options)
    return pl.pallas_call(
        kernel,
        out_shape=outs,
        compiler_params=pltpu.CompilerParams(vmem_limit_bytes=16 * 1024 * 1024),
        cost_estimate=pl.CostEstimate(flops=flops, bytes_accessed=moved // 64, transcendentals=0),
        **settings,
    )(*operands)


def body(gradients, inverse_out, inverse_in, cross_out, cross_in, momentum):
    own_block = gradients[0, 0]
    tall, wide = own_block.shape
    count = lax.axis_size("rep")
    me = lax.axis_index("rep").astype(jnp.int32).reshape(1)
    widths = [share * wide // sum(SHARES) for share in SHARES]
    rows = momentum.shape[1]
    shape = jax.ShapeDtypeStruct
    part = functools.partial

    anywhere = pl.BlockSpec(memory_space=pl.ANY)
    out_rows, out_wide = cross_out.shape[1:]
    pair, *cuts = call(
        part(cut_kernel, widths),
        [shape((2 * out_rows, out_wide), HALF)]
        + [shape((inverse_in.shape[1], width), HALF) for width in widths],
        [me, cross_out[0], inverse_out[0], inverse_in[0]],
        0,
        in_specs=[pl.BlockSpec(memory_space=pltpu.SMEM)] + [anywhere] * 3,
        scratch_shapes=[pltpu.SemaphoreType.DMA((2 + len(widths),))],
    )
    pairs = from_peers(pair, "rep")
    in_blocks = [cross_in[0], *from_peers(cross_in[0], "rep")]
    following = passed_along(own_block, "layer", -1)

    cut_peers = [from_peers(piece, "rep") for piece in cuts]
    (first,) = call(
        part(first_kernel, count),
        [shape((tall, wide), HALF)],
        [me, following, cross_out[0], *pairs],
        tall * tall * wide // 32,
    )
    previous_blocks = [passed_along(block, "layer", 1) for block in in_blocks]
    (left,) = call(
        part(left_kernel, count),
        [shape((tall, wide), HALF)],
        [me, own_block, first, inverse_out[0], *in_blocks, *pairs],
        tall * wide * (tall + wide) // 32,
    )
    preconds, backs = [], []
    for at, (piece, peers) in enumerate(zip(cuts, cut_peers)):
        weight = 256 if at == len(cuts) - 1 else 1
        precond, back = call(
            part(chunk_kernel, count),
            [shape((tall, piece.shape[1]), HALF)] * 2,
            [me, left, cross_out[0], piece, *peers, *pairs],
            weight * tall * piece.shape[1] * (tall + wide) // 32,
        )
        preconds.append(precond)
        backs.append(passed_round(back, "layer"))
    near = 5 * rows // 8 // ROWS * ROWS
    peers, last = count - 1, widths[-1]
    *nears, right_last = call(
        part(early_kernel, count, rows),
        [shape((near, wide), HALF)] * peers + [shape((wide, last), HALF)],
        [me, *preconds, *backs[:-1], *previous_blocks],
        2 * peers * near * wide * (wide - last),
        scratch_shapes=[pltpu.VMEM((near, wide), HALF), pltpu.VMEM((near, wide - last), HALF)],
    )
    nears = [to_peer(value, "rep", at + 1) for at, value in enumerate(nears)]
    (partial,) = call(
        part(gather_kernel, count),
        [shape((tall, wide), FULL)],
        [me, *preconds, *backs[:-1], *previous_blocks],
        2 * tall * wide * (wide - last),
        scratch_shapes=[pltpu.VMEM((tall, wide), HALF), pltpu.VMEM((tall, wide - last), HALF)],
    )
    squares, own, *sends = call(
        part(update_kernel, count),
        [shape((8, 128), FULL), shape((rows, wide), FULL)]
        + [shape((rows - near, wide), HALF)] * peers
        + [shape((near, last), HALF)] * peers,
        [me, partial, backs[-1], right_last],
        2 * tall * wide * last,
    )
    sends = [to_peer(value, "rep", at % peers + 1) for at, value in enumerate(sends)]
    others = [to_peer(squares, "rep", step) for step in range(1, count)]
    operands = [momentum[0], squares, own, right_last, *others, *nears, *sends]
    (result,) = call(
        part(final_kernel, count, tall * wide),
        [shape((rows, wide), FULL)],
        operands,
        4 * rows * wide,
        in_specs=[pl.BlockSpec(memory_space=pltpu.VMEM)] * len(operands),
        out_specs=[anywhere],
        scratch_shapes=[pltpu.VMEM((rows, wide), FULL), pltpu.SemaphoreType.DMA((2,))],
    )
    return result[None]


def solution(mesh):
    in_specs = (
        P("rep", "layer", None, None),
        P("layer", "rep", None),
        P("layer", "rep", None),
        P("layer", "rep", None),
        P("layer", "rep", None),
        P("layer", "rep", None),
    )
    out_specs = P("layer", "rep", None)
    return jax.shard_map(body, mesh=mesh, in_specs=in_specs, out_specs=out_specs, check_vma=False)
```

```python
import functools

import jax
import jax.numpy as jnp
from jax import lax
from jax.experimental import pallas as pl
from jax.experimental.pallas import tpu as pltpu
from jax.sharding import PartitionSpec as P

SHARES = (2, 1, 1)
ROWS = 16
TILE = 256
HALF = jnp.bfloat16
FULL = jnp.float32


def passed_along(value, axis, steps):
    count = lax.axis_size(axis)
    initial, last = (max(0, -steps), min(count, count - steps))
    return lax.ppermute(value, axis, [(source, source + steps) for source in range(initial, last)])


def passed_round(value, axis):
    count = lax.axis_size(axis)
    return lax.ppermute(value, axis, [(source, (source + 1) % count) for source in range(count)])


def from_peers(value, axis):
    count = lax.axis_size(axis)
    return [
        lax.ppermute(value, axis, [(source, (source - step) % count) for source in range(count)])
        for step in range(1, count)
    ]


def to_peer(value, axis, step):
    count = lax.axis_size(axis)
    return lax.ppermute(
        value, axis, [(source, (source + step) % count) for source in range(count)]
    )


def dot(left, right, contract=((1,), (0,))):
    return lax.dot_general(left, right, (contract, ((), ())), preferred_element_type=FULL)


def span(me_ref, step, count, size):
    start = lax.rem(me_ref[0] + step, count) * size
    return pl.ds(pl.multiple_of(start, size), size)


def cut_kernel(widths, me, cross_out, inverse_out, inverse_in, pair, *refs):
    pieces, sems = refs[:-1], refs[-1]
    rows, start = cross_out.shape[0], 0
    copies = [
        pltpu.make_async_copy(cross_out, pair.at[:rows], sems.at[0]),
        pltpu.make_async_copy(inverse_out, pair.at[rows:], sems.at[1]),
    ]
    for at, width in enumerate(widths):
        source = inverse_in.at[:, start : start + width]
        copies.append(pltpu.make_async_copy(source, pieces[at], sems.at[2 + at]))
        start += width
    for copy in copies:
        copy.start()
    for copy in copies:
        copy.wait()


def first_kernel(count, me, following, own, *refs):
    others, out = refs[: count - 1], refs[-1]
    rows = own.shape[0]

    @pl.loop(0, out.shape[1] // TILE)
    def _(at):
        columns = pl.ds(pl.multiple_of(at * TILE, TILE), TILE)
        right = following[:, columns]
        out[span(me, 0, count, rows), columns] = dot(own[...], right).astype(HALF)
        for step in range(1, count):
            block = others[step - 1][:rows, :]
            out[span(me, step, count, rows), columns] = dot(block, right).astype(HALF)


def left_kernel(count, me, grads, first, inv_own, *refs):
    rights, others, out = refs[:count], refs[count : 2 * count - 1], refs[2 * count - 1]
    depth, rows = rights[0].shape[0], inv_own.shape[0]

    @pl.loop(0, out.shape[1] // TILE)
    def _(at):
        columns = pl.ds(pl.multiple_of(at * TILE, TILE), TILE)
        cross = sum(
            dot(first[:, span(me, step, count, depth)], rights[step][:, columns])
            for step in range(count)
        )
        residual = (grads[:, columns].astype(FULL) - cross).astype(HALF)
        out[span(me, 0, count, rows), columns] = dot(inv_own[...], residual).astype(HALF)
        for step in range(1, count):
            block = others[step - 1][rows:, :]
            out[span(me, step, count, rows), columns] = dot(block, residual).astype(HALF)


def chunk_kernel(count, me, left, cross_own, own_piece, *refs):
    pieces, others = refs[: count - 1], refs[count - 1 : 2 * count - 2]
    precond, back = refs[-2:]
    depth, rows = own_piece.shape[0], cross_own.shape[0]
    product = dot(left[:, span(me, 0, count, depth)], own_piece[...])
    for step in range(1, count):
        product += dot(left[:, span(me, step, count, depth)], pieces[step - 1][...])
    precond[...] = product.astype(HALF)
    turned = ((0,), (0,))
    result = dot(cross_own[...], precond[span(me, 0, count, rows), :], turned)
    for step in range(1, count):
        block = others[step - 1][:rows, :]
        result += dot(block, precond[span(me, step, count, rows), :], turned)
    back[...] = result.astype(HALF)


def stack(target, values, lines=slice(None)):
    start = 0
    for value in values:
        target[:, start : start + value.shape[1]] = value[lines, :]
        start += value.shape[1]


def early_kernel(count, rows, me, *refs):
    total = len(SHARES)
    preconds, backs = refs[:total], refs[total : 2 * total - 1]
    rights = refs[2 * total - 1 : 2 * total - 1 + count]
    nears, (right_last, staged, stacked) = refs[2 * total - 1 + count : -3], refs[-3:]
    depth, known, near = rights[0].shape[0], stacked.shape[1], staged.shape[0]
    for row_step in range(1, count):
        start = lax.rem(me[0] + row_step, count) * rows
        lines = pl.ds(pl.multiple_of(start, ROWS), near)
        stack(staged, preconds, lines)
        stack(stacked, backs, lines)
        for step in range(count):
            columns = span(me, step, count, depth)
            product = dot(stacked[...], rights[step][:, :known], ((1,), (1,)))
            update = staged[:, columns].astype(FULL) - product
            nears[row_step - 1][:, columns] = update.astype(HALF)
    for step in range(count):
        right_last[span(me, step, count, depth), :] = rights[step][:, known:]


def gather_kernel(count, me, *refs):
    total = len(SHARES)
    preconds, backs = refs[:total], refs[total : 2 * total - 1]
    rights = refs[2 * total - 1 : 2 * total - 1 + count]
    partial, staged, stacked = refs[2 * total - 1 + count :]
    depth, known = rights[0].shape[0], stacked.shape[1]
    stack(staged, preconds)
    stack(stacked, backs)
    for step in range(count):
        columns = span(me, step, count, depth)
        right = rights[step][:, :known]
        for row in range(0, staged.shape[0], TILE):
            here = slice(row, row + TILE)
            product = dot(stacked[here, :], right, ((1,), (1,)))
            partial[here, columns] = staged[here, columns].astype(FULL) - product


def update_kernel(count, me, partial, back, right_last, *refs):
    squares, own = refs[:2]
    fars, rests = refs[2 : count + 1], refs[count + 1 :]
    rows, wide = own.shape
    total = jnp.zeros((), FULL)
    for step in range(count):
        here = span(me, step, count, rows)
        for start in range(0, wide, TILE):
            columns = slice(start, start + TILE)
            update = partial[here, columns] - dot(
                back[here, :], right_last[columns, :], ((1,), (1,))
            )
            total += jnp.sum(update * update)
            if step == 0:
                own[:, columns] = update
            else:
                near = rows - fars[step - 1].shape[0]
                fars[step - 1][:, columns] = update[near:].astype(HALF)
        if step:
            start = lax.rem(me[0] + step, count) * rows
            lines = pl.ds(pl.multiple_of(start, ROWS), rests[step - 1].shape[0])
            rests[step - 1][...] = back[lines, :]
    squares[...] = jnp.full(squares.shape, total, FULL)


def scale_of(squares, size):
    return lax.rsqrt(squares * (1.0 / size) + 1e-06)


def final_kernel(count, size, momentum, squares, own, right_last, *refs):
    peers = count - 1
    others, nears, fars, rests = (refs[at * peers : (at + 1) * peers] for at in range(4))
    out, scratch, sems = refs[-3:]
    near = nears[0].shape[0]
    scales = [scale_of(value[0:1, 0:1], size) * (1.0 / count) for value in (squares, *others)]
    copies = []
    for part, here in enumerate((slice(0, near), slice(near, scratch.shape[0]))):
        total = own[here, :] * scales[0]
        for step in range(peers):
            if part:
                update = fars[step][...].astype(FULL)
            else:
                rest = dot(rests[step][...], right_last[...], ((1,), (1,)))
                update = nears[step][...].astype(FULL) - rest
            total += update * scales[step + 1]
        scratch[here, :] = 0.9 * momentum[here, :] + total
        copies.append(
            pltpu.make_async_copy(scratch.at[here, :], out.at[here, :], sems.at[part])
        )
        copies[-1].start()
    for copy in copies:
        copy.wait()


def call(kernel, outs, operands, flops, **options):
    moved = sum(value.size * value.dtype.itemsize for value in (*operands, *outs))
    vmem = pl.BlockSpec(memory_space=pltpu.VMEM)
    specs = [pl.BlockSpec(memory_space=pltpu.SMEM)] + [vmem] * (len(operands) - 1)
    settings = dict(in_specs=specs, out_specs=[vmem] * len(outs))
    settings.update(options)
    return pl.pallas_call(
        kernel,
        out_shape=outs,
        compiler_params=pltpu.CompilerParams(vmem_limit_bytes=16 * 1024 * 1024),
        cost_estimate=pl.CostEstimate(flops=flops, bytes_accessed=moved // 64, transcendentals=0),
        **settings,
    )(*operands)


def body(gradients, inverse_out, inverse_in, cross_out, cross_in, momentum):
    own_block = gradients[0, 0]
    tall, wide = own_block.shape
    count = lax.axis_size("rep")
    me = lax.axis_index("rep").astype(jnp.int32).reshape(1)
    widths = [share * wide // sum(SHARES) for share in SHARES]
    rows = momentum.shape[1]
    shape = jax.ShapeDtypeStruct
    part = functools.partial

    anywhere = pl.BlockSpec(memory_space=pl.ANY)
    out_rows, out_wide = cross_out.shape[1:]
    pair, *cuts = call(
        part(cut_kernel, widths),
        [shape((2 * out_rows, out_wide), HALF)]
        + [shape((inverse_in.shape[1], width), HALF) for width in widths],
        [me, cross_out[0], inverse_out[0], inverse_in[0]],
        0,
        in_specs=[pl.BlockSpec(memory_space=pltpu.SMEM)] + [anywhere] * 3,
        scratch_shapes=[pltpu.SemaphoreType.DMA((2 + len(widths),))],
    )
    pairs = from_peers(pair, "rep")
    in_blocks = [cross_in[0], *from_peers(cross_in[0], "rep")]
    following = passed_along(own_block, "layer", -1)

    cut_peers = [from_peers(piece, "rep") for piece in cuts]
    (first,) = call(
        part(first_kernel, count),
        [shape((tall, wide), HALF)],
        [me, following, cross_out[0], *pairs],
        tall * tall * wide // 32,
    )
    previous_blocks = [passed_along(block, "layer", 1) for block in in_blocks]
    (left,) = call(
        part(left_kernel, count),
        [shape((tall, wide), HALF)],
        [me, own_block, first, inverse_out[0], *in_blocks, *pairs],
        tall * wide * (tall + wide) // 32,
    )
    preconds, backs = [], []
    for at, (piece, peers) in enumerate(zip(cuts, cut_peers)):
        weight = 256 if at == len(cuts) - 1 else 1
        precond, back = call(
            part(chunk_kernel, count),
            [shape((tall, piece.shape[1]), HALF)] * 2,
            [me, left, cross_out[0], piece, *peers, *pairs],
            weight * tall * piece.shape[1] * (tall + wide) // 32,
        )
        preconds.append(precond)
        backs.append(passed_round(back, "layer") if at < 2 else passed_along(back, "layer", 1))
    near = 9 * rows // 16 // ROWS * ROWS
    peers, last = count - 1, widths[-1]
    *nears, right_last = call(
        part(early_kernel, count, rows),
        [shape((near, wide), HALF)] * peers + [shape((wide, last), HALF)],
        [me, *preconds, *backs[:-1], *previous_blocks],
        2 * peers * near * wide * (wide - last),
        scratch_shapes=[pltpu.VMEM((near, wide), HALF), pltpu.VMEM((near, wide - last), HALF)],
    )
    nears = [to_peer(value, "rep", at + 1) for at, value in enumerate(nears)]
    (partial,) = call(
        part(gather_kernel, count),
        [shape((tall, wide), FULL)],
        [me, *preconds, *backs[:-1], *previous_blocks],
        2 * tall * wide * (wide - last),
        scratch_shapes=[pltpu.VMEM((tall, wide), HALF), pltpu.VMEM((tall, wide - last), HALF)],
    )
    squares, own, *sends = call(
        part(update_kernel, count),
        [shape((8, 128), FULL), shape((rows, wide), FULL)]
        + [shape((rows - near, wide), HALF)] * peers
        + [shape((near, last), HALF)] * peers,
        [me, partial, backs[-1], right_last],
        2 * tall * wide * last,
    )
    sends = [to_peer(value, "rep", at % peers + 1) for at, value in enumerate(sends)]
    others = [to_peer(squares, "rep", step) for step in range(1, count)]
    operands = [momentum[0], squares, own, right_last, *others, *nears, *sends]
    (result,) = call(
        part(final_kernel, count, tall * wide),
        [shape((rows, wide), FULL)],
        operands,
        4 * rows * wide,
        in_specs=[pl.BlockSpec(memory_space=pltpu.VMEM)] * len(operands),
        out_specs=[anywhere],
        scratch_shapes=[pltpu.VMEM((rows, wide), FULL), pltpu.SemaphoreType.DMA((2,))],
    )
    return result[None]


def solution(mesh):
    in_specs = (
        P("rep", "layer", None, None),
        P("layer", "rep", None),
        P("layer", "rep", None),
        P("layer", "rep", None),
        P("layer", "rep", None),
        P("layer", "rep", None),
    )
    out_specs = P("layer", "rep", None)
    return jax.shard_map(body, mesh=mesh, in_specs=in_specs, out_specs=out_specs, check_vma=False)
```

```python
import functools

import jax
import jax.numpy as jnp
from jax import lax
from jax.experimental import pallas as pl
from jax.experimental.pallas import tpu as pltpu
from jax.sharding import PartitionSpec as P

SHARES = (2, 1, 1)
ROWS = 16
TILE = 256
HALF = jnp.bfloat16
FULL = jnp.float32


def passed_along(value, axis, steps):
    count = lax.axis_size(axis)
    initial, last = (max(0, -steps), min(count, count - steps))
    return lax.ppermute(value, axis, [(source, source + steps) for source in range(initial, last)])


def passed_round(value, axis):
    count = lax.axis_size(axis)
    return lax.ppermute(value, axis, [(source, (source + 1) % count) for source in range(count)])


def from_peers(value, axis):
    count = lax.axis_size(axis)
    return [
        lax.ppermute(value, axis, [(source, (source - step) % count) for source in range(count)])
        for step in range(1, count)
    ]


def to_peer(value, axis, step):
    count = lax.axis_size(axis)
    return lax.ppermute(
        value, axis, [(source, (source + step) % count) for source in range(count)]
    )


def dot(left, right, contract=((1,), (0,))):
    return lax.dot_general(left, right, (contract, ((), ())), preferred_element_type=FULL)


def span(me_ref, step, count, size):
    start = lax.rem(me_ref[0] + step, count) * size
    return pl.ds(pl.multiple_of(start, size), size)


def cut_kernel(widths, me, cross_out, inverse_out, inverse_in, pair, *refs):
    pieces, sems = refs[:-1], refs[-1]
    rows, start = cross_out.shape[0], 0
    copies = [
        pltpu.make_async_copy(cross_out, pair.at[:rows], sems.at[0]),
        pltpu.make_async_copy(inverse_out, pair.at[rows:], sems.at[1]),
    ]
    for at, width in enumerate(widths):
        source = inverse_in.at[:, start : start + width]
        copies.append(pltpu.make_async_copy(source, pieces[at], sems.at[2 + at]))
        start += width
    for copy in copies:
        copy.start()
    for copy in copies:
        copy.wait()


def first_kernel(count, me, following, own, *refs):
    others, out = refs[: count - 1], refs[-1]
    rows = own.shape[0]

    @pl.loop(0, out.shape[1] // TILE)
    def _(at):
        columns = pl.ds(pl.multiple_of(at * TILE, TILE), TILE)
        right = following[:, columns]
        out[span(me, 0, count, rows), columns] = dot(own[...], right).astype(HALF)
        for step in range(1, count):
            block = others[step - 1][:rows, :]
            out[span(me, step, count, rows), columns] = dot(block, right).astype(HALF)


def left_kernel(count, me, grads, first, inv_own, *refs):
    rights, others, out = refs[:count], refs[count : 2 * count - 1], refs[2 * count - 1]
    depth, rows = rights[0].shape[0], inv_own.shape[0]

    @pl.loop(0, out.shape[1] // TILE)
    def _(at):
        columns = pl.ds(pl.multiple_of(at * TILE, TILE), TILE)
        cross = sum(
            dot(first[:, span(me, step, count, depth)], rights[step][:, columns])
            for step in range(count)
        )
        residual = (grads[:, columns].astype(FULL) - cross).astype(HALF)
        out[span(me, 0, count, rows), columns] = dot(inv_own[...], residual).astype(HALF)
        for step in range(1, count):
            block = others[step - 1][rows:, :]
            out[span(me, step, count, rows), columns] = dot(block, residual).astype(HALF)


def mine_kernel(count, me, left, inv_own, out):
    @pl.loop(0, out.shape[1] // TILE)
    def _(at):
        columns = pl.ds(pl.multiple_of(at * TILE, TILE), TILE)
        out[:, columns] = dot(left[:, span(me, 0, count, inv_own.shape[0])], inv_own[:, columns])


def chunk_kernel(count, start, me, left, mine, cross_own, *refs):
    pieces, others = refs[: count - 1], refs[count - 1 : 2 * count - 2]
    precond, back = refs[2 * count - 2 :]
    depth, rows = pieces[0].shape[0], cross_own.shape[0]
    product = mine[:, start : start + precond.shape[1]]
    for step in range(1, count):
        product += dot(left[:, span(me, step, count, depth)], pieces[step - 1][...])
    precond[...] = product.astype(HALF)
    turned = ((0,), (0,))
    result = dot(cross_own[...], precond[span(me, 0, count, rows), :], turned)
    for step in range(1, count):
        block = others[step - 1][:rows, :]
        result += dot(block, precond[span(me, step, count, rows), :], turned)
    back[...] = result.astype(HALF)


def stack(target, values, lines=slice(None)):
    start = 0
    for value in values:
        target[:, start : start + value.shape[1]] = value[lines, :]
        start += value.shape[1]


def early_kernel(count, rows, me, *refs):
    total = len(SHARES)
    preconds, backs = refs[:total], refs[total : 2 * total - 1]
    rights = refs[2 * total - 1 : 2 * total - 1 + count]
    nears, (staged, stacked) = refs[2 * total - 1 + count : -2], refs[-2:]
    depth, known, near = rights[0].shape[0], stacked.shape[1], staged.shape[0]
    for row_step in range(1, count):
        start = lax.rem(me[0] + row_step, count) * rows
        lines = pl.ds(pl.multiple_of(start, ROWS), near)
        stack(staged, preconds, lines)
        stack(stacked, backs, lines)
        for step in range(count):
            columns = span(me, step, count, depth)
            product = dot(stacked[...], rights[step][:, :known], ((1,), (1,)))
            update = staged[:, columns].astype(FULL) - product
            nears[row_step - 1][:, columns] = update.astype(HALF)


def gather_kernel(count, me, *refs):
    total = len(SHARES)
    preconds, backs = refs[:total], refs[total : 2 * total - 1]
    rights = refs[2 * total - 1 : 2 * total - 1 + count]
    partial, right_last, staged, stacked = refs[2 * total - 1 + count :]
    depth, known = rights[0].shape[0], stacked.shape[1]
    stack(staged, preconds)
    stack(stacked, backs)
    for step in range(count):
        columns = span(me, step, count, depth)
        right_last[columns, :] = rights[step][:, known:]
        right = rights[step][:, :known]
        for row in range(0, staged.shape[0], TILE):
            here = slice(row, row + TILE)
            product = dot(stacked[here, :], right, ((1,), (1,)))
            partial[here, columns] = staged[here, columns].astype(FULL) - product


def update_kernel(count, me, partial, back, right_last, *refs):
    squares, own = refs[:2]
    fars, rests = refs[2 : count + 1], refs[count + 1 :]
    rows, wide = own.shape
    total = jnp.zeros((), FULL)
    for step in range(count):
        here = span(me, step, count, rows)
        for start in range(0, wide, TILE):
            columns = slice(start, start + TILE)
            update = partial[here, columns] - dot(
                back[here, :], right_last[columns, :], ((1,), (1,))
            )
            total += jnp.sum(update * update)
            if step == 0:
                own[:, columns] = update
            else:
                near = rows - fars[step - 1].shape[0]
                fars[step - 1][:, columns] = update[near:].astype(HALF)
        if step:
            start = lax.rem(me[0] + step, count) * rows
            lines = pl.ds(pl.multiple_of(start, ROWS), rests[step - 1].shape[0])
            rests[step - 1][...] = back[lines, :]
    squares[...] = jnp.full(squares.shape, total, FULL)


def scale_of(squares, size):
    return lax.rsqrt(squares * (1.0 / size) + 1e-06)


def base_kernel(count, size, momentum, squares, own, out):
    scale = scale_of(squares[0:1, 0:1], size) * (1.0 / count)
    out[...] = 0.9 * momentum[...] + own[...] * scale


def final_kernel(count, size, base, right_last, *refs):
    peers = count - 1
    others, nears, fars, rests = (refs[at * peers : (at + 1) * peers] for at in range(4))
    out, scratch, sems = refs[-3:]
    near, rows = nears[0].shape[0], scratch.shape[0]
    middle = near // 2
    scales = [scale_of(value[0:1, 0:1], size) * (1.0 / count) for value in others]
    copies = []
    for at, here in enumerate((slice(near, rows), slice(0, middle), slice(middle, near))):
        total = base[here, :]
        for step in range(peers):
            if at == 0:
                update = fars[step][...].astype(FULL)
            else:
                rest = dot(rests[step][here, :], right_last[...], ((1,), (1,)))
                update = nears[step][here, :].astype(FULL) - rest
            total += update * scales[step]
        scratch[here, :] = total
        copies.append(pltpu.make_async_copy(scratch.at[here, :], out.at[here, :], sems.at[at]))
        copies[-1].start()
    for copy in copies:
        copy.wait()


def call(kernel, outs, operands, flops, **options):
    moved = sum(value.size * value.dtype.itemsize for value in (*operands, *outs))
    vmem = pl.BlockSpec(memory_space=pltpu.VMEM)
    specs = [pl.BlockSpec(memory_space=pltpu.SMEM)] + [vmem] * (len(operands) - 1)
    settings = dict(in_specs=specs, out_specs=[vmem] * len(outs))
    settings.update(options)
    return pl.pallas_call(
        kernel,
        out_shape=outs,
        compiler_params=pltpu.CompilerParams(vmem_limit_bytes=16 * 1024 * 1024),
        cost_estimate=pl.CostEstimate(flops=flops, bytes_accessed=moved // 64, transcendentals=0),
        **settings,
    )(*operands)


def body(gradients, inverse_out, inverse_in, cross_out, cross_in, momentum):
    own_block = gradients[0, 0]
    tall, wide = own_block.shape
    count = lax.axis_size("rep")
    me = lax.axis_index("rep").astype(jnp.int32).reshape(1)
    widths = [share * wide // sum(SHARES) for share in SHARES]
    rows = momentum.shape[1]
    shape = jax.ShapeDtypeStruct
    part = functools.partial

    anywhere = pl.BlockSpec(memory_space=pl.ANY)
    out_rows, out_wide = cross_out.shape[1:]
    pair, *cuts = call(
        part(cut_kernel, widths),
        [shape((2 * out_rows, out_wide), HALF)]
        + [shape((inverse_in.shape[1], width), HALF) for width in widths],
        [me, cross_out[0], inverse_out[0], inverse_in[0]],
        0,
        in_specs=[pl.BlockSpec(memory_space=pltpu.SMEM)] + [anywhere] * 3,
        scratch_shapes=[pltpu.SemaphoreType.DMA((2 + len(widths),))],
    )
    pairs = from_peers(pair, "rep")
    in_blocks = [cross_in[0], *from_peers(cross_in[0], "rep")]
    following = passed_along(own_block, "layer", -1)

    cut_peers = [from_peers(piece, "rep") for piece in cuts]
    (first,) = call(
        part(first_kernel, count),
        [shape((tall, wide), HALF)],
        [me, following, cross_out[0], *pairs],
        tall * tall * wide // 32,
    )
    previous_blocks = [passed_along(block, "layer", 1) for block in in_blocks]
    (left,) = call(
        part(left_kernel, count),
        [shape((tall, wide), HALF)],
        [me, own_block, first, inverse_out[0], *in_blocks, *pairs],
        tall * wide * (tall + wide) // 32,
    )
    (mine,) = call(
        part(mine_kernel, count),
        [shape((tall, wide), FULL)],
        [me, left, inverse_in[0]],
        tall * wide * wide // 64,
    )
    preconds, backs = [], []
    for at, peers in enumerate(cut_peers):
        precond, back = call(
            part(chunk_kernel, count, sum(widths[:at])),
            [shape((tall, widths[at]), HALF)] * 2,
            [me, left, mine, cross_out[0], *peers, *pairs],
            tall * widths[at] * (tall + wide) // 32,
        )
        preconds.append(precond)
        backs.append(passed_round(back, "layer"))
    near = 9 * rows // 16 // ROWS * ROWS
    peers, last = count - 1, widths[-1]
    nears = call(
        part(early_kernel, count, rows),
        [shape((near, wide), HALF)] * peers,
        [me, *preconds, *backs[:-1], *previous_blocks],
        2 * peers * near * wide * (wide - last),
        scratch_shapes=[pltpu.VMEM((near, wide), HALF), pltpu.VMEM((near, wide - last), HALF)],
    )
    nears = [to_peer(value, "rep", at + 1) for at, value in enumerate(nears)]
    partial, right_last = call(
        part(gather_kernel, count),
        [shape((tall, wide), FULL), shape((wide, last), HALF)],
        [me, *preconds, *backs[:-1], *previous_blocks],
        2 * tall * wide * (wide - last),
        scratch_shapes=[pltpu.VMEM((tall, wide), HALF), pltpu.VMEM((tall, wide - last), HALF)],
    )
    squares, own, *sends = call(
        part(update_kernel, count),
        [shape((8, 128), FULL), shape((rows, wide), FULL)]
        + [shape((rows - near, wide), HALF)] * peers
        + [shape((near, last), HALF)] * peers,
        [me, partial, backs[-1], right_last],
        2 * tall * wide * last,
    )
    sends = [to_peer(value, "rep", at % peers + 1) for at, value in enumerate(sends)]
    others = [to_peer(squares, "rep", step) for step in range(1, count)]
    (base,) = call(
        part(base_kernel, count, tall * wide),
        [shape((rows, wide), FULL)],
        [momentum[0], squares, own],
        2 * rows * wide,
        in_specs=[pl.BlockSpec(memory_space=pltpu.VMEM)] * 3,
    )
    operands = [base, right_last, *others, *nears, *sends]
    (result,) = call(
        part(final_kernel, count, tall * wide),
        [shape((rows, wide), FULL)],
        operands,
        4 * rows * wide,
        in_specs=[pl.BlockSpec(memory_space=pltpu.VMEM)] * len(operands),
        out_specs=[anywhere],
        scratch_shapes=[pltpu.VMEM((rows, wide), FULL), pltpu.SemaphoreType.DMA((3,))],
    )
    return result[None]


def solution(mesh):
    in_specs = (
        P("rep", "layer", None, None),
        P("layer", "rep", None),
        P("layer", "rep", None),
        P("layer", "rep", None),
        P("layer", "rep", None),
        P("layer", "rep", None),
    )
    out_specs = P("layer", "rep", None)
    return jax.shard_map(body, mesh=mesh, in_specs=in_specs, out_specs=out_specs, check_vma=False)
```

```python
import functools

import jax
import jax.numpy as jnp
from jax import lax
from jax.experimental import pallas as pl
from jax.experimental.pallas import tpu as pltpu
from jax.sharding import PartitionSpec as P

SHARES = (2, 1, 1)
EARLY = 2
PARTS = 2
ROWS = 16
TILE = 256
HALF = jnp.bfloat16
FULL = jnp.float32


def passed_along(value, axis, steps):
    count = lax.axis_size(axis)
    initial, last = (max(0, -steps), min(count, count - steps))
    return lax.ppermute(value, axis, [(source, source + steps) for source in range(initial, last)])


def passed_round(value, axis):
    count = lax.axis_size(axis)
    return lax.ppermute(value, axis, [(source, (source + 1) % count) for source in range(count)])


def from_peers(value, axis):
    count = lax.axis_size(axis)
    return [
        lax.ppermute(value, axis, [(source, (source - step) % count) for source in range(count)])
        for step in range(1, count)
    ]


def to_peer(value, axis, step):
    count = lax.axis_size(axis)
    return lax.ppermute(
        value, axis, [(source, (source + step) % count) for source in range(count)]
    )


def dot(left, right, contract=((1,), (0,))):
    return lax.dot_general(left, right, (contract, ((), ())), preferred_element_type=FULL)


def span(me_ref, step, count, size):
    start = lax.rem(me_ref[0] + step, count) * size
    return pl.ds(pl.multiple_of(start, size), size)


def cut_kernel(widths, me, cross_out, inverse_out, inverse_in, pair, *refs):
    pieces, sems = refs[:-1], refs[-1]
    rows, start = cross_out.shape[0], 0
    copies = [
        pltpu.make_async_copy(cross_out, pair.at[:rows], sems.at[0]),
        pltpu.make_async_copy(inverse_out, pair.at[rows:], sems.at[1]),
    ]
    for at, width in enumerate(widths):
        source = inverse_in.at[:, start : start + width]
        copies.append(pltpu.make_async_copy(source, pieces[at], sems.at[2 + at]))
        start += width
    for copy in copies:
        copy.start()
    for copy in copies:
        copy.wait()


def first_kernel(count, me, following, own, *refs):
    others, out = refs[: count - 1], refs[-1]
    rows = own.shape[0]

    @pl.loop(0, out.shape[1] // TILE)
    def _(at):
        columns = pl.ds(pl.multiple_of(at * TILE, TILE), TILE)
        right = following[:, columns]
        out[span(me, 0, count, rows), columns] = dot(own[...], right).astype(HALF)
        for step in range(1, count):
            block = others[step - 1][:rows, :]
            out[span(me, step, count, rows), columns] = dot(block, right).astype(HALF)


def left_kernel(count, me, grads, first, inv_own, *refs):
    rights, others, out = refs[:count], refs[count : 2 * count - 1], refs[2 * count - 1]
    depth, rows = rights[0].shape[0], inv_own.shape[0]

    @pl.loop(0, out.shape[1] // TILE)
    def _(at):
        columns = pl.ds(pl.multiple_of(at * TILE, TILE), TILE)
        cross = sum(
            dot(first[:, span(me, step, count, depth)], rights[step][:, columns])
            for step in range(count)
        )
        residual = (grads[:, columns].astype(FULL) - cross).astype(HALF)
        out[span(me, 0, count, rows), columns] = dot(inv_own[...], residual).astype(HALF)
        for step in range(1, count):
            block = others[step - 1][rows:, :]
            out[span(me, step, count, rows), columns] = dot(block, residual).astype(HALF)


def mine_kernel(count, me, left, inv_own, out):
    @pl.loop(0, out.shape[1] // TILE)
    def _(at):
        columns = pl.ds(pl.multiple_of(at * TILE, TILE), TILE)
        out[:, columns] = dot(left[:, span(me, 0, count, inv_own.shape[0])], inv_own[:, columns])


def chunk_kernel(count, start, me, left, mine, cross_own, *refs):
    pieces, others = refs[: count - 1], refs[count - 1 : 2 * count - 2]
    precond, back = refs[2 * count - 2 :]
    depth, rows = pieces[0].shape[0], cross_own.shape[0]
    product = mine[:, start : start + precond.shape[1]]
    for step in range(1, count):
        product += dot(left[:, span(me, step, count, depth)], pieces[step - 1][...])
    precond[...] = product.astype(HALF)
    turned = ((0,), (0,))
    result = dot(cross_own[...], precond[span(me, 0, count, rows), :], turned)
    for step in range(1, count):
        block = others[step - 1][:rows, :]
        result += dot(block, precond[span(me, step, count, rows), :], turned)
    back[...] = result.astype(HALF)


def stack(target, values, lines=slice(None)):
    start = 0
    for value in values:
        target[:, start : start + value.shape[1]] = value[lines, :]
        start += value.shape[1]


def early_kernel(count, rows, me, *refs):
    total = len(SHARES)
    preconds, backs = refs[:total], refs[total : total + EARLY]
    rights = refs[total + EARLY : total + EARLY + count]
    nears, (staged, stacked) = refs[total + EARLY + count : -2], refs[-2:]
    depth, known, near = rights[0].shape[0], stacked.shape[1], staged.shape[0]
    for row_step in range(1, count):
        start = lax.rem(me[0] + row_step, count) * rows
        lines = pl.ds(pl.multiple_of(start, ROWS), near)
        stack(staged, preconds, lines)
        stack(stacked, backs, lines)
        for step in range(count):
            columns = span(me, step, count, depth)
            product = dot(stacked[...], rights[step][:, :known], ((1,), (1,)))
            update = staged[:, columns].astype(FULL) - product
            nears[row_step - 1][:, columns] = update.astype(HALF)


def gather_kernel(count, me, *refs):
    total = len(SHARES)
    preconds, backs = refs[:total], refs[total : 2 * total - 1]
    rights = refs[2 * total - 1 : 2 * total - 1 + count]
    partial, right_rest, staged, stacked = refs[2 * total - 1 + count :]
    depth, known = rights[0].shape[0], stacked.shape[1]
    stack(staged, preconds)
    stack(stacked, backs)
    for step in range(count):
        columns = span(me, step, count, depth)
        right_rest[columns, :] = rights[step][:, right_rest.shape[0] - right_rest.shape[1] :]
        right = rights[step][:, :known]
        for row in range(0, staged.shape[0], TILE):
            here = slice(row, row + TILE)
            product = dot(stacked[here, :], right, ((1,), (1,)))
            partial[here, columns] = staged[here, columns].astype(FULL) - product


def update_kernel(count, me, partial, right_rest, *refs):
    late = len(SHARES) - EARLY
    backs, (squares, own), refs = refs[:late], refs[late : late + 2], refs[late + 2 :]
    rests, fars = refs[: count - 1], refs[count - 1 :]
    rows, wide = own.shape
    back, total = backs[-1], jnp.zeros((), FULL)
    skipped = right_rest.shape[1] - back.shape[1]
    for step in range(count):
        here = span(me, step, count, rows)
        for start in range(0, wide, TILE):
            columns = slice(start, start + TILE)
            update = partial[here, columns] - dot(
                back[here, :], right_rest[columns, skipped:], ((1,), (1,))
            )
            total += jnp.sum(update * update)
            if step == 0:
                own[:, columns] = update
            else:
                row = rests[step - 1].shape[0]
                for far in fars[(step - 1) * PARTS : step * PARTS]:
                    far[:, columns] = update[row : row + far.shape[0]].astype(HALF)
                    row += far.shape[0]
        if step:
            start = lax.rem(me[0] + step, count) * rows
            lines = pl.ds(pl.multiple_of(start, ROWS), rests[step - 1].shape[0])
            stack(rests[step - 1], backs, lines)
    squares[...] = jnp.full(squares.shape, total, FULL)


def scale_of(squares, size):
    return lax.rsqrt(squares * (1.0 / size) + 1e-06)


def base_kernel(count, size, momentum, squares, own, out):
    scale = scale_of(squares[0:1, 0:1], size) * (1.0 / count)
    out[...] = 0.9 * momentum[...] + own[...] * scale


def final_kernel(count, size, base, right_rest, *refs):
    peers = count - 1
    others, nears, rests = (refs[at * peers : (at + 1) * peers] for at in range(3))
    fars = refs[3 * peers : (3 + PARTS) * peers]
    out, scratch, sems = refs[-3:]
    scales = [scale_of(value[0:1, 0:1], size) * (1.0 / count) for value in others]
    copies, row = [], nears[0].shape[0]
    for at in range(PARTS + 1):
        if at < PARTS:
            here = slice(row, row + fars[at].shape[0])
            row = here.stop
        else:
            here = slice(0, nears[0].shape[0])
        total = base[here, :]
        for step in range(peers):
            if at < PARTS:
                update = fars[step * PARTS + at][...].astype(FULL)
            else:
                rest = dot(rests[step][...], right_rest[...], ((1,), (1,)))
                update = nears[step][...].astype(FULL) - rest
            total += update * scales[step]
        scratch[here, :] = total
        copies.append(pltpu.make_async_copy(scratch.at[here, :], out.at[here, :], sems.at[at]))
        copies[-1].start()
    for copy in copies:
        copy.wait()


def call(kernel, outs, operands, flops, **options):
    moved = sum(value.size * value.dtype.itemsize for value in (*operands, *outs))
    vmem = pl.BlockSpec(memory_space=pltpu.VMEM)
    specs = [pl.BlockSpec(memory_space=pltpu.SMEM)] + [vmem] * (len(operands) - 1)
    settings = dict(in_specs=specs, out_specs=[vmem] * len(outs))
    settings.update(options)
    return pl.pallas_call(
        kernel,
        out_shape=outs,
        compiler_params=pltpu.CompilerParams(vmem_limit_bytes=16 * 1024 * 1024),
        cost_estimate=pl.CostEstimate(flops=flops, bytes_accessed=moved // 64, transcendentals=0),
        **settings,
    )(*operands)


def body(gradients, inverse_out, inverse_in, cross_out, cross_in, momentum):
    own_block = gradients[0, 0]
    tall, wide = own_block.shape
    count = lax.axis_size("rep")
    me = lax.axis_index("rep").astype(jnp.int32).reshape(1)
    widths = [share * wide // sum(SHARES) for share in SHARES]
    rows = momentum.shape[1]
    shape = jax.ShapeDtypeStruct
    part = functools.partial

    anywhere = pl.BlockSpec(memory_space=pl.ANY)
    out_rows, out_wide = cross_out.shape[1:]
    pair, *cuts = call(
        part(cut_kernel, widths),
        [shape((2 * out_rows, out_wide), HALF)]
        + [shape((inverse_in.shape[1], width), HALF) for width in widths],
        [me, cross_out[0], inverse_out[0], inverse_in[0]],
        0,
        in_specs=[pl.BlockSpec(memory_space=pltpu.SMEM)] + [anywhere] * 3,
        scratch_shapes=[pltpu.SemaphoreType.DMA((2 + len(widths),))],
    )
    pairs = from_peers(pair, "rep")
    in_blocks = [cross_in[0], *from_peers(cross_in[0], "rep")]
    following = passed_along(own_block, "layer", -1)

    cut_peers = [from_peers(piece, "rep") for piece in cuts]
    (first,) = call(
        part(first_kernel, count),
        [shape((tall, wide), HALF)],
        [me, following, cross_out[0], *pairs],
        tall * tall * wide // 32,
    )
    previous_blocks = [passed_along(block, "layer", 1) for block in in_blocks]
    (left,) = call(
        part(left_kernel, count),
        [shape((tall, wide), HALF)],
        [me, own_block, first, inverse_out[0], *in_blocks, *pairs],
        tall * wide * (tall + wide) // 32,
    )
    (mine,) = call(
        part(mine_kernel, count),
        [shape((tall, wide), FULL)],
        [me, left, inverse_in[0]],
        tall * wide * wide // 64,
    )
    preconds, backs = [], []
    for at, peers in enumerate(cut_peers):
        precond, back = call(
            part(chunk_kernel, count, sum(widths[:at])),
            [shape((tall, widths[at]), HALF)] * 2,
            [me, left, mine, cross_out[0], *peers, *pairs],
            tall * widths[at] * (tall + wide) // 32,
        )
        preconds.append(precond)
        backs.append(passed_round(back, "layer"))
    near = 3 * rows // 8 // ROWS * ROWS
    peers, last, later = count - 1, widths[-1], sum(widths[EARLY:])
    far_rows, left_rows = [], rows - near
    for at in range(PARTS, 0, -1):
        far_rows.append(left_rows if at == 1 else left_rows // at // ROWS * ROWS)
        left_rows -= far_rows[-1]
    nears = call(
        part(early_kernel, count, rows),
        [shape((near, wide), HALF)] * peers,
        [me, *preconds, *backs[:EARLY], *previous_blocks],
        2 * peers * near * wide * (wide - later),
        scratch_shapes=[pltpu.VMEM((near, wide), HALF), pltpu.VMEM((near, wide - later), HALF)],
    )
    nears = [to_peer(value, "rep", at + 1) for at, value in enumerate(nears)]
    partial, right_rest = call(
        part(gather_kernel, count),
        [shape((tall, wide), FULL), shape((wide, later), HALF)],
        [me, *preconds, *backs[:-1], *previous_blocks],
        2 * tall * wide * (wide - last),
        scratch_shapes=[pltpu.VMEM((tall, wide), HALF), pltpu.VMEM((tall, wide - last), HALF)],
    )
    squares, own, *sends = call(
        part(update_kernel, count),
        [shape((8, 128), FULL), shape((rows, wide), FULL)]
        + [shape((near, later), HALF)] * peers
        + [shape((size, wide), HALF) for size in far_rows] * peers,
        [me, partial, right_rest, *backs[EARLY:]],
        2 * tall * wide * last,
    )
    rests = [to_peer(value, "rep", at + 1) for at, value in enumerate(sends[:peers])]
    fars = [to_peer(value, "rep", at // PARTS + 1) for at, value in enumerate(sends[peers:])]
    others = [to_peer(squares, "rep", step) for step in range(1, count)]
    (base,) = call(
        part(base_kernel, count, tall * wide),
        [shape((rows, wide), FULL)],
        [momentum[0], squares, own],
        2 * rows * wide,
        in_specs=[pl.BlockSpec(memory_space=pltpu.VMEM)] * 3,
    )
    operands = [base, right_rest, *others, *nears, *rests, *fars]
    (result,) = call(
        part(final_kernel, count, tall * wide),
        [shape((rows, wide), FULL)],
        operands,
        4 * rows * wide,
        in_specs=[pl.BlockSpec(memory_space=pltpu.VMEM)] * len(operands),
        out_specs=[anywhere],
        scratch_shapes=[pltpu.VMEM((rows, wide), FULL), pltpu.SemaphoreType.DMA((PARTS + 1,))],
    )
    return result[None]


def solution(mesh):
    in_specs = (
        P("rep", "layer", None, None),
        P("layer", "rep", None),
        P("layer", "rep", None),
        P("layer", "rep", None),
        P("layer", "rep", None),
        P("layer", "rep", None),
    )
    out_specs = P("layer", "rep", None)
    return jax.shard_map(body, mesh=mesh, in_specs=in_specs, out_specs=out_specs, check_vma=False)
```

```python
import functools

import jax
import jax.numpy as jnp
from jax import lax
from jax.experimental import pallas as pl
from jax.experimental.pallas import tpu as pltpu
from jax.sharding import PartitionSpec as P

SHARES = (2, 1, 1)
ROWS = 16
TILE = 256
HALF = jnp.bfloat16
FULL = jnp.float32


def passed_along(value, axis, steps):
    count = lax.axis_size(axis)
    initial, last = (max(0, -steps), min(count, count - steps))
    return lax.ppermute(value, axis, [(source, source + steps) for source in range(initial, last)])


def passed_round(value, axis):
    count = lax.axis_size(axis)
    return lax.ppermute(value, axis, [(source, (source + 1) % count) for source in range(count)])


def from_peers(value, axis):
    count = lax.axis_size(axis)
    return [
        lax.ppermute(value, axis, [(source, (source - step) % count) for source in range(count)])
        for step in range(1, count)
    ]


def to_peer(value, axis, step):
    count = lax.axis_size(axis)
    return lax.ppermute(
        value, axis, [(source, (source + step) % count) for source in range(count)]
    )


def dot(left, right, contract=((1,), (0,))):
    return lax.dot_general(left, right, (contract, ((), ())), preferred_element_type=FULL)


def span(me_ref, step, count, size):
    start = lax.rem(me_ref[0] + step, count) * size
    return pl.ds(pl.multiple_of(start, size), size)


def cut_kernel(widths, me, cross_out, inverse_out, inverse_in, pair, *refs):
    pieces, sems = refs[:-1], refs[-1]
    rows, start = cross_out.shape[0], 0
    copies = [
        pltpu.make_async_copy(cross_out, pair.at[:rows], sems.at[0]),
        pltpu.make_async_copy(inverse_out, pair.at[rows:], sems.at[1]),
    ]
    for at, width in enumerate(widths):
        source = inverse_in.at[:, start : start + width]
        copies.append(pltpu.make_async_copy(source, pieces[at], sems.at[2 + at]))
        start += width
    for copy in copies:
        copy.start()
    for copy in copies:
        copy.wait()


def first_kernel(count, me, following, own, *refs):
    others, out = refs[: count - 1], refs[-1]
    rows = own.shape[0]

    @pl.loop(0, out.shape[1] // TILE)
    def _(at):
        columns = pl.ds(pl.multiple_of(at * TILE, TILE), TILE)
        right = following[:, columns]
        out[span(me, 0, count, rows), columns] = dot(own[...], right).astype(HALF)
        for step in range(1, count):
            block = others[step - 1][:rows, :]
            out[span(me, step, count, rows), columns] = dot(block, right).astype(HALF)


def left_kernel(count, me, grads, first, inv_own, *refs):
    rights, others, out = refs[:count], refs[count : 2 * count - 1], refs[2 * count - 1]
    depth, rows = rights[0].shape[0], inv_own.shape[0]

    @pl.loop(0, out.shape[1] // TILE)
    def _(at):
        columns = pl.ds(pl.multiple_of(at * TILE, TILE), TILE)
        cross = sum(
            dot(first[:, span(me, step, count, depth)], rights[step][:, columns])
            for step in range(count)
        )
        residual = (grads[:, columns].astype(FULL) - cross).astype(HALF)
        out[span(me, 0, count, rows), columns] = dot(inv_own[...], residual).astype(HALF)
        for step in range(1, count):
            block = others[step - 1][rows:, :]
            out[span(me, step, count, rows), columns] = dot(block, residual).astype(HALF)


def mine_kernel(count, me, left, inv_own, out):
    @pl.loop(0, out.shape[1] // TILE)
    def _(at):
        columns = pl.ds(pl.multiple_of(at * TILE, TILE), TILE)
        out[:, columns] = dot(left[:, span(me, 0, count, inv_own.shape[0])], inv_own[:, columns])


def chunk_kernel(count, start, me, left, mine, cross_own, *refs):
    pieces, others = refs[: count - 1], refs[count - 1 : 2 * count - 2]
    precond, back = refs[2 * count - 2 :]
    depth, rows = pieces[0].shape[0], cross_own.shape[0]
    product = mine[:, start : start + precond.shape[1]]
    for step in range(1, count):
        product += dot(left[:, span(me, step, count, depth)], pieces[step - 1][...])
    precond[...] = product.astype(HALF)
    turned = ((0,), (0,))
    result = dot(cross_own[...], precond[span(me, 0, count, rows), :], turned)
    for step in range(1, count):
        block = others[step - 1][:rows, :]
        result += dot(block, precond[span(me, step, count, rows), :], turned)
    back[...] = result.astype(HALF)


def stack(target, values, lines=slice(None)):
    start = 0
    for value in values:
        target[:, start : start + value.shape[1]] = value[lines, :]
        start += value.shape[1]


def early_kernel(count, rows, me, *refs):
    total = len(SHARES)
    preconds, backs = refs[:total], refs[total : 2 * total - 1]
    rights = refs[2 * total - 1 : 2 * total - 1 + count]
    nears, (staged, stacked) = refs[2 * total - 1 + count : -2], refs[-2:]
    depth, known, near = rights[0].shape[0], stacked.shape[1], staged.shape[0]
    for row_step in range(1, count):
        start = lax.rem(me[0] + row_step, count) * rows
        lines = pl.ds(pl.multiple_of(start, ROWS), near)
        stack(staged, preconds, lines)
        stack(stacked, backs, lines)
        for step in range(count):
            columns = span(me, step, count, depth)
            product = dot(stacked[...], rights[step][:, :known], ((1,), (1,)))
            update = staged[:, columns].astype(FULL) - product
            nears[row_step - 1][:, columns] = update.astype(HALF)


def gather_kernel(count, me, *refs):
    total = len(SHARES)
    preconds, backs = refs[:total], refs[total : 2 * total - 1]
    rights = refs[2 * total - 1 : 2 * total - 1 + count]
    partial, right_last, staged, stacked = refs[2 * total - 1 + count :]
    depth, known = rights[0].shape[0], stacked.shape[1]
    stack(staged, preconds)
    stack(stacked, backs)
    for step in range(count):
        columns = span(me, step, count, depth)
        right_last[columns, :] = rights[step][:, known:]
        right = rights[step][:, :known]
        for row in range(0, staged.shape[0], TILE):
            here = slice(row, row + TILE)
            product = dot(stacked[here, :], right, ((1,), (1,)))
            partial[here, columns] = staged[here, columns].astype(FULL) - product


def update_kernel(count, me, partial, back, right_last, *refs):
    squares, own = refs[:2]
    fars, rests = refs[2 : count + 1], refs[count + 1 :]
    rows, wide = own.shape
    total = jnp.zeros((), FULL)
    for step in range(count):
        here = span(me, step, count, rows)
        for start in range(0, wide, TILE):
            columns = slice(start, start + TILE)
            update = partial[here, columns] - dot(
                back[here, :], right_last[columns, :], ((1,), (1,))
            )
            total += jnp.sum(update * update)
            if step == 0:
                own[:, columns] = update
            else:
                near = rows - fars[step - 1].shape[0]
                fars[step - 1][:, columns] = update[near:].astype(HALF)
        if step:
            start = lax.rem(me[0] + step, count) * rows
            lines = pl.ds(pl.multiple_of(start, ROWS), rests[step - 1].shape[0])
            rests[step - 1][...] = back[lines, :]
    squares[...] = jnp.full(squares.shape, total, FULL)


def scale_of(squares, size):
    return lax.rsqrt(squares * (1.0 / size) + 1e-06)


def base_kernel(count, size, momentum, squares, own, out):
    scale = scale_of(squares[0:1, 0:1], size) * (1.0 / count)
    out[...] = 0.9 * momentum[...] + own[...] * scale


def final_kernel(count, size, base, right_last, *refs):
    peers = count - 1
    others, nears, fars, rests = (refs[at * peers : (at + 1) * peers] for at in range(4))
    out, scratch, sems = refs[-3:]
    near, rows = nears[0].shape[0], scratch.shape[0]
    middle = near // 2
    scales = [scale_of(value[0:1, 0:1], size) * (1.0 / count) for value in others]
    copies = []
    for at, here in enumerate((slice(near, rows), slice(0, middle), slice(middle, near))):
        total = base[here, :]
        for step in range(peers):
            if at == 0:
                update = fars[step][...].astype(FULL)
            else:
                rest = dot(rests[step][here, :], right_last[...], ((1,), (1,)))
                update = nears[step][here, :].astype(FULL) - rest
            total += update * scales[step]
        scratch[here, :] = total
        copies.append(pltpu.make_async_copy(scratch.at[here, :], out.at[here, :], sems.at[at]))
        copies[-1].start()
    for copy in copies:
        copy.wait()


def call(kernel, outs, operands, flops, **options):
    moved = sum(value.size * value.dtype.itemsize for value in (*operands, *outs))
    vmem = pl.BlockSpec(memory_space=pltpu.VMEM)
    specs = [pl.BlockSpec(memory_space=pltpu.SMEM)] + [vmem] * (len(operands) - 1)
    settings = dict(in_specs=specs, out_specs=[vmem] * len(outs))
    settings.update(options)
    return pl.pallas_call(
        kernel,
        out_shape=outs,
        compiler_params=pltpu.CompilerParams(vmem_limit_bytes=16 * 1024 * 1024),
        cost_estimate=pl.CostEstimate(flops=flops, bytes_accessed=moved // 64, transcendentals=0),
        **settings,
    )(*operands)


def body(gradients, inverse_out, inverse_in, cross_out, cross_in, momentum):
    own_block = gradients[0, 0]
    tall, wide = own_block.shape
    count = lax.axis_size("rep")
    me = lax.axis_index("rep").astype(jnp.int32).reshape(1)
    widths = [share * wide // sum(SHARES) for share in SHARES]
    rows = momentum.shape[1]
    shape = jax.ShapeDtypeStruct
    part = functools.partial

    anywhere = pl.BlockSpec(memory_space=pl.ANY)
    out_rows, out_wide = cross_out.shape[1:]
    pair, *cuts = call(
        part(cut_kernel, widths),
        [shape((2 * out_rows, out_wide), HALF)]
        + [shape((inverse_in.shape[1], width), HALF) for width in widths],
        [me, cross_out[0], inverse_out[0], inverse_in[0]],
        0,
        in_specs=[pl.BlockSpec(memory_space=pltpu.SMEM)] + [anywhere] * 3,
        scratch_shapes=[pltpu.SemaphoreType.DMA((2 + len(widths),))],
    )
    pairs = from_peers(pair, "rep")
    in_blocks = [cross_in[0], *from_peers(cross_in[0], "rep")]
    following = passed_along(own_block, "layer", -1)

    cut_peers = [from_peers(piece, "rep") for piece in cuts]
    (first,) = call(
        part(first_kernel, count),
        [shape((tall, wide), HALF)],
        [me, following, cross_out[0], *pairs],
        tall * tall * wide // 32,
    )
    previous_blocks = [passed_along(block, "layer", 1) for block in in_blocks]
    (left,) = call(
        part(left_kernel, count),
        [shape((tall, wide), HALF)],
        [me, own_block, first, inverse_out[0], *in_blocks, *pairs],
        tall * wide * (tall + wide) // 32,
    )
    (mine,) = call(
        part(mine_kernel, count),
        [shape((tall, wide), FULL)],
        [me, left, inverse_in[0]],
        tall * wide * wide // 64,
    )
    preconds, backs = [], []
    for at, peers in enumerate(cut_peers):
        precond, back = call(
            part(chunk_kernel, count, sum(widths[:at])),
            [shape((tall, widths[at]), HALF)] * 2,
            [me, left, mine, cross_out[0], *peers, *pairs],
            tall * widths[at] * (tall + wide) // 32,
        )
        preconds.append(precond)
        ring = at != 1
        backs.append(passed_round(back, "layer") if ring else passed_along(back, "layer", 1))
    near = 9 * rows // 16 // ROWS * ROWS
    peers, last = count - 1, widths[-1]
    nears = call(
        part(early_kernel, count, rows),
        [shape((near, wide), HALF)] * peers,
        [me, *preconds, *backs[:-1], *previous_blocks],
        2 * peers * near * wide * (wide - last),
        scratch_shapes=[pltpu.VMEM((near, wide), HALF), pltpu.VMEM((near, wide - last), HALF)],
    )
    nears = [to_peer(value, "rep", at + 1) for at, value in enumerate(nears)]
    partial, right_last = call(
        part(gather_kernel, count),
        [shape((tall, wide), FULL), shape((wide, last), HALF)],
        [me, *preconds, *backs[:-1], *previous_blocks],
        2 * tall * wide * (wide - last),
        scratch_shapes=[pltpu.VMEM((tall, wide), HALF), pltpu.VMEM((tall, wide - last), HALF)],
    )
    squares, own, *sends = call(
        part(update_kernel, count),
        [shape((8, 128), FULL), shape((rows, wide), FULL)]
        + [shape((rows - near, wide), HALF)] * peers
        + [shape((near, last), HALF)] * peers,
        [me, partial, backs[-1], right_last],
        2 * tall * wide * last,
    )
    sends = [to_peer(value, "rep", at % peers + 1) for at, value in enumerate(sends)]
    others = [to_peer(squares, "rep", step) for step in range(1, count)]
    (base,) = call(
        part(base_kernel, count, tall * wide),
        [shape((rows, wide), FULL)],
        [momentum[0], squares, own],
        2 * rows * wide,
        in_specs=[pl.BlockSpec(memory_space=pltpu.VMEM)] * 3,
    )
    operands = [base, right_last, *others, *nears, *sends]
    (result,) = call(
        part(final_kernel, count, tall * wide),
        [shape((rows, wide), FULL)],
        operands,
        4 * rows * wide,
        in_specs=[pl.BlockSpec(memory_space=pltpu.VMEM)] * len(operands),
        out_specs=[anywhere],
        scratch_shapes=[pltpu.VMEM((rows, wide), FULL), pltpu.SemaphoreType.DMA((3,))],
    )
    return result[None]


def solution(mesh):
    in_specs = (
        P("rep", "layer", None, None),
        P("layer", "rep", None),
        P("layer", "rep", None),
        P("layer", "rep", None),
        P("layer", "rep", None),
        P("layer", "rep", None),
    )
    out_specs = P("layer", "rep", None)
    return jax.shard_map(body, mesh=mesh, in_specs=in_specs, out_specs=out_specs, check_vma=False)
```

```python
import functools

import jax
import jax.numpy as jnp
from jax import lax
from jax.experimental import pallas as pl
from jax.experimental.pallas import tpu as pltpu
from jax.sharding import PartitionSpec as P

SHARES = (2, 1, 1)
EARLY = 2
PARTS = 2
ROWS = 16
TILE = 256
HALF = jnp.bfloat16
FULL = jnp.float32


def passed_along(value, axis, steps):
    count = lax.axis_size(axis)
    initial, last = (max(0, -steps), min(count, count - steps))
    return lax.ppermute(value, axis, [(source, source + steps) for source in range(initial, last)])


def passed_round(value, axis):
    count = lax.axis_size(axis)
    return lax.ppermute(value, axis, [(source, (source + 1) % count) for source in range(count)])


def from_peers(value, axis):
    count = lax.axis_size(axis)
    return [
        lax.ppermute(value, axis, [(source, (source - step) % count) for source in range(count)])
        for step in range(1, count)
    ]


def to_peer(value, axis, step):
    count = lax.axis_size(axis)
    return lax.ppermute(
        value, axis, [(source, (source + step) % count) for source in range(count)]
    )


def dot(left, right, contract=((1,), (0,))):
    return lax.dot_general(left, right, (contract, ((), ())), preferred_element_type=FULL)


def span(me_ref, step, count, size):
    start = lax.rem(me_ref[0] + step, count) * size
    return pl.ds(pl.multiple_of(start, size), size)


def cut_kernel(widths, me, cross_out, inverse_out, inverse_in, pair, *refs):
    pieces, sems = refs[:-1], refs[-1]
    rows, start = cross_out.shape[0], 0
    copies = [
        pltpu.make_async_copy(cross_out, pair.at[:rows], sems.at[0]),
        pltpu.make_async_copy(inverse_out, pair.at[rows:], sems.at[1]),
    ]
    for at, width in enumerate(widths):
        source = inverse_in.at[:, start : start + width]
        copies.append(pltpu.make_async_copy(source, pieces[at], sems.at[2 + at]))
        start += width
    for copy in copies:
        copy.start()
    for copy in copies:
        copy.wait()


def first_kernel(count, me, following, own, *refs):
    others, out = refs[: count - 1], refs[-1]
    rows = own.shape[0]

    @pl.loop(0, out.shape[1] // TILE)
    def _(at):
        columns = pl.ds(pl.multiple_of(at * TILE, TILE), TILE)
        right = following[:, columns]
        out[span(me, 0, count, rows), columns] = dot(own[...], right).astype(HALF)
        for step in range(1, count):
            block = others[step - 1][:rows, :]
            out[span(me, step, count, rows), columns] = dot(block, right).astype(HALF)


def left_kernel(count, me, grads, first, inv_own, *refs):
    rights, others, out = refs[:count], refs[count : 2 * count - 1], refs[2 * count - 1]
    depth, rows = rights[0].shape[0], inv_own.shape[0]

    @pl.loop(0, out.shape[1] // TILE)
    def _(at):
        columns = pl.ds(pl.multiple_of(at * TILE, TILE), TILE)
        cross = sum(
            dot(first[:, span(me, step, count, depth)], rights[step][:, columns])
            for step in range(count)
        )
        residual = (grads[:, columns].astype(FULL) - cross).astype(HALF)
        out[span(me, 0, count, rows), columns] = dot(inv_own[...], residual).astype(HALF)
        for step in range(1, count):
            block = others[step - 1][rows:, :]
            out[span(me, step, count, rows), columns] = dot(block, residual).astype(HALF)


def mine_kernel(count, me, left, inv_own, out):
    @pl.loop(0, out.shape[1] // TILE)
    def _(at):
        columns = pl.ds(pl.multiple_of(at * TILE, TILE), TILE)
        out[:, columns] = dot(left[:, span(me, 0, count, inv_own.shape[0])], inv_own[:, columns])


def chunk_kernel(count, start, me, left, mine, cross_own, *refs):
    pieces, others = refs[: count - 1], refs[count - 1 : 2 * count - 2]
    precond, back = refs[2 * count - 2 :]
    depth, rows = pieces[0].shape[0], cross_own.shape[0]
    product = mine[:, start : start + precond.shape[1]]
    for step in range(1, count):
        product += dot(left[:, span(me, step, count, depth)], pieces[step - 1][...])
    precond[...] = product.astype(HALF)
    turned = ((0,), (0,))
    result = dot(cross_own[...], precond[span(me, 0, count, rows), :], turned)
    for step in range(1, count):
        block = others[step - 1][:rows, :]
        result += dot(block, precond[span(me, step, count, rows), :], turned)
    back[...] = result.astype(HALF)


def stack(target, values, lines=slice(None)):
    start = 0
    for value in values:
        target[:, start : start + value.shape[1]] = value[lines, :]
        start += value.shape[1]


def early_kernel(count, rows, me, *refs):
    total = len(SHARES)
    preconds, backs = refs[:total], refs[total : total + EARLY]
    rights = refs[total + EARLY : total + EARLY + count]
    nears, (staged, stacked) = refs[total + EARLY + count : -2], refs[-2:]
    depth, known, near = rights[0].shape[0], stacked.shape[1], staged.shape[0]
    for row_step in range(1, count):
        start = lax.rem(me[0] + row_step, count) * rows
        lines = pl.ds(pl.multiple_of(start, ROWS), near)
        stack(staged, preconds, lines)
        stack(stacked, backs, lines)
        for step in range(count):
            columns = span(me, step, count, depth)
            product = dot(stacked[...], rights[step][:, :known], ((1,), (1,)))
            update = staged[:, columns].astype(FULL) - product
            nears[row_step - 1][:, columns] = update.astype(HALF)


def gather_kernel(count, me, *refs):
    total = len(SHARES)
    preconds, backs = refs[:total], refs[total : 2 * total - 1]
    rights = refs[2 * total - 1 : 2 * total - 1 + count]
    partial, right_rest, staged, stacked = refs[2 * total - 1 + count :]
    depth, known = rights[0].shape[0], stacked.shape[1]
    stack(staged, preconds)
    stack(stacked, backs)
    for step in range(count):
        columns = span(me, step, count, depth)
        right_rest[columns, :] = rights[step][:, right_rest.shape[0] - right_rest.shape[1] :]
        right = rights[step][:, :known]
        for row in range(0, staged.shape[0], TILE):
            here = slice(row, row + TILE)
            product = dot(stacked[here, :], right, ((1,), (1,)))
            partial[here, columns] = staged[here, columns].astype(FULL) - product


def update_kernel(count, me, partial, right_rest, *refs):
    late = len(SHARES) - EARLY
    backs, (squares, own), refs = refs[:late], refs[late : late + 2], refs[late + 2 :]
    rests, fars = refs[: count - 1], refs[count - 1 :]
    rows, wide = own.shape
    back, total = backs[-1], jnp.zeros((), FULL)
    skipped = right_rest.shape[1] - back.shape[1]
    for step in range(count):
        here = span(me, step, count, rows)
        for start in range(0, wide, TILE):
            columns = slice(start, start + TILE)
            update = partial[here, columns] - dot(
                back[here, :], right_rest[columns, skipped:], ((1,), (1,))
            )
            total += jnp.sum(update * update)
            if step == 0:
                own[:, columns] = update
            else:
                row = rests[step - 1].shape[0]
                for far in fars[(step - 1) * PARTS : step * PARTS]:
                    far[:, columns] = update[row : row + far.shape[0]].astype(HALF)
                    row += far.shape[0]
        if step:
            start = lax.rem(me[0] + step, count) * rows
            lines = pl.ds(pl.multiple_of(start, ROWS), rests[step - 1].shape[0])
            stack(rests[step - 1], backs, lines)
    squares[...] = jnp.full(squares.shape, total, FULL)


def scale_of(squares, size):
    return lax.rsqrt(squares * (1.0 / size) + 1e-06)


def base_kernel(count, size, momentum, squares, own, out):
    scale = scale_of(squares[0:1, 0:1], size) * (1.0 / count)
    out[...] = 0.9 * momentum[...] + own[...] * scale


def final_kernel(count, size, base, right_rest, *refs):
    peers = count - 1
    others, nears, rests = (refs[at * peers : (at + 1) * peers] for at in range(3))
    fars = refs[3 * peers : (3 + PARTS) * peers]
    out, scratch, sems = refs[-3:]
    scales = [scale_of(value[0:1, 0:1], size) * (1.0 / count) for value in others]
    copies, row = [], nears[0].shape[0]
    for at in range(PARTS + 1):
        if at < PARTS:
            here = slice(row, row + fars[at].shape[0])
            row = here.stop
        else:
            here = slice(0, nears[0].shape[0])
        total = base[here, :]
        for step in range(peers):
            if at < PARTS:
                update = fars[step * PARTS + at][...].astype(FULL)
            else:
                rest = dot(rests[step][...], right_rest[...], ((1,), (1,)))
                update = nears[step][...].astype(FULL) - rest
            total += update * scales[step]
        scratch[here, :] = total
        copies.append(pltpu.make_async_copy(scratch.at[here, :], out.at[here, :], sems.at[at]))
        copies[-1].start()
    for copy in copies:
        copy.wait()


def call(kernel, outs, operands, flops, **options):
    moved = sum(value.size * value.dtype.itemsize for value in (*operands, *outs))
    vmem = pl.BlockSpec(memory_space=pltpu.VMEM)
    specs = [pl.BlockSpec(memory_space=pltpu.SMEM)] + [vmem] * (len(operands) - 1)
    settings = dict(in_specs=specs, out_specs=[vmem] * len(outs))
    settings.update(options)
    return pl.pallas_call(
        kernel,
        out_shape=outs,
        compiler_params=pltpu.CompilerParams(vmem_limit_bytes=16 * 1024 * 1024),
        cost_estimate=pl.CostEstimate(flops=flops, bytes_accessed=moved // 64, transcendentals=0),
        **settings,
    )(*operands)


def body(gradients, inverse_out, inverse_in, cross_out, cross_in, momentum):
    own_block = gradients[0, 0]
    tall, wide = own_block.shape
    count = lax.axis_size("rep")
    me = lax.axis_index("rep").astype(jnp.int32).reshape(1)
    widths = [share * wide // sum(SHARES) for share in SHARES]
    rows = momentum.shape[1]
    shape = jax.ShapeDtypeStruct
    part = functools.partial

    anywhere = pl.BlockSpec(memory_space=pl.ANY)
    out_rows, out_wide = cross_out.shape[1:]
    pair, *cuts = call(
        part(cut_kernel, widths),
        [shape((2 * out_rows, out_wide), HALF)]
        + [shape((inverse_in.shape[1], width), HALF) for width in widths],
        [me, cross_out[0], inverse_out[0], inverse_in[0]],
        0,
        in_specs=[pl.BlockSpec(memory_space=pltpu.SMEM)] + [anywhere] * 3,
        scratch_shapes=[pltpu.SemaphoreType.DMA((2 + len(widths),))],
    )
    pairs = from_peers(pair, "rep")
    in_blocks = [cross_in[0], *from_peers(cross_in[0], "rep")]
    following = passed_along(own_block, "layer", -1)

    cut_peers = [from_peers(piece, "rep") for piece in cuts]
    (first,) = call(
        part(first_kernel, count),
        [shape((tall, wide), HALF)],
        [me, following, cross_out[0], *pairs],
        tall * tall * wide // 32,
    )
    previous_blocks = [passed_along(block, "layer", 1) for block in in_blocks]
    (left,) = call(
        part(left_kernel, count),
        [shape((tall, wide), HALF)],
        [me, own_block, first, inverse_out[0], *in_blocks, *pairs],
        tall * wide * (tall + wide) // 32,
    )
    (mine,) = call(
        part(mine_kernel, count),
        [shape((tall, wide), FULL)],
        [me, left, inverse_in[0]],
        tall * wide * wide // 64,
    )
    preconds, backs = [], []
    for at, peers in enumerate(cut_peers):
        precond, back = call(
            part(chunk_kernel, count, sum(widths[:at])),
            [shape((tall, widths[at]), HALF)] * 2,
            [me, left, mine, cross_out[0], *peers, *pairs],
            tall * widths[at] * (tall + wide) // 32,
        )
        preconds.append(precond)
        ring = at != 1
        backs.append(passed_round(back, "layer") if ring else passed_along(back, "layer", 1))
    near = 3 * rows // 8 // ROWS * ROWS
    peers, last, later = count - 1, widths[-1], sum(widths[EARLY:])
    far_rows, left_rows = [], rows - near
    for at in range(PARTS, 0, -1):
        far_rows.append(left_rows if at == 1 else left_rows // at // ROWS * ROWS)
        left_rows -= far_rows[-1]
    nears = call(
        part(early_kernel, count, rows),
        [shape((near, wide), HALF)] * peers,
        [me, *preconds, *backs[:EARLY], *previous_blocks],
        2 * peers * near * wide * (wide - later),
        scratch_shapes=[pltpu.VMEM((near, wide), HALF), pltpu.VMEM((near, wide - later), HALF)],
    )
    nears = [to_peer(value, "rep", at + 1) for at, value in enumerate(nears)]
    partial, right_rest = call(
        part(gather_kernel, count),
        [shape((tall, wide), FULL), shape((wide, later), HALF)],
        [me, *preconds, *backs[:-1], *previous_blocks],
        2 * tall * wide * (wide - last),
        scratch_shapes=[pltpu.VMEM((tall, wide), HALF), pltpu.VMEM((tall, wide - last), HALF)],
    )
    squares, own, *sends = call(
        part(update_kernel, count),
        [shape((8, 128), FULL), shape((rows, wide), FULL)]
        + [shape((near, later), HALF)] * peers
        + [shape((size, wide), HALF) for size in far_rows] * peers,
        [me, partial, right_rest, *backs[EARLY:]],
        2 * tall * wide * last,
    )
    rests = [to_peer(value, "rep", at + 1) for at, value in enumerate(sends[:peers])]
    fars = [to_peer(value, "rep", at // PARTS + 1) for at, value in enumerate(sends[peers:])]
    others = [to_peer(squares, "rep", step) for step in range(1, count)]
    (base,) = call(
        part(base_kernel, count, tall * wide),
        [shape((rows, wide), FULL)],
        [momentum[0], squares, own],
        2 * rows * wide,
        in_specs=[pl.BlockSpec(memory_space=pltpu.VMEM)] * 3,
    )
    operands = [base, right_rest, *others, *nears, *rests, *fars]
    (result,) = call(
        part(final_kernel, count, tall * wide),
        [shape((rows, wide), FULL)],
        operands,
        4 * rows * wide,
        in_specs=[pl.BlockSpec(memory_space=pltpu.VMEM)] * len(operands),
        out_specs=[anywhere],
        scratch_shapes=[pltpu.VMEM((rows, wide), FULL), pltpu.SemaphoreType.DMA((PARTS + 1,))],
    )
    return result[None]


def solution(mesh):
    in_specs = (
        P("rep", "layer", None, None),
        P("layer", "rep", None),
        P("layer", "rep", None),
        P("layer", "rep", None),
        P("layer", "rep", None),
        P("layer", "rep", None),
    )
    out_specs = P("layer", "rep", None)
    return jax.shard_map(body, mesh=mesh, in_specs=in_specs, out_specs=out_specs, check_vma=False)
```

```python
import functools

import jax
import jax.numpy as jnp
from jax import lax
from jax.experimental import pallas as pl
from jax.experimental.pallas import tpu as pltpu
from jax.sharding import PartitionSpec as P

SHARES = (2, 1, 1)
EARLY = 2
PARTS = 2
ROWS = 16
TILE = 256
HALF = jnp.bfloat16
FULL = jnp.float32


def passed_along(value, axis, steps):
    count = lax.axis_size(axis)
    initial, last = (max(0, -steps), min(count, count - steps))
    return lax.ppermute(value, axis, [(source, source + steps) for source in range(initial, last)])


def passed_round(value, axis):
    count = lax.axis_size(axis)
    return lax.ppermute(value, axis, [(source, (source + 1) % count) for source in range(count)])


def from_peers(value, axis):
    count = lax.axis_size(axis)
    return [
        lax.ppermute(value, axis, [(source, (source - step) % count) for source in range(count)])
        for step in range(1, count)
    ]


def to_peer(value, axis, step):
    count = lax.axis_size(axis)
    return lax.ppermute(
        value, axis, [(source, (source + step) % count) for source in range(count)]
    )


def dot(left, right, contract=((1,), (0,))):
    return lax.dot_general(left, right, (contract, ((), ())), preferred_element_type=FULL)


def span(me_ref, step, count, size):
    start = lax.rem(me_ref[0] + step, count) * size
    return pl.ds(pl.multiple_of(start, size), size)


def cut_kernel(widths, me, cross_out, inverse_out, inverse_in, pair, *refs):
    pieces, sems = refs[:-1], refs[-1]
    rows, start = cross_out.shape[0], 0
    copies = [
        pltpu.make_async_copy(cross_out, pair.at[:rows], sems.at[0]),
        pltpu.make_async_copy(inverse_out, pair.at[rows:], sems.at[1]),
    ]
    for at, width in enumerate(widths):
        source = inverse_in.at[:, start : start + width]
        copies.append(pltpu.make_async_copy(source, pieces[at], sems.at[2 + at]))
        start += width
    for copy in copies:
        copy.start()
    for copy in copies:
        copy.wait()


def first_kernel(count, me, following, own, *refs):
    others, out = refs[: count - 1], refs[-1]
    rows = own.shape[0]

    @pl.loop(0, out.shape[1] // TILE)
    def _(at):
        columns = pl.ds(pl.multiple_of(at * TILE, TILE), TILE)
        right = following[:, columns]
        out[span(me, 0, count, rows), columns] = dot(own[...], right).astype(HALF)
        for step in range(1, count):
            block = others[step - 1][:rows, :]
            out[span(me, step, count, rows), columns] = dot(block, right).astype(HALF)


def left_kernel(count, me, grads, first, inv_own, *refs):
    rights, others, out = refs[:count], refs[count : 2 * count - 1], refs[2 * count - 1]
    depth, rows = rights[0].shape[0], inv_own.shape[0]

    @pl.loop(0, out.shape[1] // TILE)
    def _(at):
        columns = pl.ds(pl.multiple_of(at * TILE, TILE), TILE)
        cross = sum(
            dot(first[:, span(me, step, count, depth)], rights[step][:, columns])
            for step in range(count)
        )
        residual = (grads[:, columns].astype(FULL) - cross).astype(HALF)
        out[span(me, 0, count, rows), columns] = dot(inv_own[...], residual).astype(HALF)
        for step in range(1, count):
            block = others[step - 1][rows:, :]
            out[span(me, step, count, rows), columns] = dot(block, residual).astype(HALF)


def mine_kernel(count, me, left, inv_own, out):
    @pl.loop(0, out.shape[1] // TILE)
    def _(at):
        columns = pl.ds(pl.multiple_of(at * TILE, TILE), TILE)
        out[:, columns] = dot(left[:, span(me, 0, count, inv_own.shape[0])], inv_own[:, columns])


def chunk_kernel(count, start, me, left, mine, cross_own, *refs):
    pieces, others = refs[: count - 1], refs[count - 1 : 2 * count - 2]
    precond, back = refs[2 * count - 2 :]
    depth, rows = pieces[0].shape[0], cross_own.shape[0]
    product = mine[:, start : start + precond.shape[1]]
    for step in range(1, count):
        product += dot(left[:, span(me, step, count, depth)], pieces[step - 1][...])
    precond[...] = product.astype(HALF)
    turned = ((0,), (0,))
    result = dot(cross_own[...], precond[span(me, 0, count, rows), :], turned)
    for step in range(1, count):
        block = others[step - 1][:rows, :]
        result += dot(block, precond[span(me, step, count, rows), :], turned)
    back[...] = result.astype(HALF)


def stack(target, values, lines=slice(None)):
    start = 0
    for value in values:
        target[:, start : start + value.shape[1]] = value[lines, :]
        start += value.shape[1]


def early_kernel(count, rows, me, *refs):
    total = len(SHARES)
    preconds, backs = refs[:total], refs[total : total + EARLY]
    rights = refs[total + EARLY : total + EARLY + count]
    nears, (staged, stacked) = refs[total + EARLY + count : -2], refs[-2:]
    depth, known, near = rights[0].shape[0], stacked.shape[1], staged.shape[0]
    for row_step in range(1, count):
        start = lax.rem(me[0] + row_step, count) * rows
        lines = pl.ds(pl.multiple_of(start, ROWS), near)
        stack(staged, preconds, lines)
        stack(stacked, backs, lines)
        for step in range(count):
            columns = span(me, step, count, depth)
            product = dot(stacked[...], rights[step][:, :known], ((1,), (1,)))
            update = staged[:, columns].astype(FULL) - product
            nears[row_step - 1][:, columns] = update.astype(HALF)


def gather_kernel(count, me, *refs):
    total = len(SHARES)
    preconds, backs = refs[:total], refs[total : 2 * total - 1]
    rights = refs[2 * total - 1 : 2 * total - 1 + count]
    partial, right_rest, staged, stacked = refs[2 * total - 1 + count :]
    depth, known = rights[0].shape[0], stacked.shape[1]
    stack(staged, preconds)
    stack(stacked, backs)
    for step in range(count):
        columns = span(me, step, count, depth)
        right_rest[columns, :] = rights[step][:, right_rest.shape[0] - right_rest.shape[1] :]
        right = rights[step][:, :known]
        for row in range(0, staged.shape[0], TILE):
            here = slice(row, row + TILE)
            product = dot(stacked[here, :], right, ((1,), (1,)))
            partial[here, columns] = staged[here, columns].astype(FULL) - product


def update_kernel(count, me, partial, right_rest, *refs):
    late = len(SHARES) - EARLY
    backs, (squares, own), refs = refs[:late], refs[late : late + 2], refs[late + 2 :]
    rests, fars = refs[: count - 1], refs[count - 1 :]
    rows, wide = own.shape
    back, total = backs[-1], jnp.zeros((), FULL)
    skipped = right_rest.shape[1] - back.shape[1]
    for step in range(count):
        here = span(me, step, count, rows)
        for start in range(0, wide, TILE):
            columns = slice(start, start + TILE)
            update = partial[here, columns] - dot(
                back[here, :], right_rest[columns, skipped:], ((1,), (1,))
            )
            total += jnp.sum(update * update)
            if step == 0:
                own[:, columns] = update
            else:
                row = rests[step - 1].shape[0]
                for far in fars[(step - 1) * PARTS : step * PARTS]:
                    far[:, columns] = update[row : row + far.shape[0]].astype(HALF)
                    row += far.shape[0]
        if step:
            start = lax.rem(me[0] + step, count) * rows
            lines = pl.ds(pl.multiple_of(start, ROWS), rests[step - 1].shape[0])
            stack(rests[step - 1], backs, lines)
    squares[...] = jnp.full(squares.shape, total, FULL)


def scale_of(squares, size):
    return lax.rsqrt(squares * (1.0 / size) + 1e-06)


def base_kernel(count, size, momentum, squares, own, out):
    scale = scale_of(squares[0:1, 0:1], size) * (1.0 / count)
    out[...] = 0.9 * momentum[...] + own[...] * scale


def final_kernel(count, size, base, right_rest, *refs):
    peers = count - 1
    others, nears, rests = (refs[at * peers : (at + 1) * peers] for at in range(3))
    fars = refs[3 * peers : (3 + PARTS) * peers]
    out, scratch, sems = refs[-3:]
    scales = [scale_of(value[0:1, 0:1], size) * (1.0 / count) for value in others]
    near, copies = nears[0].shape[0], []

    def store(here, updates):
        total = base[here, :]
        for step in range(peers):
            total += updates[step] * scales[step]
        scratch[here, :] = total
        at = len(copies)
        copies.append(pltpu.make_async_copy(scratch.at[here, :], out.at[here, :], sems.at[at]))
        copies[-1].start()

    store(
        slice(0, near),
        [
            nears[step][...].astype(FULL) - dot(rests[step][...], right_rest[...], ((1,), (1,)))
            for step in range(peers)
        ],
    )
    row = near
    for at in range(PARTS):
        size_here = fars[at].shape[0]
        blocks = [fars[step * PARTS + at] for step in range(peers)]
        first = size_here // 2 // ROWS * ROWS
        for lines in (slice(0, first), slice(first, size_here)):
            if lines.stop > lines.start:
                here = slice(row + lines.start, row + lines.stop)
                store(here, [block[lines, :].astype(FULL) for block in blocks])
        row += size_here
    for copy in copies:
        copy.wait()


def call(kernel, outs, operands, flops, **options):
    moved = sum(value.size * value.dtype.itemsize for value in (*operands, *outs))
    vmem = pl.BlockSpec(memory_space=pltpu.VMEM)
    specs = [pl.BlockSpec(memory_space=pltpu.SMEM)] + [vmem] * (len(operands) - 1)
    settings = dict(in_specs=specs, out_specs=[vmem] * len(outs))
    settings.update(options)
    return pl.pallas_call(
        kernel,
        out_shape=outs,
        compiler_params=pltpu.CompilerParams(vmem_limit_bytes=16 * 1024 * 1024),
        cost_estimate=pl.CostEstimate(flops=flops, bytes_accessed=moved // 64, transcendentals=0),
        **settings,
    )(*operands)


def body(gradients, inverse_out, inverse_in, cross_out, cross_in, momentum):
    own_block = gradients[0, 0]
    tall, wide = own_block.shape
    count = lax.axis_size("rep")
    me = lax.axis_index("rep").astype(jnp.int32).reshape(1)
    widths = [share * wide // sum(SHARES) for share in SHARES]
    rows = momentum.shape[1]
    shape = jax.ShapeDtypeStruct
    part = functools.partial

    anywhere = pl.BlockSpec(memory_space=pl.ANY)
    out_rows, out_wide = cross_out.shape[1:]
    pair, *cuts = call(
        part(cut_kernel, widths),
        [shape((2 * out_rows, out_wide), HALF)]
        + [shape((inverse_in.shape[1], width), HALF) for width in widths],
        [me, cross_out[0], inverse_out[0], inverse_in[0]],
        0,
        in_specs=[pl.BlockSpec(memory_space=pltpu.SMEM)] + [anywhere] * 3,
        scratch_shapes=[pltpu.SemaphoreType.DMA((2 + len(widths),))],
    )
    pairs = from_peers(pair, "rep")
    in_blocks = [cross_in[0], *from_peers(cross_in[0], "rep")]
    following = passed_along(own_block, "layer", -1)

    cut_peers = [from_peers(piece, "rep") for piece in cuts]
    (first,) = call(
        part(first_kernel, count),
        [shape((tall, wide), HALF)],
        [me, following, cross_out[0], *pairs],
        tall * tall * wide // 32,
    )
    previous_blocks = [passed_along(block, "layer", 1) for block in in_blocks]
    (left,) = call(
        part(left_kernel, count),
        [shape((tall, wide), HALF)],
        [me, own_block, first, inverse_out[0], *in_blocks, *pairs],
        tall * wide * (tall + wide) // 32,
    )
    (mine,) = call(
        part(mine_kernel, count),
        [shape((tall, wide), FULL)],
        [me, left, inverse_in[0]],
        tall * wide * wide // 64,
    )
    preconds, backs = [], []
    for at, peers in enumerate(cut_peers):
        precond, back = call(
            part(chunk_kernel, count, sum(widths[:at])),
            [shape((tall, widths[at]), HALF)] * 2,
            [me, left, mine, cross_out[0], *peers, *pairs],
            tall * widths[at] * (tall + wide) // 32,
        )
        preconds.append(precond)
        ring = at != 1
        backs.append(passed_round(back, "layer") if ring else passed_along(back, "layer", 1))
    near = 3 * rows // 8 // ROWS * ROWS
    peers, last, later = count - 1, widths[-1], sum(widths[EARLY:])
    far_rows, left_rows = [], rows - near
    for at in range(PARTS, 0, -1):
        far_rows.append(left_rows if at == 1 else left_rows // at // ROWS * ROWS)
        left_rows -= far_rows[-1]
    nears = call(
        part(early_kernel, count, rows),
        [shape((near, wide), HALF)] * peers,
        [me, *preconds, *backs[:EARLY], *previous_blocks],
        2 * peers * near * wide * (wide - later),
        scratch_shapes=[pltpu.VMEM((near, wide), HALF), pltpu.VMEM((near, wide - later), HALF)],
    )
    nears = [to_peer(value, "rep", at + 1) for at, value in enumerate(nears)]
    partial, right_rest = call(
        part(gather_kernel, count),
        [shape((tall, wide), FULL), shape((wide, later), HALF)],
        [me, *preconds, *backs[:-1], *previous_blocks],
        2 * tall * wide * (wide - last),
        scratch_shapes=[pltpu.VMEM((tall, wide), HALF), pltpu.VMEM((tall, wide - last), HALF)],
    )
    squares, own, *sends = call(
        part(update_kernel, count),
        [shape((8, 128), FULL), shape((rows, wide), FULL)]
        + [shape((near, later), HALF)] * peers
        + [shape((size, wide), HALF) for size in far_rows] * peers,
        [me, partial, right_rest, *backs[EARLY:]],
        2 * tall * wide * last,
    )
    rests = [to_peer(value, "rep", at + 1) for at, value in enumerate(sends[:peers])]
    fars = [to_peer(value, "rep", at // PARTS + 1) for at, value in enumerate(sends[peers:])]
    others = [to_peer(squares, "rep", step) for step in range(1, count)]
    (base,) = call(
        part(base_kernel, count, tall * wide),
        [shape((rows, wide), FULL)],
        [momentum[0], squares, own],
        2 * rows * wide,
        in_specs=[pl.BlockSpec(memory_space=pltpu.VMEM)] * 3,
    )
    pieces = 1 + sum(1 + (size // 2 >= ROWS) for size in far_rows)
    operands = [base, right_rest, *others, *nears, *rests, *fars]
    (result,) = call(
        part(final_kernel, count, tall * wide),
        [shape((rows, wide), FULL)],
        operands,
        4 * rows * wide,
        in_specs=[pl.BlockSpec(memory_space=pltpu.VMEM)] * len(operands),
        out_specs=[anywhere],
        scratch_shapes=[pltpu.VMEM((rows, wide), FULL), pltpu.SemaphoreType.DMA((pieces,))],
    )
    return result[None]


def solution(mesh):
    in_specs = (
        P("rep", "layer", None, None),
        P("layer", "rep", None),
        P("layer", "rep", None),
        P("layer", "rep", None),
        P("layer", "rep", None),
        P("layer", "rep", None),
    )
    out_specs = P("layer", "rep", None)
    return jax.shard_map(body, mesh=mesh, in_specs=in_specs, out_specs=out_specs, check_vma=False)
```

```python
import functools

import jax
import jax.numpy as jnp
from jax import lax
from jax.experimental import pallas as pl
from jax.experimental.pallas import tpu as pltpu
from jax.sharding import PartitionSpec as P

SHARES = (2, 1, 1)
EARLY = 2
PARTS = 2
ROWS = 16
TILE = 256
HALF = jnp.bfloat16
FULL = jnp.float32


def passed_along(value, axis, steps):
    count = lax.axis_size(axis)
    initial, last = (max(0, -steps), min(count, count - steps))
    return lax.ppermute(value, axis, [(source, source + steps) for source in range(initial, last)])


def passed_round(value, axis):
    count = lax.axis_size(axis)
    return lax.ppermute(value, axis, [(source, (source + 1) % count) for source in range(count)])


def from_peers(value, axis):
    count = lax.axis_size(axis)
    return [
        lax.ppermute(value, axis, [(source, (source - step) % count) for source in range(count)])
        for step in range(1, count)
    ]


def to_peer(value, axis, step):
    count = lax.axis_size(axis)
    return lax.ppermute(
        value, axis, [(source, (source + step) % count) for source in range(count)]
    )


def dot(left, right, contract=((1,), (0,))):
    return lax.dot_general(left, right, (contract, ((), ())), preferred_element_type=FULL)


def span(me_ref, step, count, size):
    start = lax.rem(me_ref[0] + step, count) * size
    return pl.ds(pl.multiple_of(start, size), size)


def cut_kernel(widths, me, cross_out, inverse_out, inverse_in, pair, *refs):
    pieces, sems = refs[:-1], refs[-1]
    rows, start = cross_out.shape[0], 0
    copies = [
        pltpu.make_async_copy(cross_out, pair.at[:rows], sems.at[0]),
        pltpu.make_async_copy(inverse_out, pair.at[rows:], sems.at[1]),
    ]
    for at, width in enumerate(widths):
        source = inverse_in.at[:, start : start + width]
        copies.append(pltpu.make_async_copy(source, pieces[at], sems.at[2 + at]))
        start += width
    for copy in copies:
        copy.start()
    for copy in copies:
        copy.wait()


def first_kernel(count, me, following, own, *refs):
    others, out = refs[: count - 1], refs[-1]
    rows = own.shape[0]

    @pl.loop(0, out.shape[1] // TILE)
    def _(at):
        columns = pl.ds(pl.multiple_of(at * TILE, TILE), TILE)
        right = following[:, columns]
        out[span(me, 0, count, rows), columns] = dot(own[...], right).astype(HALF)
        for step in range(1, count):
            block = others[step - 1][:rows, :]
            out[span(me, step, count, rows), columns] = dot(block, right).astype(HALF)


def left_kernel(count, me, grads, first, inv_own, *refs):
    rights, others, out = refs[:count], refs[count : 2 * count - 1], refs[2 * count - 1]
    depth, rows = rights[0].shape[0], inv_own.shape[0]

    @pl.loop(0, out.shape[1] // TILE)
    def _(at):
        columns = pl.ds(pl.multiple_of(at * TILE, TILE), TILE)
        cross = sum(
            dot(first[:, span(me, step, count, depth)], rights[step][:, columns])
            for step in range(count)
        )
        residual = (grads[:, columns].astype(FULL) - cross).astype(HALF)
        out[span(me, 0, count, rows), columns] = dot(inv_own[...], residual).astype(HALF)
        for step in range(1, count):
            block = others[step - 1][rows:, :]
            out[span(me, step, count, rows), columns] = dot(block, residual).astype(HALF)


def mine_kernel(count, me, left, inv_own, out):
    @pl.loop(0, out.shape[1] // TILE)
    def _(at):
        columns = pl.ds(pl.multiple_of(at * TILE, TILE), TILE)
        out[:, columns] = dot(left[:, span(me, 0, count, inv_own.shape[0])], inv_own[:, columns])


def chunk_kernel(count, start, me, left, mine, cross_own, *refs):
    pieces, others = refs[: count - 1], refs[count - 1 : 2 * count - 2]
    precond, back = refs[2 * count - 2 :]
    depth, rows = pieces[0].shape[0], cross_own.shape[0]
    product = mine[:, start : start + precond.shape[1]]
    for step in range(1, count):
        product += dot(left[:, span(me, step, count, depth)], pieces[step - 1][...])
    precond[...] = product.astype(HALF)
    turned = ((0,), (0,))
    result = dot(cross_own[...], precond[span(me, 0, count, rows), :], turned)
    for step in range(1, count):
        block = others[step - 1][:rows, :]
        result += dot(block, precond[span(me, step, count, rows), :], turned)
    back[...] = result.astype(HALF)


def stack(target, values, lines=slice(None)):
    start = 0
    for value in values:
        target[:, start : start + value.shape[1]] = value[lines, :]
        start += value.shape[1]


def early_kernel(count, rows, me, *refs):
    total = len(SHARES)
    preconds, backs = refs[:total], refs[total : total + EARLY]
    rights = refs[total + EARLY : total + EARLY + count]
    nears, (staged, stacked) = refs[total + EARLY + count : -2], refs[-2:]
    depth, known, near = rights[0].shape[0], stacked.shape[1], staged.shape[0]
    for row_step in range(1, count):
        start = lax.rem(me[0] + row_step, count) * rows
        lines = pl.ds(pl.multiple_of(start, ROWS), near)
        stack(staged, preconds, lines)
        stack(stacked, backs, lines)
        for step in range(count):
            columns = span(me, step, count, depth)
            product = dot(stacked[...], rights[step][:, :known], ((1,), (1,)))
            update = staged[:, columns].astype(FULL) - product
            nears[row_step - 1][:, columns] = update.astype(HALF)


def gather_kernel(count, me, *refs):
    total = len(SHARES)
    preconds, backs = refs[:total], refs[total : 2 * total - 1]
    rights = refs[2 * total - 1 : 2 * total - 1 + count]
    partial, right_rest, staged, stacked = refs[2 * total - 1 + count :]
    depth, known = rights[0].shape[0], stacked.shape[1]
    stack(staged, preconds)
    stack(stacked, backs)
    for step in range(count):
        columns = span(me, step, count, depth)
        right_rest[columns, :] = rights[step][:, right_rest.shape[0] - right_rest.shape[1] :]
        right = rights[step][:, :known]
        for row in range(0, staged.shape[0], TILE):
            here = slice(row, row + TILE)
            product = dot(stacked[here, :], right, ((1,), (1,)))
            partial[here, columns] = staged[here, columns].astype(FULL) - product


def update_kernel(count, me, partial, right_rest, *refs):
    late = len(SHARES) - EARLY
    backs, (squares, own), refs = refs[:late], refs[late : late + 2], refs[late + 2 :]
    rests, fars = refs[: count - 1], refs[count - 1 :]
    rows, wide = own.shape
    back, total = backs[-1], jnp.zeros((), FULL)
    skipped = right_rest.shape[1] - back.shape[1]
    for step in range(count):
        here = span(me, step, count, rows)
        for start in range(0, wide, TILE):
            columns = slice(start, start + TILE)
            update = partial[here, columns] - dot(
                back[here, :], right_rest[columns, skipped:], ((1,), (1,))
            )
            total += jnp.sum(update * update)
            if step == 0:
                own[:, columns] = update
            else:
                row = rests[step - 1].shape[0]
                for far in fars[(step - 1) * PARTS : step * PARTS]:
                    far[:, columns] = update[row : row + far.shape[0]].astype(HALF)
                    row += far.shape[0]
        if step:
            start = lax.rem(me[0] + step, count) * rows
            lines = pl.ds(pl.multiple_of(start, ROWS), rests[step - 1].shape[0])
            stack(rests[step - 1], backs, lines)
    squares[...] = jnp.full(squares.shape, total, FULL)


def scale_of(squares, size):
    return lax.rsqrt(squares * (1.0 / size) + 1e-06)


def base_kernel(count, size, momentum, squares, own, out):
    scale = scale_of(squares[0:1, 0:1], size) * (1.0 / count)
    out[...] = 0.9 * momentum[...] + own[...] * scale


def final_kernel(count, size, base, right_rest, *refs):
    peers = count - 1
    others, nears, rests = (refs[at * peers : (at + 1) * peers] for at in range(3))
    fars = refs[3 * peers : (3 + PARTS) * peers]
    out, scratch, sems = refs[-3:]
    scales = [scale_of(value[0:1, 0:1], size) * (1.0 / count) for value in others]
    copies, row = [], nears[0].shape[0]
    for at in range(PARTS + 1):
        if at < PARTS:
            here = slice(row, row + fars[at].shape[0])
            row = here.stop
        else:
            here = slice(0, nears[0].shape[0])
        total = base[here, :]
        for step in range(peers):
            if at < PARTS:
                update = fars[step * PARTS + at][...].astype(FULL)
            else:
                rest = dot(rests[step][...], right_rest[...], ((1,), (1,)))
                update = nears[step][...].astype(FULL) - rest
            total += update * scales[step]
        scratch[here, :] = total
        if at >= PARTS - 1:
            done = slice(nears[0].shape[0], row) if at < PARTS else here
            sem = sems.at[at - PARTS + 1]
            copies.append(pltpu.make_async_copy(scratch.at[done, :], out.at[done, :], sem))
            copies[-1].start()
    for copy in copies:
        copy.wait()


def call(kernel, outs, operands, flops, **options):
    moved = sum(value.size * value.dtype.itemsize for value in (*operands, *outs))
    vmem = pl.BlockSpec(memory_space=pltpu.VMEM)
    specs = [pl.BlockSpec(memory_space=pltpu.SMEM)] + [vmem] * (len(operands) - 1)
    settings = dict(in_specs=specs, out_specs=[vmem] * len(outs))
    settings.update(options)
    return pl.pallas_call(
        kernel,
        out_shape=outs,
        compiler_params=pltpu.CompilerParams(vmem_limit_bytes=16 * 1024 * 1024),
        cost_estimate=pl.CostEstimate(flops=flops, bytes_accessed=moved // 64, transcendentals=0),
        **settings,
    )(*operands)


def body(gradients, inverse_out, inverse_in, cross_out, cross_in, momentum):
    own_block = gradients[0, 0]
    tall, wide = own_block.shape
    count = lax.axis_size("rep")
    me = lax.axis_index("rep").astype(jnp.int32).reshape(1)
    widths = [share * wide // sum(SHARES) for share in SHARES]
    rows = momentum.shape[1]
    shape = jax.ShapeDtypeStruct
    part = functools.partial

    anywhere = pl.BlockSpec(memory_space=pl.ANY)
    out_rows, out_wide = cross_out.shape[1:]
    pair, *cuts = call(
        part(cut_kernel, widths),
        [shape((2 * out_rows, out_wide), HALF)]
        + [shape((inverse_in.shape[1], width), HALF) for width in widths],
        [me, cross_out[0], inverse_out[0], inverse_in[0]],
        0,
        in_specs=[pl.BlockSpec(memory_space=pltpu.SMEM)] + [anywhere] * 3,
        scratch_shapes=[pltpu.SemaphoreType.DMA((2 + len(widths),))],
    )
    pairs = from_peers(pair, "rep")
    in_blocks = [cross_in[0], *from_peers(cross_in[0], "rep")]
    following = passed_along(own_block, "layer", -1)

    cut_peers = [from_peers(piece, "rep") for piece in cuts]
    (first,) = call(
        part(first_kernel, count),
        [shape((tall, wide), HALF)],
        [me, following, cross_out[0], *pairs],
        tall * tall * wide // 32,
    )
    previous_blocks = [passed_along(block, "layer", 1) for block in in_blocks]
    (left,) = call(
        part(left_kernel, count),
        [shape((tall, wide), HALF)],
        [me, own_block, first, inverse_out[0], *in_blocks, *pairs],
        tall * wide * (tall + wide) // 32,
    )
    (mine,) = call(
        part(mine_kernel, count),
        [shape((tall, wide), FULL)],
        [me, left, inverse_in[0]],
        tall * wide * wide // 64,
    )
    preconds, backs = [], []
    for at, peers in enumerate(cut_peers):
        precond, back = call(
            part(chunk_kernel, count, sum(widths[:at])),
            [shape((tall, widths[at]), HALF)] * 2,
            [me, left, mine, cross_out[0], *peers, *pairs],
            tall * widths[at] * (tall + wide) // 32,
        )
        preconds.append(precond)
        ring = at != 1
        backs.append(passed_round(back, "layer") if ring else passed_along(back, "layer", 1))
    near = 3 * rows // 8 // ROWS * ROWS
    peers, last, later = count - 1, widths[-1], sum(widths[EARLY:])
    far_rows, left_rows = [], rows - near
    for at in range(PARTS, 0, -1):
        far_rows.append(left_rows if at == 1 else left_rows // at // ROWS * ROWS)
        left_rows -= far_rows[-1]
    nears = call(
        part(early_kernel, count, rows),
        [shape((near, wide), HALF)] * peers,
        [me, *preconds, *backs[:EARLY], *previous_blocks],
        2 * peers * near * wide * (wide - later),
        scratch_shapes=[pltpu.VMEM((near, wide), HALF), pltpu.VMEM((near, wide - later), HALF)],
    )
    nears = [to_peer(value, "rep", at + 1) for at, value in enumerate(nears)]
    partial, right_rest = call(
        part(gather_kernel, count),
        [shape((tall, wide), FULL), shape((wide, later), HALF)],
        [me, *preconds, *backs[:-1], *previous_blocks],
        2 * tall * wide * (wide - last),
        scratch_shapes=[pltpu.VMEM((tall, wide), HALF), pltpu.VMEM((tall, wide - last), HALF)],
    )
    squares, own, *sends = call(
        part(update_kernel, count),
        [shape((8, 128), FULL), shape((rows, wide), FULL)]
        + [shape((near, later), HALF)] * peers
        + [shape((size, wide), HALF) for size in far_rows] * peers,
        [me, partial, right_rest, *backs[EARLY:]],
        2 * tall * wide * last,
    )
    rests = [to_peer(value, "rep", at + 1) for at, value in enumerate(sends[:peers])]
    fars = [to_peer(value, "rep", at // PARTS + 1) for at, value in enumerate(sends[peers:])]
    others = [to_peer(squares, "rep", step) for step in range(1, count)]
    (base,) = call(
        part(base_kernel, count, tall * wide),
        [shape((rows, wide), FULL)],
        [momentum[0], squares, own],
        2 * rows * wide,
        in_specs=[pl.BlockSpec(memory_space=pltpu.VMEM)] * 3,
    )
    operands = [base, right_rest, *others, *nears, *rests, *fars]
    (result,) = call(
        part(final_kernel, count, tall * wide),
        [shape((rows, wide), FULL)],
        operands,
        4 * rows * wide,
        in_specs=[pl.BlockSpec(memory_space=pltpu.VMEM)] * len(operands),
        out_specs=[anywhere],
        scratch_shapes=[pltpu.VMEM((rows, wide), FULL), pltpu.SemaphoreType.DMA((2,))],
    )
    return result[None]


def solution(mesh):
    in_specs = (
        P("rep", "layer", None, None),
        P("layer", "rep", None),
        P("layer", "rep", None),
        P("layer", "rep", None),
        P("layer", "rep", None),
        P("layer", "rep", None),
    )
    out_specs = P("layer", "rep", None)
    return jax.shard_map(body, mesh=mesh, in_specs=in_specs, out_specs=out_specs, check_vma=False)
```

```python
import functools

import jax
import jax.numpy as jnp
from jax import lax
from jax.experimental import pallas as pl
from jax.experimental.pallas import tpu as pltpu
from jax.sharding import PartitionSpec as P

SHARES = (2, 1, 1)
EARLY = 2
PARTS = 2
ROWS = 16
TILE = 256
HALF = jnp.bfloat16
FULL = jnp.float32


def passed_along(value, axis, steps):
    count = lax.axis_size(axis)
    initial, last = (max(0, -steps), min(count, count - steps))
    return lax.ppermute(value, axis, [(source, source + steps) for source in range(initial, last)])


def passed_round(value, axis):
    count = lax.axis_size(axis)
    return lax.ppermute(value, axis, [(source, (source + 1) % count) for source in range(count)])


def from_peers(value, axis):
    count = lax.axis_size(axis)
    return [
        lax.ppermute(value, axis, [(source, (source - step) % count) for source in range(count)])
        for step in range(1, count)
    ]


def to_peer(value, axis, step):
    count = lax.axis_size(axis)
    return lax.ppermute(
        value, axis, [(source, (source + step) % count) for source in range(count)]
    )


def dot(left, right, contract=((1,), (0,))):
    return lax.dot_general(left, right, (contract, ((), ())), preferred_element_type=FULL)


def span(me_ref, step, count, size):
    start = lax.rem(me_ref[0] + step, count) * size
    return pl.ds(pl.multiple_of(start, size), size)


def cut_kernel(widths, me, cross_out, inverse_out, inverse_in, pair, *refs):
    pieces, sems = refs[:-1], refs[-1]
    rows, start = cross_out.shape[0], 0
    copies = [
        pltpu.make_async_copy(cross_out, pair.at[:rows], sems.at[0]),
        pltpu.make_async_copy(inverse_out, pair.at[rows:], sems.at[1]),
    ]
    for at, width in enumerate(widths):
        source = inverse_in.at[:, start : start + width]
        copies.append(pltpu.make_async_copy(source, pieces[at], sems.at[2 + at]))
        start += width
    for copy in copies:
        copy.start()
    for copy in copies:
        copy.wait()


def first_kernel(count, me, following, own, *refs):
    others, out = refs[: count - 1], refs[-1]
    rows = own.shape[0]

    @pl.loop(0, out.shape[1] // TILE)
    def _(at):
        columns = pl.ds(pl.multiple_of(at * TILE, TILE), TILE)
        right = following[:, columns]
        out[span(me, 0, count, rows), columns] = dot(own[...], right).astype(HALF)
        for step in range(1, count):
            block = others[step - 1][:rows, :]
            out[span(me, step, count, rows), columns] = dot(block, right).astype(HALF)


def left_kernel(count, me, grads, first, inv_own, *refs):
    rights, others, out = refs[:count], refs[count : 2 * count - 1], refs[2 * count - 1]
    depth, rows = rights[0].shape[0], inv_own.shape[0]

    @pl.loop(0, out.shape[1] // TILE)
    def _(at):
        columns = pl.ds(pl.multiple_of(at * TILE, TILE), TILE)
        cross = sum(
            dot(first[:, span(me, step, count, depth)], rights[step][:, columns])
            for step in range(count)
        )
        residual = (grads[:, columns].astype(FULL) - cross).astype(HALF)
        out[span(me, 0, count, rows), columns] = dot(inv_own[...], residual).astype(HALF)
        for step in range(1, count):
            block = others[step - 1][rows:, :]
            out[span(me, step, count, rows), columns] = dot(block, residual).astype(HALF)


def mine_kernel(count, me, left, inv_own, out):
    @pl.loop(0, out.shape[1] // TILE)
    def _(at):
        columns = pl.ds(pl.multiple_of(at * TILE, TILE), TILE)
        out[:, columns] = dot(left[:, span(me, 0, count, inv_own.shape[0])], inv_own[:, columns])


def chunk_kernel(count, start, me, left, mine, cross_own, *refs):
    pieces, others = refs[: count - 1], refs[count - 1 : 2 * count - 2]
    precond, back = refs[2 * count - 2 :]
    depth, rows = pieces[0].shape[0], cross_own.shape[0]
    product = mine[:, start : start + precond.shape[1]]
    for step in range(1, count):
        product += dot(left[:, span(me, step, count, depth)], pieces[step - 1][...])
    precond[...] = product.astype(HALF)
    turned = ((0,), (0,))
    result = dot(cross_own[...], precond[span(me, 0, count, rows), :], turned)
    for step in range(1, count):
        block = others[step - 1][:rows, :]
        result += dot(block, precond[span(me, step, count, rows), :], turned)
    back[...] = result.astype(HALF)


def stack(target, values, lines=slice(None)):
    start = 0
    for value in values:
        target[:, start : start + value.shape[1]] = value[lines, :]
        start += value.shape[1]


def early_kernel(count, rows, me, *refs):
    total = len(SHARES)
    preconds, backs = refs[:total], refs[total : total + EARLY]
    rights = refs[total + EARLY : total + EARLY + count]
    nears, (staged, stacked) = refs[total + EARLY + count : -2], refs[-2:]
    depth, known, near = rights[0].shape[0], stacked.shape[1], staged.shape[0]
    for row_step in range(1, count):
        start = lax.rem(me[0] + row_step, count) * rows
        lines = pl.ds(pl.multiple_of(start, ROWS), near)
        stack(staged, preconds, lines)
        stack(stacked, backs, lines)
        for step in range(count):
            columns = span(me, step, count, depth)
            product = dot(stacked[...], rights[step][:, :known], ((1,), (1,)))
            update = staged[:, columns].astype(FULL) - product
            nears[row_step - 1][:, columns] = update.astype(HALF)


def gather_kernel(count, me, *refs):
    total = len(SHARES)
    preconds, backs = refs[:total], refs[total : 2 * total - 1]
    rights = refs[2 * total - 1 : 2 * total - 1 + count]
    partial, right_rest, staged, stacked = refs[2 * total - 1 + count :]
    depth, known = rights[0].shape[0], stacked.shape[1]
    stack(staged, preconds)
    stack(stacked, backs)
    for step in range(count):
        columns = span(me, step, count, depth)
        right_rest[columns, :] = rights[step][:, right_rest.shape[0] - right_rest.shape[1] :]
        right = rights[step][:, :known]
        for row in range(0, staged.shape[0], TILE):
            here = slice(row, row + TILE)
            product = dot(stacked[here, :], right, ((1,), (1,)))
            partial[here, columns] = staged[here, columns].astype(FULL) - product


def update_kernel(count, me, partial, right_rest, *refs):
    late = len(SHARES) - EARLY
    backs, (squares, own), refs = refs[:late], refs[late : late + 2], refs[late + 2 :]
    rests, fars = refs[: count - 1], refs[count - 1 :]
    rows, wide = own.shape
    back, total = backs[-1], jnp.zeros((), FULL)
    skipped = right_rest.shape[1] - back.shape[1]
    for step in range(count):
        here = span(me, step, count, rows)
        for start in range(0, wide, TILE):
            columns = slice(start, start + TILE)
            update = partial[here, columns] - dot(
                back[here, :], right_rest[columns, skipped:], ((1,), (1,))
            )
            total += jnp.sum(update * update)
            if step == 0:
                own[:, columns] = update
            else:
                row = rests[step - 1].shape[0]
                for far in fars[(step - 1) * PARTS : step * PARTS]:
                    far[:, columns] = update[row : row + far.shape[0]].astype(HALF)
                    row += far.shape[0]
        if step:
            start = lax.rem(me[0] + step, count) * rows
            lines = pl.ds(pl.multiple_of(start, ROWS), rests[step - 1].shape[0])
            stack(rests[step - 1], backs, lines)
    squares[...] = jnp.full(squares.shape, total, FULL)


def scale_of(squares, size):
    return lax.rsqrt(squares * (1.0 / size) + 1e-06)


def base_kernel(count, size, momentum, squares, own, out):
    scale = scale_of(squares[0:1, 0:1], size) * (1.0 / count)
    out[...] = 0.9 * momentum[...] + own[...] * scale


def final_kernel(count, size, base, right_rest, *refs):
    peers = count - 1
    others, nears, rests = (refs[at * peers : (at + 1) * peers] for at in range(3))
    fars = refs[3 * peers : (3 + PARTS) * peers]
    out, scratch, sems = refs[-3:]
    scales = [scale_of(value[0:1, 0:1], size) * (1.0 / count) for value in others]
    copies, row = [], nears[0].shape[0]
    for at in range(PARTS + 1):
        if at < PARTS:
            here = slice(row, row + fars[at].shape[0])
            row = here.stop
        else:
            here = slice(0, nears[0].shape[0])
        total = base[here, :]
        for step in range(peers):
            if at < PARTS:
                update = fars[step * PARTS + at][...].astype(FULL)
            else:
                rest = dot(rests[step][...], right_rest[...], ((1,), (1,)))
                update = nears[step][...].astype(FULL) - rest
            total += update * scales[step]
        scratch[here, :] = total
        copies.append(pltpu.make_async_copy(scratch.at[here, :], out.at[here, :], sems.at[at]))
        copies[-1].start()
    for copy in copies:
        copy.wait()


def call(kernel, outs, operands, flops, **options):
    moved = sum(value.size * value.dtype.itemsize for value in (*operands, *outs))
    vmem = pl.BlockSpec(memory_space=pltpu.VMEM)
    specs = [pl.BlockSpec(memory_space=pltpu.SMEM)] + [vmem] * (len(operands) - 1)
    settings = dict(in_specs=specs, out_specs=[vmem] * len(outs))
    settings.update(options)
    return pl.pallas_call(
        kernel,
        out_shape=outs,
        compiler_params=pltpu.CompilerParams(vmem_limit_bytes=16 * 1024 * 1024),
        cost_estimate=pl.CostEstimate(flops=flops, bytes_accessed=moved // 64, transcendentals=0),
        **settings,
    )(*operands)


def body(gradients, inverse_out, inverse_in, cross_out, cross_in, momentum):
    own_block = gradients[0, 0]
    tall, wide = own_block.shape
    count = lax.axis_size("rep")
    me = lax.axis_index("rep").astype(jnp.int32).reshape(1)
    widths = [share * wide // sum(SHARES) for share in SHARES]
    rows = momentum.shape[1]
    shape = jax.ShapeDtypeStruct
    part = functools.partial

    anywhere = pl.BlockSpec(memory_space=pl.ANY)
    out_rows, out_wide = cross_out.shape[1:]
    pair, *cuts = call(
        part(cut_kernel, widths),
        [shape((2 * out_rows, out_wide), HALF)]
        + [shape((inverse_in.shape[1], width), HALF) for width in widths],
        [me, cross_out[0], inverse_out[0], inverse_in[0]],
        0,
        in_specs=[pl.BlockSpec(memory_space=pltpu.SMEM)] + [anywhere] * 3,
        scratch_shapes=[pltpu.SemaphoreType.DMA((2 + len(widths),))],
    )
    pairs = from_peers(pair, "rep")
    in_blocks = [cross_in[0], *from_peers(cross_in[0], "rep")]
    following = passed_along(own_block, "layer", -1)

    cut_peers = [from_peers(piece, "rep") for piece in cuts]
    (first,) = call(
        part(first_kernel, count),
        [shape((tall, wide), HALF)],
        [me, following, cross_out[0], *pairs],
        tall * tall * wide // 32,
    )
    previous_blocks = [passed_along(block, "layer", 1) for block in in_blocks]
    (left,) = call(
        part(left_kernel, count),
        [shape((tall, wide), HALF)],
        [me, own_block, first, inverse_out[0], *in_blocks, *pairs],
        tall * wide * (tall + wide) // 32,
    )
    (mine,) = call(
        part(mine_kernel, count),
        [shape((tall, wide), FULL)],
        [me, left, inverse_in[0]],
        tall * wide * wide // 64,
    )
    preconds, backs = [], []
    for at, peers in enumerate(cut_peers):
        precond, back = call(
            part(chunk_kernel, count, sum(widths[:at])),
            [shape((tall, widths[at]), HALF)] * 2,
            [me, left, mine, cross_out[0], *peers, *pairs],
            tall * widths[at] * (tall + wide) // 32,
        )
        preconds.append(precond)
        ring = at != 1
        backs.append(passed_round(back, "layer") if ring else passed_along(back, "layer", 1))
    near = 7 * rows // 16 // ROWS * ROWS
    peers, last, later = count - 1, widths[-1], sum(widths[EARLY:])
    far_rows, left_rows = [], rows - near
    for at in range(PARTS, 0, -1):
        far_rows.append(left_rows if at == 1 else left_rows // at // ROWS * ROWS)
        left_rows -= far_rows[-1]
    nears = call(
        part(early_kernel, count, rows),
        [shape((near, wide), HALF)] * peers,
        [me, *preconds, *backs[:EARLY], *previous_blocks],
        2 * peers * near * wide * (wide - later),
        scratch_shapes=[pltpu.VMEM((near, wide), HALF), pltpu.VMEM((near, wide - later), HALF)],
    )
    nears = [to_peer(value, "rep", at + 1) for at, value in enumerate(nears)]
    partial, right_rest = call(
        part(gather_kernel, count),
        [shape((tall, wide), FULL), shape((wide, later), HALF)],
        [me, *preconds, *backs[:-1], *previous_blocks],
        2 * tall * wide * (wide - last),
        scratch_shapes=[pltpu.VMEM((tall, wide), HALF), pltpu.VMEM((tall, wide - last), HALF)],
    )
    squares, own, *sends = call(
        part(update_kernel, count),
        [shape((8, 128), FULL), shape((rows, wide), FULL)]
        + [shape((near, later), HALF)] * peers
        + [shape((size, wide), HALF) for size in far_rows] * peers,
        [me, partial, right_rest, *backs[EARLY:]],
        2 * tall * wide * last,
    )
    rests = [to_peer(value, "rep", at + 1) for at, value in enumerate(sends[:peers])]
    fars = [to_peer(value, "rep", at // PARTS + 1) for at, value in enumerate(sends[peers:])]
    others = [to_peer(squares, "rep", step) for step in range(1, count)]
    (base,) = call(
        part(base_kernel, count, tall * wide),
        [shape((rows, wide), FULL)],
        [momentum[0], squares, own],
        2 * rows * wide,
        in_specs=[pl.BlockSpec(memory_space=pltpu.VMEM)] * 3,
    )
    operands = [base, right_rest, *others, *nears, *rests, *fars]
    (result,) = call(
        part(final_kernel, count, tall * wide),
        [shape((rows, wide), FULL)],
        operands,
        4 * rows * wide,
        in_specs=[pl.BlockSpec(memory_space=pltpu.VMEM)] * len(operands),
        out_specs=[anywhere],
        scratch_shapes=[pltpu.VMEM((rows, wide), FULL), pltpu.SemaphoreType.DMA((PARTS + 1,))],
    )
    return result[None]


def solution(mesh):
    in_specs = (
        P("rep", "layer", None, None),
        P("layer", "rep", None),
        P("layer", "rep", None),
        P("layer", "rep", None),
        P("layer", "rep", None),
        P("layer", "rep", None),
    )
    out_specs = P("layer", "rep", None)
    return jax.shard_map(body, mesh=mesh, in_specs=in_specs, out_specs=out_specs, check_vma=False)
```
